32 devices in a mesh: ctx: 16 (over z, y, core), head: 2 (over x).
Axes of the slice: x: 2, y: 2, z: 4, core: 2. Of those that a mesh axis runs over, the one named last changes fastest.
Arguments:
- queries: bfloat16 [4096, 256], P('ctx', 'head'), may hold values from -6 to 6
- keys: bfloat16 [4096, 256], P('ctx', 'head'), may hold values from -6 to 6
- values: bfloat16 [4096, 2048], P('ctx', 'head'), may hold values from -6 to 6
- conv_keys: float32 [3, 256], P(None, 'head'), may hold values from -3.5 to 3.5
- conv_values: float32 [3, 2048], P(None, 'head'), may hold values from -3.5 to 3.5
- out_weight: bfloat16 [2048, 2048], P('head'), may hold values from -0.125 to 0.125
- cotangent: bfloat16 [4096, 2048], P('ctx', 'head'), may hold values from -6 to 6
Outputs:
- mixed_out: bfloat16 [4096, 2048], P('ctx', 'head')
- value_grad: bfloat16 [4096, 2048], P('ctx', 'head')
The draws below stay inside these ranges and needn't reach their ends.
All inputs are finite; a program needn't handle non-finite values.
Results may differ from the reference program's by a relative error of at most 0.004.
The reference program's roundings to bfloat16 on the way count: a program that leaves them out, or rounds other values in their place, can miss the bound.
Values may be sent and summed in bfloat16 or wider, within the bound.
No kernel may reach another device: no remote copies, remote signals or barrier semaphores. Data moves between devices by JAX's collectives and lax.ppermute only.
A program may use at most 64 MiB of HBM per device.

```python
import jax
import jax.numpy as jnp
from jax import lax

D = 2048
HEADS = 16
FEAT = 16
VDIM = 128
CONV = 3
TOK_DEV = 256
PHI = 273
TOKENS = 4096


def block_levels(stream_key, dims, cuts, least, high):
    gain, own = 1.0, jax.random.fold_in(stream_key, 6)
    for axis_at, blocks in cuts:
        draws = jnp.exp(jax.random.uniform(jax.random.fold_in(own, axis_at), (blocks,), jnp.float32, least / len(cuts), high / len(cuts)))
        gain = gain * jnp.repeat(draws, dims[axis_at] // blocks).reshape([-1 if axis == axis_at else 1 for axis in range(len(dims))])
    return gain


def bell_draw(own_key, dims, deviation, bound, cuts=(), kind=jnp.bfloat16):
    drawn = jax.random.normal(own_key, dims, jnp.float32) * deviation
    if len(cuts) > 0:
        drawn = block_levels(own_key, dims, cuts, -0.22, 0.18) * drawn
    return jnp.clip(drawn, min=-bound, max=bound).astype(kind)


def setup_inputs(seed: int = 0) -> dict:
    streams_of = jax.random.split(jax.random.key(seed), 8)
    queries = bell_draw(streams_of[0], (TOKENS, HEADS * FEAT), 1.0, 6.0, ((0, 16), (1, 2)))
    keys = bell_draw(streams_of[1], (TOKENS, HEADS * FEAT), 1.0, 6.0, ((0, 16), (1, 2)))
    values = bell_draw(streams_of[2], (TOKENS, HEADS * VDIM), 1.0, 6.0, ((0, 16), (1, 2)))
    conv_keys = bell_draw(streams_of[3], (CONV, HEADS * FEAT), CONV ** -0.5, 3.5, ((1, 2),), jnp.float32)
    conv_values = bell_draw(streams_of[4], (CONV, HEADS * VDIM), CONV ** -0.5, 3.5, ((1, 2),), jnp.float32)
    out_weight = bell_draw(streams_of[5], (HEADS * VDIM, D), (HEADS * VDIM) ** -0.5, 0.125, ((0, 2),))
    cotangent = bell_draw(streams_of[6], (TOKENS, D), 1.0, 6.0, ((0, 16), (1, 2)))
    return dict(queries=queries, keys=keys, values=values, conv_keys=conv_keys, conv_values=conv_values, out_weight=out_weight, cotangent=cotangent)


def features(inputs):
    scaled = inputs * FEAT ** -0.25
    square = scaled[..., :, None] * scaled[..., None, :]
    square = square.reshape(scaled.shape[:-1] + (FEAT * FEAT,)) * 0.5 ** 0.5
    constant = jnp.ones(scaled.shape[:-1] + (1,), jnp.float32)
    return jnp.concatenate([constant, scaled, square], -1).astype(jnp.bfloat16)


def convolve(token_block, before, weights):
    joined = jnp.concatenate([before, token_block], 0).astype(jnp.float32)
    block_rows = token_block.shape[0]
    running = weights[0] * joined[CONV - 1:CONV - 1 + block_rows]
    for offset in range(1, CONV):
        running = running + weights[offset] * joined[CONV - 1 - offset:CONV - 1 - offset + block_rows]
    return running


def lowered(array_in):
    return lax.optimization_barrier(array_in.astype(jnp.bfloat16)).astype(jnp.float32)


def reference(queries, keys, values, conv_keys, conv_values, out_weight, cotangent):
    highest = lax.Precision.HIGHEST
    key_conv = convolve(keys, jnp.zeros((CONV - 1, keys.shape[1]), jnp.bfloat16), conv_keys)
    value_conv = convolve(values, jnp.zeros((CONV - 1, values.shape[1]), jnp.bfloat16), conv_values).astype(jnp.bfloat16)
    blocks = TOKENS // TOK_DEV
    query_blocks = queries.reshape(blocks, TOK_DEV, HEADS, FEAT)
    key_blocks = key_conv.reshape(blocks, TOK_DEV, HEADS, FEAT)
    value_blocks = value_conv.reshape(blocks, TOK_DEV, HEADS, VDIM)
    causal = jnp.arange(TOK_DEV)[:, None] >= jnp.arange(TOK_DEV)[None, :]

    def block_scores(query_feat, key_feat):
        scores = jnp.einsum("thp,shp->hts", query_feat.astype(jnp.float32), key_feat.astype(jnp.float32), precision=highest)
        return jnp.where(causal[None], scores, 0.0)

    def forward_step(running, block_items):
        value_state, norm_sum = running
        query_raw, key_raw, value_block = block_items
        query_feat = features(query_raw.astype(jnp.float32))
        key_feat = features(key_raw)
        scores = block_scores(query_feat, key_feat)
        scores_low = lowered(scores)
        query_wide = query_feat.astype(jnp.float32)
        key_wide = key_feat.astype(jnp.float32)
        value_wide = value_block.astype(jnp.float32)
        numerator = jnp.einsum("hts,shv->thv", scores_low, value_wide, precision=highest)
        numerator = numerator + jnp.einsum("thp,hpv->thv", query_wide, lowered(value_state), precision=highest)
        denominator = jnp.sum(scores, 2).T + jnp.einsum("thp,hp->th", query_wide, norm_sum, precision=highest)
        attended = (numerator / denominator[..., None]).astype(jnp.bfloat16)
        value_state = value_state + jnp.einsum("shp,shv->hpv", key_wide, value_wide, precision=highest)
        norm_sum = norm_sum + jnp.sum(key_wide, 0)
        return (value_state, norm_sum), (attended, denominator)

    start_state = (jnp.zeros((HEADS, PHI, VDIM), jnp.float32), jnp.zeros((HEADS, PHI), jnp.float32))
    _, (attended, denominator) = lax.scan(forward_step, start_state, (query_blocks, key_blocks, value_blocks))
    attended = attended.reshape(TOKENS, HEADS * VDIM)
    mixed_out = jnp.dot(attended, out_weight, preferred_element_type=jnp.float32).astype(jnp.bfloat16)
    out_grad = jnp.dot(cotangent, out_weight.T, preferred_element_type=jnp.float32)
    scaled_grad = (out_grad.reshape(blocks, TOK_DEV, HEADS, VDIM) / denominator[..., None]).astype(jnp.bfloat16)

    def backward_step(later_state, block_items):
        query_raw, key_raw, grad_block = block_items
        query_feat = features(query_raw.astype(jnp.float32))
        key_feat = features(key_raw)
        scores_low = lowered(block_scores(query_feat, key_feat))
        grad_wide = grad_block.astype(jnp.float32)
        grad_here = jnp.einsum("hts,thv->shv", scores_low, grad_wide, precision=highest)
        grad_here = grad_here + jnp.einsum("shp,hpv->shv", key_feat.astype(jnp.float32), lowered(later_state), precision=highest)
        later_state = later_state + jnp.einsum("thp,thv->hpv", query_feat.astype(jnp.float32), grad_wide, precision=highest)
        return later_state, grad_here.astype(jnp.bfloat16)

    _, value_grad = lax.scan(backward_step, jnp.zeros((HEADS, PHI, VDIM), jnp.float32), (query_blocks, key_blocks, scaled_grad), reverse=True)
    return mixed_out, value_grad.reshape(TOKENS, HEADS * VDIM)
```

```python
import jax
import jax.numpy as jnp
from jax import lax
from jax.experimental import pallas as pl
from jax.experimental.pallas import tpu as pltpu
from jax.sharding import PartitionSpec as P

FEAT = 16
VDIM = 128
CONV = 3
ROWS = 160
PLANE = 4

F32 = jnp.float32
BF16 = jnp.bfloat16
TN = (((0,), (0,)), ((), ()))
NT = (((1,), (1,)), ((), ()))
NN = (((1,), (0,)), ((), ()))


def mm(a, b, dims):
    return lax.dot_general(a, b, dims, preferred_element_type=F32)


def call(body, scalars, operands, in_specs, out_shape, out_specs, flops, scratch=()):
    moved = sum(x.size * x.dtype.itemsize for x in operands)
    moved += sum(x.size * x.dtype.itemsize for x in out_shape)
    return pl.pallas_call(
        body,
        out_shape=out_shape,
        grid_spec=pltpu.PrefetchScalarGridSpec(
            num_scalar_prefetch=1,
            grid=(1,),
            in_specs=in_specs,
            out_specs=out_specs,
            scratch_shapes=list(scratch),
        ),
        compiler_params=pltpu.CompilerParams(vmem_limit_bytes=28 * 1024 * 1024),
        cost_estimate=pl.CostEstimate(flops=flops, bytes_accessed=moved, transcendentals=0),
    )(scalars, *operands)


def whole(x):
    shape = x.shape
    return pl.BlockSpec(shape, lambda i, s: (0,) * len(shape))


def column_block(x, width, distance):
    return pl.BlockSpec((x.shape[0], width), lambda i, s: (0, s[1] ^ distance))


def store_features(out_ref, rows_in, doubled):
    heads = rows_in.shape[0] // FEAT
    tokens = rows_in.shape[1]
    grid = rows_in.reshape(heads, FEAT, tokens) * FEAT ** (-0.25)
    twice = jnp.concatenate([grid, grid], 1)
    out_ref[:, 0:FEAT, :] = grid.astype(BF16)
    half = FEAT // 2
    for turn in range(half):
        square = grid * twice[:, turn : turn + FEAT, :] * 0.5**0.5
        if doubled and turn > 0:
            square = square * 2.0
        out_ref[:, FEAT * (turn + 1) : FEAT * (turn + 2), :] = square.astype(BF16)
    square = grid[:, :half, :] * grid[:, half:, :] * 0.5**0.5
    if doubled:
        square = square * 2.0
    first = lax.broadcasted_iota(jnp.int32, (heads, half, tokens), 1) == 0
    constant = jnp.where(first, 1.0, 0.0)
    out_ref[:, FEAT * (half + 1) :, :] = jnp.concatenate([square, constant], 1).astype(BF16)


def store_piece(rank, head, per_piece, state, own_ref, send_ref):
    slot = rank ^ (head // per_piece)
    at = (head % per_piece) * ROWS

    @pl.when(slot == 0)
    def _():
        own_ref[at : at + ROWS, :] = state

    @pl.when(slot != 0)
    def _():
        send_ref[slot - 1, at : at + ROWS, :] = state.astype(BF16)


def load_piece(rank, head, per_piece, ref):
    at = (head % per_piece) * ROWS
    return ref[rank ^ (head // per_piece), at : at + ROWS, :]


def query_kernel(s_ref, q_ref, cot_ref, w_ref, qd_ref, og_ref):
    store_features(qd_ref, q_ref[...].astype(F32).T, True)
    og_ref[...] = mm(cot_ref[...], w_ref[...], NT)


def grad_kernel(s_ref, cot_ref, w_ref, before_ref, og_ref):
    og_ref[...] = before_ref[...] + mm(cot_ref[...], w_ref[...], NT)


def conv_rows(x, before, taps):
    x = x.astype(F32)
    row = lax.broadcasted_iota(jnp.int32, x.shape, 0)
    running = taps[0:1, :] * x
    for offset in range(1, CONV):
        moved = pltpu.roll(x, offset, 0)
        for at in range(offset):
            source = before[CONV - 1 - offset + at : CONV - offset + at, :]
            moved = jnp.where(row == at, source, moved)
        running = running + taps[offset : offset + 1, :] * moved
    return running


def key_kernel(
    s_ref, k_ref, v_ref, before_ref, ck_ref, cv_ref, kf_ref, vc_ref, own_ref, send_ref, norm_ref
):
    rank = s_ref[0]
    heads = kf_ref.shape[0]
    per_piece = heads // PLANE
    width = k_ref.shape[1]
    before = before_ref[...].astype(F32)
    key_conv = conv_rows(k_ref[...], before[:, :width], ck_ref[...])
    store_features(kf_ref, key_conv.T, False)
    ones = jnp.ones((heads, k_ref.shape[0]), BF16)
    row = lax.broadcasted_iota(jnp.int32, (heads, ROWS), 0)
    norm = jnp.zeros((heads, ROWS), F32)
    for head in range(heads):
        at = head * VDIM
        value = conv_rows(
            v_ref[:, at : at + VDIM],
            before[:, width + at : width + at + VDIM],
            cv_ref[:, at : at + VDIM],
        ).astype(BF16)
        vc_ref[:, at : at + VDIM] = value
        feat = kf_ref[head]
        norm = jnp.where(row == head, mm(ones, feat, NT), norm)
        store_piece(rank, head, per_piece, mm(feat, value, NN), own_ref, send_ref)
    norm_ref[...] = norm


def score_kernel(s_ref, qd_ref, kf_ref, vc_ref, low_ref, den_ref, num_ref):
    heads = kf_ref.shape[0]
    tokens = kf_ref.shape[2]
    key_at = lax.broadcasted_iota(jnp.int32, (tokens, tokens), 0)
    query_at = lax.broadcasted_iota(jnp.int32, (tokens, tokens), 1)
    causal = key_at <= query_at
    for head in range(heads):
        scores = jnp.where(causal, mm(kf_ref[head], qd_ref[head], TN), 0.0)
        den_ref[head : head + 1, :] = jnp.sum(scores, 0, keepdims=True)
        low = scores.astype(BF16)
        low_ref[head] = low
        at = head * VDIM
        num_ref[:, at : at + VDIM] = mm(low, vc_ref[:, at : at + VDIM], TN)


def scale_kernel(s_ref, norm_ref, den_ref, qd_ref, og_ref, inv_ref, sg_ref, own_ref, send_ref):
    rank = s_ref[0]
    heads = qd_ref.shape[0]
    per_piece = heads // PLANE
    norm = norm_ref[...]
    high = norm.astype(BF16).astype(F32)
    middle = (norm - high).astype(BF16).astype(F32)
    rest = norm - high - middle
    parts = jnp.concatenate([high, middle, rest, jnp.zeros_like(rest)], 0).astype(BF16)
    lines = []
    for head in range(heads):
        terms = mm(parts, qd_ref[head], NN)
        line = den_ref[head : head + 1, :] + terms[head : head + 1, :]
        line = line + terms[heads + head : heads + head + 1, :]
        lines.append(line + terms[2 * heads + head : 2 * heads + head + 1, :])
    inverse = (1.0 / jnp.concatenate(lines, 0)).T
    inv_ref[...] = inverse
    for head in range(heads):
        at = head * VDIM
        scaled = (og_ref[:, at : at + VDIM] * inverse[:, head : head + 1]).astype(BF16)
        sg_ref[:, at : at + VDIM] = scaled
        store_piece(rank, head, per_piece, mm(qd_ref[head], scaled, NN), own_ref, send_ref)


def near_kernel(s_ref, low_ref, sg_ref, vg_ref):
    for head in range(low_ref.shape[0]):
        at = head * VDIM
        vg_ref[:, at : at + VDIM] = mm(low_ref[head], sg_ref[:, at : at + VDIM], NN)


def attend_kernel(s_ref, qd_ref, prior_ref, num_ref, inv_ref, w_ref, att_ref, part_ref):
    rank = s_ref[0]
    heads = qd_ref.shape[0]
    per_piece = heads // PLANE
    for head in range(heads):
        at = head * VDIM
        prior = load_piece(rank, head, per_piece, prior_ref)
        total = num_ref[:, at : at + VDIM] + mm(qd_ref[head], prior, TN)
        att_ref[:, at : at + VDIM] = (total * inv_ref[:, head : head + 1]).astype(BF16)
    part_ref[...] = mm(att_ref[...], w_ref[...], NN).astype(BF16)


def mix_kernel(s_ref, att_ref, w_ref, part_ref):
    part_ref[...] = mm(att_ref[...], w_ref[...], NN).astype(part_ref.dtype)


def far_kernel(s_ref, kf_ref, later_ref, near_ref, vg_ref):
    rank = s_ref[0]
    heads = kf_ref.shape[0]
    per_piece = heads // PLANE
    for head in range(heads):
        at = head * VDIM
        later = load_piece(rank, head, per_piece, later_ref)
        total = near_ref[:, at : at + VDIM] + mm(kf_ref[head], later, TN)
        vg_ref[:, at : at + VDIM] = total.astype(BF16)


def shifted(x, axis, by):
    peers = lax.axis_size(axis)
    pairs = [(i, i + by) for i in range(peers) if 0 <= i + by < peers]
    return lax.ppermute(x, axis, pairs)


def swapped(x, axis, distance):
    peers = lax.axis_size(axis)
    return lax.ppermute(x, axis, [(i, i ^ distance) for i in range(peers)])


def planes_before(total, sign, kind):
    planes = lax.axis_size("ctx") // PLANE
    running = total
    before = jnp.zeros_like(total)
    distance = 1
    while distance < planes:
        moved = shifted(running.astype(kind), "ctx", sign * distance * PLANE).astype(F32)
        before = before + moved
        running = running + moved
        distance = distance * 2
    return before


def scan_states(own, send, rank, sign):
    got = [own] + [swapped(send[j - 1], "ctx", j).astype(F32) for j in range(1, PLANE)]
    total = got[0] + got[1] + got[2] + got[3]
    before = planes_before(total, sign, BF16)
    pieces = []
    for j in range(PLANE):
        piece = before
        for i in range(PLANE):
            if i == j:
                continue
            ahead = (rank ^ i) < (rank ^ j) if sign > 0 else (rank ^ i) > (rank ^ j)
            piece = piece + jnp.where(ahead, got[i], 0.0)
        pieces.append(piece.astype(BF16))
    return jnp.stack([pieces[0]] + [swapped(pieces[j], "ctx", j) for j in range(1, PLANE)], 0)


def scan_norms(norm, rank):
    before = jnp.zeros_like(norm)
    total = norm
    distance = 1
    while distance < PLANE:
        moved = swapped(total, "ctx", distance)
        before = before + jnp.where((rank & distance) != 0, moved, 0.0)
        total = total + moved
        distance = distance * 2
    return before + planes_before(total, 1, F32)


def per_device(queries, keys, values, conv_keys, conv_values, out_weight, cotangent):
    tokens = queries.shape[0]
    heads = queries.shape[1] // FEAT
    width = heads * VDIM
    columns = cotangent.shape[1]
    groups = lax.axis_size("head")
    rank = lax.axis_index("ctx") % PLANE
    scalars = jnp.stack([rank, lax.axis_index("head")]).astype(jnp.int32)
    piece_rows = heads // PLANE * ROWS
    S = jax.ShapeDtypeStruct
    step = 2 * tokens * ROWS * VDIM * heads
    project = 2 * tokens * width * columns

    last_rows = jnp.concatenate([keys[tokens - CONV + 1 :], values[tokens - CONV + 1 :]], 1)
    before = shifted(last_rows, "ctx", 1)
    cots = [swapped(cotangent, "head", j) for j in range(1, groups)]

    with jax.named_scope("query_features"):
        qd, out_grad = call(
            query_kernel,
            scalars,
            (queries, cotangent, out_weight),
            [whole(queries), whole(cotangent), column_block(out_weight, columns, 0)],
            [S((heads, ROWS, tokens), BF16), S((tokens, width), F32)],
            [whole(S((heads, ROWS, tokens), BF16)), whole(S((tokens, width), F32))],
            project,
        )
    with jax.named_scope("key_features"):
        outs = [
            S((heads, ROWS, tokens), BF16),
            S((tokens, width), BF16),
            S((piece_rows, VDIM), F32),
            S((PLANE - 1, piece_rows, VDIM), BF16),
            S((heads, ROWS), F32),
        ]
        ops = (keys, values, before, conv_keys, conv_values)
        kf, vc, own, send, norm = call(
            key_kernel, scalars, ops, [whole(x) for x in ops], outs, [whole(x) for x in outs], step
        )
    with jax.named_scope("norm_scan"):
        prior_norm = scan_norms(norm, rank)
    with jax.named_scope("scores"):
        outs = [
            S((heads, tokens, tokens), BF16),
            S((heads, tokens), F32),
            S((tokens, width), F32),
        ]
        ops = (qd, kf, vc)
        low, den, num = call(
            score_kernel,
            scalars,
            ops,
            [whole(x) for x in ops],
            outs,
            [whole(x) for x in outs],
            4 * step,
        )
    with jax.named_scope("prior_scan"):
        prior = scan_states(own, send, rank, 1)
    with jax.named_scope("out_grad"):
        for j in range(1, groups):
            outs = [S((tokens, width), F32)]
            ops = (cots[j - 1], out_weight, out_grad)
            specs = [whole(ops[0]), column_block(out_weight, columns, j), whole(out_grad)]
            (out_grad,) = call(
                grad_kernel, scalars, ops, specs, outs, [whole(x) for x in outs], project
            )
    with jax.named_scope("scaled_grad"):
        outs = [
            S((tokens, heads), F32),
            S((tokens, width), BF16),
            S((piece_rows, VDIM), F32),
            S((PLANE - 1, piece_rows, VDIM), BF16),
        ]
        ops = (prior_norm, den, qd, out_grad)
        inverse, scaled, own_later, send_later = call(
            scale_kernel,
            scalars,
            ops,
            [whole(x) for x in ops],
            outs,
            [whole(x) for x in outs],
            step,
        )
    with jax.named_scope("later_scan"):
        later = scan_states(own_later, send_later, rank, -1)
    with jax.named_scope("near_grad"):
        outs = [S((tokens, width), F32)]
        ops = (low, scaled)
        (near,) = call(
            near_kernel,
            scalars,
            ops,
            [whole(x) for x in ops],
            outs,
            [whole(x) for x in outs],
            2 * step,
        )
    with jax.named_scope("attended"):
        outs = [S((tokens, width), BF16), S((tokens, columns), BF16)]
        ops = (qd, prior, num, inverse, out_weight)
        specs = [whole(x) for x in ops[:4]] + [column_block(out_weight, columns, 1)]
        attended, part = call(
            attend_kernel, scalars, ops, specs, outs, [whole(x) for x in outs], step + project
        )
        parts = [swapped(part, "head", 1)]
    with jax.named_scope("mixed"):
        for j in list(range(2, groups)) + [0]:
            outs = [S((tokens, columns), BF16 if j else F32)]
            ops = (attended, out_weight)
            specs = [whole(attended), column_block(out_weight, columns, j)]
            (part,) = call(
                mix_kernel, scalars, ops, specs, outs, [whole(x) for x in outs], project
            )
            if j:
                parts.append(swapped(part, "head", j))
        mixed_out = part
        for other in parts:
            mixed_out = mixed_out + other.astype(F32)
        mixed_out = mixed_out.astype(BF16)
    with jax.named_scope("far_grad"):
        outs = [S((tokens, width), BF16)]
        ops = (kf, later, near)
        (value_grad,) = call(
            far_kernel, scalars, ops, [whole(x) for x in ops], outs, [whole(x) for x in outs], step
        )
    return mixed_out, value_grad


def solution(mesh):
    in_specs = (
        P("ctx", "head"),
        P("ctx", "head"),
        P("ctx", "head"),
        P(None, "head"),
        P(None, "head"),
        P("head", None),
        P("ctx", "head"),
    )
    out_specs = (P("ctx", "head"), P("ctx", "head"))
    return jax.shard_map(
        per_device, mesh=mesh, in_specs=in_specs, out_specs=out_specs, check_vma=False
    )
```

```python
import functools

import jax
import jax.numpy as jnp
from jax import lax
from jax.experimental import pallas as pl
from jax.experimental.pallas import tpu as pltpu
from jax.sharding import PartitionSpec as P

FEAT = 16
VDIM = 128
CONV = 3
ROWS = 160
VMEM_LIMIT = 14 * 1024 * 1024
PLANE = 4

F32 = jnp.float32
BF16 = jnp.bfloat16
TN = (((0,), (0,)), ((), ()))
NT = (((1,), (1,)), ((), ()))
NN = (((1,), (0,)), ((), ()))


def mm(a, b, dims):
    return lax.dot_general(a, b, dims, preferred_element_type=F32)


def call(body, scalars, operands, out_shape, flops, far=(), scratch=()):
    moved = sum(x.size * x.dtype.itemsize for x in operands)
    moved += sum(x.size * x.dtype.itemsize for x in out_shape)
    vmem = pl.BlockSpec(memory_space=pltpu.VMEM)
    hbm = pl.BlockSpec(memory_space=pltpu.HBM)
    return pl.pallas_call(
        body,
        out_shape=out_shape,
        in_specs=[pl.BlockSpec(memory_space=pltpu.SMEM)]
        + [hbm if i in far else vmem for i in range(len(operands))],
        out_specs=[vmem for _ in out_shape],
        scratch_shapes=list(scratch),
        compiler_params=pltpu.CompilerParams(vmem_limit_bytes=VMEM_LIMIT),
        cost_estimate=pl.CostEstimate(flops=flops, bytes_accessed=moved, transcendentals=0),
    )(scalars, *[in_hbm(x) if i in far else x for i, x in enumerate(operands)])


def in_hbm(x):
    return pltpu.with_memory_space_constraint(x, pltpu.HBM)


def fetch(source, target, sem):
    copy = pltpu.make_async_copy(source, target, sem)
    copy.start()
    return copy


def store_features(out_ref, rows_in, doubled):
    heads = rows_in.shape[0] // FEAT
    tokens = rows_in.shape[1]
    grid = rows_in.reshape(heads, FEAT, tokens) * FEAT ** (-0.25)
    twice = jnp.concatenate([grid, grid], 1)
    out_ref[:, 0:FEAT, :] = grid.astype(BF16)
    half = FEAT // 2
    for turn in range(half):
        square = grid * twice[:, turn : turn + FEAT, :] * 0.5**0.5
        if doubled and turn > 0:
            square = square * 2.0
        out_ref[:, FEAT * (turn + 1) : FEAT * (turn + 2), :] = square.astype(BF16)
    square = grid[:, :half, :] * grid[:, half:, :] * 0.5**0.5
    if doubled:
        square = square * 2.0
    first = lax.broadcasted_iota(jnp.int32, (heads, half, tokens), 1) == 0
    constant = jnp.where(first, 1.0, 0.0)
    out_ref[:, FEAT * (half + 1) :, :] = jnp.concatenate([square, constant], 1).astype(BF16)


def store_piece(rank, head, per_piece, state, own_ref, send_ref):
    slot = rank ^ (head // per_piece)
    at = (head % per_piece) * ROWS
    own_ref[slot, at : at + ROWS, :] = state
    send_ref[slot, at : at + ROWS, :] = state.astype(BF16)


def load_piece(rank, head, per_piece, ref):
    at = (head % per_piece) * ROWS
    return ref[rank ^ (head // per_piece), at : at + ROWS, :]


def edge_kernel(k_far, v_far, ck_far, cv_far, edge_ref, k_ref, v_ref, ck_ref, cv_ref, sems):
    pairs = ((k_far, k_ref), (v_far, v_ref), (ck_far, ck_ref), (cv_far, cv_ref))
    copies = [fetch(a, b, sems.at[i]) for i, (a, b) in enumerate(pairs)]
    for copy in copies:
        copy.wait()
    tokens, width = k_ref.shape
    last = 16 - CONV + 1
    edge_ref[:, :width] = k_ref[tokens - 16 :, :].astype(F32)[last:].astype(BF16)
    edge_ref[:, width:] = v_ref[tokens - 16 :, :].astype(F32)[last:].astype(BF16)


def query_kernel(s_ref, q_far, qd_ref, q_ref, sem):
    fetch(q_far, q_ref, sem).wait()
    store_features(qd_ref, q_ref[...].astype(F32).T, True)


def columns_of(s_ref, w_ref, distance):
    columns = w_ref.shape[1] // lax.axis_size("head")
    return pl.ds(pl.multiple_of((s_ref[1] ^ distance) * columns, columns), columns)


def grad_kernel(s_ref, *refs):
    *cots, w_ref, og_ref = refs
    total = None
    for j, cot_ref in enumerate(cots):
        term = mm(cot_ref[...], w_ref[:, columns_of(s_ref, w_ref, j)], NT)
        total = term if total is None else total + term
    og_ref[...] = total


def conv_rows(x, before, taps):
    x = x.astype(F32)
    row = lax.broadcasted_iota(jnp.int32, x.shape, 0)
    running = taps[0:1, :] * x
    for offset in range(1, CONV):
        moved = pltpu.roll(x, offset, 0)
        for at in range(offset):
            source = before[CONV - 1 - offset + at : CONV - offset + at, :]
            moved = jnp.where(row == at, source, moved)
        running = running + taps[offset : offset + 1, :] * moved
    return running


def norm_rows(norm):
    high = norm.astype(BF16).astype(F32)
    middle = (norm - high).astype(BF16).astype(F32)
    rest = norm - high - middle
    parts = (high, middle, rest)
    tail = [x[:, VDIM:] for x in parts]
    filler = jnp.zeros((norm.shape[0], VDIM - 3 * (ROWS - VDIM)), F32)
    tail = jnp.concatenate(tail + [filler], 1)
    return jnp.concatenate([x[:, :VDIM] for x in parts] + [tail], 0)


def norm_values(rows):
    heads = rows.shape[0] // 4
    extra = ROWS - VDIM
    tail = rows[3 * heads :]
    tail = tail[:, :extra] + tail[:, extra : 2 * extra] + tail[:, 2 * extra : 3 * extra]
    main = rows[:heads] + rows[heads : 2 * heads] + rows[2 * heads : 3 * heads]
    return jnp.concatenate([main, tail], 1)


def key_kernel(
    s_ref,
    k_ref,
    v_ref,
    before_ref,
    ck_ref,
    cv_ref,
    kf_ref,
    vc_ref,
    own_ref,
    send_ref,
    slots,
):
    rank = s_ref[0]
    heads = kf_ref.shape[0]
    per_piece = heads // PLANE
    width = k_ref.shape[1]
    before = before_ref[...].astype(F32)
    key_conv = conv_rows(k_ref[...], before[:, :width], ck_ref[...])
    store_features(kf_ref, key_conv.T, False)
    ones = jnp.ones((heads, k_ref.shape[0]), BF16)
    row = lax.broadcasted_iota(jnp.int32, (heads, ROWS), 0)
    norm = jnp.zeros((heads, ROWS), F32)
    for head in range(heads):
        at = head * VDIM
        value = conv_rows(
            v_ref[:, at : at + VDIM],
            before[:, width + at : width + at + VDIM],
            cv_ref[:, at : at + VDIM],
        ).astype(BF16)
        vc_ref[:, at : at + VDIM] = value
        feat = kf_ref[head]
        norm = jnp.where(row == head, mm(ones, feat, NT), norm)
        store_piece(rank, head, per_piece, mm(feat, value, NN), slots, send_ref)
    lines = norm_rows(norm)
    at = per_piece * ROWS
    own_ref[:at, :] = slots[0]
    own_ref[at:, :] = lines
    for slot in range(PLANE):
        send_ref[slot, at:, :] = lines.astype(BF16)


def share_kernel(norm_at, s_ref, own_ref, *refs):
    sent_at = -1 if refs[-1].dtype == BF16 else -2
    got_refs, sent_ref = refs[:sent_at], refs[sent_at]
    total = own_ref[...]
    for got_ref in got_refs:
        total = total + got_ref[...].astype(F32)
    if norm_at is not None:
        lines = norm_rows(norm_values(total[norm_at:]))
        total = jnp.concatenate([total[:norm_at], lines], 0)
    sent_ref[...] = total.astype(BF16)
    if sent_at == -2:
        refs[-1][...] = total


def piece_kernel(sign, strides, s_ref, *refs):
    rows = refs[-1].shape[1] if len(refs[-1].shape) == 3 else refs[-2].shape[1]
    norm_ref = refs[-1] if len(refs[-1].shape) == 2 else None
    pieces_ref = refs[-1] if norm_ref is None else refs[-2]
    got_refs, moved_refs = refs[:PLANE], refs[PLANE : PLANE + len(strides)]

    def masked(ahead, ref):
        return jnp.where(ahead, ref[...].astype(F32), 0.0)

    def is_ahead(other, here):
        return other < here if sign > 0 else other > here

    before = jnp.zeros(got_refs[0].shape, F32)
    for ref, (stride, distance) in zip(moved_refs, strides):
        if distance:
            group = lax.div(s_ref[2], stride)
            before = before + masked(is_ahead(group ^ distance, group), ref)
        else:
            before = before + ref[...].astype(F32)
    rank = s_ref[0]
    for slot in range(PLANE):
        total = before
        for i in range(PLANE):
            if i != slot:
                total = total + masked(is_ahead(rank ^ i, rank ^ slot), got_refs[i])
        pieces_ref[slot] = total[:rows].astype(BF16)
        if norm_ref is not None and slot == 0:
            norm_ref[...] = total[rows:]


def score_kernel(s_ref, qd_ref, kf_ref, vc_ref, low_ref, den_ref, num_ref):
    heads = kf_ref.shape[0]
    tokens = kf_ref.shape[2]
    key_at = lax.broadcasted_iota(jnp.int32, (tokens, tokens), 0)
    query_at = lax.broadcasted_iota(jnp.int32, (tokens, tokens), 1)
    causal = key_at <= query_at
    for head in range(heads):
        scores = jnp.where(causal, mm(kf_ref[head], qd_ref[head], TN), 0.0)
        den_ref[head : head + 1, :] = jnp.sum(scores, 0, keepdims=True)
        low = scores.astype(BF16)
        low_ref[head] = low
        at = head * VDIM
        num_ref[:, at : at + VDIM] = mm(low, vc_ref[:, at : at + VDIM], TN)


def scale_kernel(s_ref, norm_ref, den_ref, qd_ref, og_ref, inv_ref, sg_ref, own_ref, send_ref, slots):
    rank = s_ref[0]
    heads = qd_ref.shape[0]
    per_piece = heads // PLANE
    norm = norm_values(norm_ref[...])
    high = norm.astype(BF16).astype(F32)
    middle = (norm - high).astype(BF16).astype(F32)
    rest = norm - high - middle
    parts = jnp.concatenate([high, middle, rest, jnp.zeros_like(rest)], 0).astype(BF16)
    lines = []
    for head in range(heads):
        terms = mm(parts, qd_ref[head], NN)
        line = den_ref[head : head + 1, :] + terms[head : head + 1, :]
        line = line + terms[heads + head : heads + head + 1, :]
        lines.append(line + terms[2 * heads + head : 2 * heads + head + 1, :])
    inverse = (1.0 / jnp.concatenate(lines, 0)).T
    inv_ref[...] = inverse
    for head in range(heads):
        at = head * VDIM
        scaled = (og_ref[:, at : at + VDIM] * inverse[:, head : head + 1]).astype(BF16)
        sg_ref[:, at : at + VDIM] = scaled
        store_piece(rank, head, per_piece, mm(qd_ref[head], scaled, NN), slots, send_ref)
    own_ref[...] = slots[0]


def near_kernel(s_ref, low_ref, sg_ref, vg_ref):
    for head in range(low_ref.shape[0]):
        at = head * VDIM
        vg_ref[:, at : at + VDIM] = mm(low_ref[head], sg_ref[:, at : at + VDIM], NN)


def attend_kernel(s_ref, qd_ref, prior_ref, num_ref, inv_ref, w_ref, att_ref, part_ref):
    rank = s_ref[0]
    heads = qd_ref.shape[0]
    per_piece = heads // PLANE
    for head in range(heads):
        at = head * VDIM
        prior = load_piece(rank, head, per_piece, prior_ref)
        total = num_ref[:, at : at + VDIM] + mm(qd_ref[head], prior, TN)
        att_ref[:, at : at + VDIM] = (total * inv_ref[:, head : head + 1]).astype(BF16)
    part_ref[...] = mm(att_ref[...], w_ref[:, columns_of(s_ref, w_ref, 1)], NN).astype(BF16)


def mix_kernel(distance, s_ref, att_ref, w_ref, part_ref):
    weight = w_ref[:, columns_of(s_ref, w_ref, distance)]
    part_ref[...] = mm(att_ref[...], weight, NN).astype(part_ref.dtype)


def far_kernel(s_ref, kf_ref, later_ref, near_ref, vg_ref):
    rank = s_ref[0]
    heads = kf_ref.shape[0]
    per_piece = heads // PLANE
    for head in range(heads):
        at = head * VDIM
        later = load_piece(rank, head, per_piece, later_ref)
        total = near_ref[:, at : at + VDIM] + mm(kf_ref[head], later, TN)
        vg_ref[:, at : at + VDIM] = total.astype(BF16)


def shifted(x, axis, by):
    peers = lax.axis_size(axis)
    pairs = [(i, i + by) for i in range(peers) if 0 <= i + by < peers]
    return lax.ppermute(x, axis, pairs)


def after(x, *others):
    return lax.optimization_barrier((x, *others))[0]


def planes_ahead(total, sent, sign, join):
    planes = lax.axis_size("ctx") // PLANE
    received, strides = [], []
    stride = 1
    while stride < planes:
        if (planes // stride) % 4 == 0:
            moved = [swapped(sent, "ctx", j, stride * PLANE) for j in range(1, 4)]
            strides += [(stride, j) for j in range(1, 4)]
            stride = stride * 4
        else:
            moved = [shifted(sent, "ctx", sign * stride * PLANE)]
            strides.append((stride, 0))
            stride = stride * 2
        received += moved
        if stride < planes:
            sent, total = join(total, moved, stride * 2 < planes)
    return received, strides


def swapped(x, axis, distance, stride=1):
    peers = lax.axis_size(axis)
    pairs = [(i, (i // stride ^ distance) * stride + i % stride) for i in range(peers)]
    return lax.ppermute(x, axis, pairs)


def handed_back(pieces):
    back = [swapped(pieces[j], "ctx", j) for j in range(1, PLANE)]
    return jnp.stack([pieces[0]] + back, 0)


def per_device(queries, keys, values, conv_keys, conv_values, out_weight, cotangent):
    tokens = queries.shape[0]
    heads = queries.shape[1] // FEAT
    width = heads * VDIM
    columns = cotangent.shape[1]
    groups = lax.axis_size("head")
    rank = lax.axis_index("ctx") % PLANE
    places = [rank, lax.axis_index("head"), lax.axis_index("ctx") // PLANE]
    scalars = jnp.stack(places).astype(jnp.int32)
    piece_rows = heads // PLANE * ROWS
    message = (piece_rows + 4 * heads, VDIM)
    S = jax.ShapeDtypeStruct
    step = 2 * tokens * ROWS * VDIM * heads
    project_flops = 2 * tokens * width * columns
    dma = pltpu.SemaphoreType.DMA
    vmem = pltpu.VMEM
    slots = vmem((PLANE, piece_rows, VDIM), F32)

    with jax.named_scope("edge"):
        arrays = (keys, values, conv_keys, conv_values)
        spec = pl.BlockSpec(memory_space=vmem)
        last_rows, k_near, v_near, ck_near, cv_near = pl.pallas_call(
            edge_kernel,
            out_shape=[S((CONV - 1, keys.shape[1] + width), BF16)]
            + [S(x.shape, x.dtype) for x in arrays],
            in_specs=[pl.BlockSpec(memory_space=pltpu.HBM)] * 4,
            out_specs=[spec] * 5,
            scratch_shapes=[dma((4,))],
            compiler_params=pltpu.CompilerParams(vmem_limit_bytes=VMEM_LIMIT),
        )(*[in_hbm(x) for x in arrays])
        before = shifted(last_rows, "ctx", 1)
    with jax.named_scope("cotangent"):
        cots = [swapped(cotangent, "head", j) for j in range(1, groups)]
    with jax.named_scope("key_features"):
        outs = [
            S((heads, ROWS, tokens), BF16),
            S((tokens, width), BF16),
            S(message, F32),
            S((PLANE, *message), BF16),
        ]
        ops = (k_near, v_near, before, ck_near, cv_near)
        kf, vc, own, send = call(key_kernel, scalars, ops, outs, step, scratch=[slots])
    with jax.named_scope("query_features"):
        (qd,) = call(
            query_kernel,
            scalars,
            (after(queries, send),),
            [S((heads, ROWS, tokens), BF16)],
            step,
            far=(0,),
            scratch=[vmem(queries.shape, BF16), dma(())],
        )
    with jax.named_scope("prior_share"):
        got = [swapped(send[j], "ctx", j) for j in range(1, PLANE)]

        def join(norm_at, total, received, more):
            outs = [S(total.shape, BF16), S(total.shape, F32)]
            body = functools.partial(share_kernel, norm_at)
            made = call(body, scalars, (total, *received), outs[: 2 if more else 1], 1 << 20)
            return made if more else (made[0], None)

        more = lax.axis_size("ctx") > 4 * PLANE
        sent, total = join(piece_rows, own, got, more)
    with jax.named_scope("scores"):
        outs = [
            S((heads, tokens, tokens), BF16),
            S((heads, tokens), F32),
            S((tokens, width), F32),
        ]
        low, den, num = call(score_kernel, scalars, (qd, kf, vc), outs, 4 * step)
    with jax.named_scope("prior_planes"):
        sent = after(sent, den)
        norm_join = functools.partial(join, piece_rows)
        moved, strides = planes_ahead(total, sent, 1, norm_join)
    with jax.named_scope("out_grad"):
        ops = (after(cotangent, sent), *cots, out_weight)
        (out_grad,) = call(
            grad_kernel, scalars, ops, [S((tokens, width), F32)], groups * project_flops
        )
    with jax.named_scope("prior_back"):
        outs = [S((PLANE, piece_rows, VDIM), BF16), S((4 * heads, VDIM), F32)]
        body = functools.partial(piece_kernel, 1, strides)
        ops = (own, *got, after(moved[0], out_grad), *moved[1:])
        pieces, prior_norm = call(body, scalars, ops, outs, 1 << 20)
        prior = handed_back(pieces)
    with jax.named_scope("scaled_grad"):
        outs = [
            S((tokens, heads), F32),
            S((tokens, width), BF16),
            S((piece_rows, VDIM), F32),
            S((PLANE, piece_rows, VDIM), BF16),
        ]
        ops = (prior_norm, den, qd, out_grad)
        inverse, scaled, own_later, send_later = call(
            scale_kernel, scalars, ops, outs, step, scratch=[slots]
        )
    with jax.named_scope("later_share"):
        got_later = [swapped(send_later[j], "ctx", j) for j in range(1, PLANE)]
    with jax.named_scope("later_planes"):
        plain_join = functools.partial(join, None)
        sent_later, total_later = plain_join(own_later, got_later, more)
        moved_later, strides = planes_ahead(total_later, sent_later, -1, plain_join)
    with jax.named_scope("attended"):
        outs = [S((tokens, width), BF16), S((tokens, columns), BF16)]
        ops = (qd, prior, after(num, sent_later), inverse, out_weight)
        attended, part = call(attend_kernel, scalars, ops, outs, step + project_flops)
        parts = [swapped(part, "head", 1)]
    with jax.named_scope("near"):
        ops = (low, after(scaled, sent_later))
        (near,) = call(near_kernel, scalars, ops, [S((tokens, width), F32)], 2 * step)
    with jax.named_scope("mixed"):
        for j in list(range(2, groups)) + [0]:
            outs = [S((tokens, columns), BF16 if j else F32)]
            body = functools.partial(mix_kernel, j)
            ops = (after(attended, sent_later), out_weight)
            (part,) = call(body, scalars, ops, outs, 2 * project_flops)
            if j:
                parts.append(swapped(part, "head", j))
    with jax.named_scope("later_back"):
        outs = [S((PLANE, piece_rows, VDIM), BF16)]
        body = functools.partial(piece_kernel, -1, strides)
        ops = (own_later, *got_later, after(moved_later[0], part, near), *moved_later[1:])
        (pieces,) = call(body, scalars, ops, outs, 1 << 20)
        later = handed_back(pieces)
    with jax.named_scope("mixed_out"):
        mixed_out = part
        for other in parts:
            mixed_out = mixed_out + other.astype(F32)
        mixed_out = mixed_out.astype(BF16)
    with jax.named_scope("far_grad"):
        (value_grad,) = call(
            far_kernel, scalars, (after(kf, mixed_out), later, near), [S((tokens, width), BF16)], step
        )
    return mixed_out, value_grad


def solution(mesh):
    in_specs = (
        P("ctx", "head"),
        P("ctx", "head"),
        P("ctx", "head"),
        P(None, "head"),
        P(None, "head"),
        P("head", None),
        P("ctx", "head"),
    )
    out_specs = (P("ctx", "head"), P("ctx", "head"))
    return jax.shard_map(
        per_device, mesh=mesh, in_specs=in_specs, out_specs=out_specs, check_vma=False
    )
```

```python
import functools

import jax
import jax.numpy as jnp
from jax import lax
from jax.experimental import pallas as pl
from jax.experimental.pallas import tpu as pltpu
from jax.sharding import PartitionSpec as P

FEAT = 16
VDIM = 128
CONV = 3
ROWS = 160
VMEM_LIMIT = 14 * 1024 * 1024
PLANE = 4

F32 = jnp.float32
BF16 = jnp.bfloat16
TN = (((0,), (0,)), ((), ()))
NT = (((1,), (1,)), ((), ()))
NN = (((1,), (0,)), ((), ()))


def mm(a, b, dims):
    return lax.dot_general(a, b, dims, preferred_element_type=F32)


def call(body, scalars, operands, out_shape, flops, far=(), scratch=()):
    moved = sum(x.size * x.dtype.itemsize for x in operands)
    moved += sum(x.size * x.dtype.itemsize for x in out_shape)
    vmem = pl.BlockSpec(memory_space=pltpu.VMEM)
    hbm = pl.BlockSpec(memory_space=pltpu.HBM)
    return pl.pallas_call(
        body,
        out_shape=out_shape,
        in_specs=[pl.BlockSpec(memory_space=pltpu.SMEM)]
        + [hbm if i in far else vmem for i in range(len(operands))],
        out_specs=[vmem for _ in out_shape],
        scratch_shapes=list(scratch),
        compiler_params=pltpu.CompilerParams(vmem_limit_bytes=VMEM_LIMIT),
        cost_estimate=pl.CostEstimate(flops=flops, bytes_accessed=moved, transcendentals=0),
    )(scalars, *[in_hbm(x) if i in far else x for i, x in enumerate(operands)])


def in_hbm(x):
    return pltpu.with_memory_space_constraint(x, pltpu.HBM)


def fetch(source, target, sem):
    copy = pltpu.make_async_copy(source, target, sem)
    copy.start()
    return copy


def store_features(out_ref, rows_in, doubled):
    heads = rows_in.shape[0] // FEAT
    tokens = rows_in.shape[1]
    grid = rows_in.reshape(heads, FEAT, tokens) * FEAT ** (-0.25)
    twice = jnp.concatenate([grid, grid], 1)
    out_ref[:, 0:FEAT, :] = grid.astype(BF16)
    half = FEAT // 2
    for turn in range(half):
        square = grid * twice[:, turn : turn + FEAT, :] * 0.5**0.5
        if doubled and turn > 0:
            square = square * 2.0
        out_ref[:, FEAT * (turn + 1) : FEAT * (turn + 2), :] = square.astype(BF16)
    square = grid[:, :half, :] * grid[:, half:, :] * 0.5**0.5
    if doubled:
        square = square * 2.0
    first = lax.broadcasted_iota(jnp.int32, (heads, half, tokens), 1) == 0
    constant = jnp.where(first, 1.0, 0.0)
    out_ref[:, FEAT * (half + 1) :, :] = jnp.concatenate([square, constant], 1).astype(BF16)


def store_piece(rank, head, per_piece, state, own_ref, send_ref):
    slot = rank ^ (head // per_piece)
    at = (head % per_piece) * ROWS
    own_ref[slot, at : at + ROWS, :] = state
    send_ref[slot, at : at + ROWS, :] = state.astype(BF16)


def load_piece(rank, head, per_piece, ref):
    at = (head % per_piece) * ROWS
    return ref[rank ^ (head // per_piece), at : at + ROWS, :]


def edge_kernel(k_far, v_far, edge_ref, k_ref, v_ref, sems):
    tokens, width = k_far.shape
    deep = k_ref.shape[0]
    rows = pl.ds(tokens - deep, deep)
    copies = [fetch(k_far.at[rows], k_ref, sems.at[0]), fetch(v_far.at[rows], v_ref, sems.at[1])]
    last = deep - CONV + 1
    copies[0].wait()
    edge_ref[:, :width] = k_ref[...].astype(F32)[last:].astype(BF16)
    copies[1].wait()
    edge_ref[:, width:] = v_ref[...].astype(F32)[last:].astype(BF16)


def load_kernel(k_far, v_far, ck_far, cv_far, k_ref, v_ref, ck_ref, cv_ref, sems):
    pairs = ((k_far, k_ref), (v_far, v_ref), (ck_far, ck_ref), (cv_far, cv_ref))
    copies = [fetch(a, b, sems.at[i]) for i, (a, b) in enumerate(pairs)]
    for copy in copies:
        copy.wait()


def query_kernel(s_ref, q_far, qd_ref, q_ref, sem):
    fetch(q_far, q_ref, sem).wait()
    store_features(qd_ref, q_ref[...].astype(F32).T, True)


def columns_of(s_ref, w_ref, distance):
    columns = w_ref.shape[1] // lax.axis_size("head")
    return pl.ds(pl.multiple_of((s_ref[1] ^ distance) * columns, columns), columns)


def turn_kernel(s_ref, qd_ref, kf_ref, qt_ref, kt_ref):
    for head in range(qd_ref.shape[0]):
        qt_ref[head] = qd_ref[head].T
        kt_ref[head] = kf_ref[head].T


def grad_kernel(s_ref, *refs):
    *cots, w_ref, og_ref = refs
    total = None
    for j, cot_ref in enumerate(cots):
        term = mm(cot_ref[...], w_ref[:, columns_of(s_ref, w_ref, j)], NT)
        total = term if total is None else total + term
    og_ref[...] = total


def conv_rows(x, before, taps):
    x = x.astype(F32)
    row = lax.broadcasted_iota(jnp.int32, x.shape, 0)
    running = taps[0:1, :] * x
    for offset in range(1, CONV):
        moved = pltpu.roll(x, offset, 0)
        for at in range(offset):
            source = before[CONV - 1 - offset + at : CONV - offset + at, :]
            moved = jnp.where(row == at, source, moved)
        running = running + taps[offset : offset + 1, :] * moved
    return running


def norm_rows(norm):
    high = norm.astype(BF16).astype(F32)
    middle = (norm - high).astype(BF16).astype(F32)
    rest = norm - high - middle
    parts = (high, middle, rest)
    tail = [x[:, VDIM:] for x in parts]
    filler = jnp.zeros((norm.shape[0], VDIM - 3 * (ROWS - VDIM)), F32)
    tail = jnp.concatenate(tail + [filler], 1)
    return jnp.concatenate([x[:, :VDIM] for x in parts] + [tail], 0)


def norm_values(rows):
    heads = rows.shape[0] // 4
    extra = ROWS - VDIM
    tail = rows[3 * heads :]
    tail = tail[:, :extra] + tail[:, extra : 2 * extra] + tail[:, 2 * extra : 3 * extra]
    main = rows[:heads] + rows[heads : 2 * heads] + rows[2 * heads : 3 * heads]
    return jnp.concatenate([main, tail], 1)


def key_kernel(
    s_ref,
    k_ref,
    v_ref,
    before_ref,
    ck_ref,
    cv_ref,
    kf_ref,
    vc_ref,
    own_ref,
    send_ref,
    slots,
):
    rank = s_ref[0]
    heads = kf_ref.shape[0]
    per_piece = heads // PLANE
    width = k_ref.shape[1]
    before = before_ref[...].astype(F32)
    key_conv = conv_rows(k_ref[...], before[:, :width], ck_ref[...])
    store_features(kf_ref, key_conv.T, False)
    ones = jnp.ones((heads, k_ref.shape[0]), BF16)
    row = lax.broadcasted_iota(jnp.int32, (heads, ROWS), 0)
    norm = jnp.zeros((heads, ROWS), F32)
    for head in range(heads):
        at = head * VDIM
        value = conv_rows(
            v_ref[:, at : at + VDIM],
            before[:, width + at : width + at + VDIM],
            cv_ref[:, at : at + VDIM],
        ).astype(BF16)
        vc_ref[:, at : at + VDIM] = value
        feat = kf_ref[head]
        norm = jnp.where(row == head, mm(ones, feat, NT), norm)
        store_piece(rank, head, per_piece, mm(feat, value, NN), slots, send_ref)
    lines = norm_rows(norm)
    at = per_piece * ROWS
    own_ref[:at, :] = slots[0]
    own_ref[at:, :] = lines
    for slot in range(PLANE):
        send_ref[slot, at:, :] = lines.astype(BF16)


def share_kernel(norm_at, s_ref, own_ref, *refs):
    sent_at = -1 if refs[-1].dtype == BF16 else -2
    got_refs, sent_ref = refs[:sent_at], refs[sent_at]
    total = own_ref[...]
    for got_ref in got_refs:
        total = total + got_ref[...].astype(F32)
    if norm_at is not None:
        lines = norm_rows(norm_values(total[norm_at:]))
        total = jnp.concatenate([total[:norm_at], lines], 0)
    sent_ref[...] = total.astype(BF16)
    if sent_at == -2:
        refs[-1][...] = total


def store_pieces(sign, strides, s_ref, got_refs, moved_refs, pieces_ref):
    rows = pieces_ref.shape[1]

    def masked(ahead, ref):
        return jnp.where(ahead, ref[...].astype(F32), 0.0)

    def is_ahead(other, here):
        return other < here if sign > 0 else other > here

    before = jnp.zeros(got_refs[0].shape, F32)
    for ref, (stride, distance) in zip(moved_refs, strides):
        if distance:
            group = lax.div(s_ref[2], stride)
            before = before + masked(is_ahead(group ^ distance, group), ref)
        else:
            before = before + ref[...].astype(F32)
    rank = s_ref[0]
    extra = None
    for slot in range(PLANE):
        total = before
        for i in range(PLANE):
            if i != slot:
                total = total + masked(is_ahead(rank ^ i, rank ^ slot), got_refs[i])
        pieces_ref[slot] = total[:rows].astype(BF16)
        extra = total[rows:] if slot == 0 else extra
    return extra


def piece_kernel(sign, strides, s_ref, *refs):
    store_pieces(sign, strides, s_ref, refs[:PLANE], refs[PLANE:-1], refs[-1])


def score_kernel(s_ref, qd_ref, kf_ref, vc_ref, low_ref, den_ref, num_ref):
    heads = kf_ref.shape[0]
    tokens = kf_ref.shape[2]
    key_at = lax.broadcasted_iota(jnp.int32, (tokens, tokens), 0)
    query_at = lax.broadcasted_iota(jnp.int32, (tokens, tokens), 1)
    causal = key_at <= query_at
    for head in range(heads):
        scores = jnp.where(causal, mm(kf_ref[head], qd_ref[head], TN), 0.0)
        den_ref[head : head + 1, :] = jnp.sum(scores, 0, keepdims=True)
        low = scores.astype(BF16)
        low_ref[head] = low
        at = head * VDIM
        num_ref[:, at : at + VDIM] = mm(low, vc_ref[:, at : at + VDIM], TN)


def scale_kernel(strides, s_ref, den_ref, qd_ref, og_ref, *refs):
    *refs, pieces_ref, inv_ref, sg_ref, own_ref, send_ref, slots = refs
    rank = s_ref[0]
    heads = qd_ref.shape[0]
    per_piece = heads // PLANE
    lines = store_pieces(1, strides, s_ref, refs[:PLANE], refs[PLANE:], pieces_ref)
    norm = norm_values(lines)
    high = norm.astype(BF16).astype(F32)
    middle = (norm - high).astype(BF16).astype(F32)
    rest = norm - high - middle
    parts = jnp.concatenate([high, middle, rest, jnp.zeros_like(rest)], 0).astype(BF16)
    lines = []
    for head in range(heads):
        terms = mm(parts, qd_ref[head], NN)
        line = den_ref[head : head + 1, :] + terms[head : head + 1, :]
        line = line + terms[heads + head : heads + head + 1, :]
        lines.append(line + terms[2 * heads + head : 2 * heads + head + 1, :])
    inverse = (1.0 / jnp.concatenate(lines, 0)).T
    inv_ref[...] = inverse
    for head in range(heads):
        at = head * VDIM
        scaled = (og_ref[:, at : at + VDIM] * inverse[:, head : head + 1]).astype(BF16)
        sg_ref[:, at : at + VDIM] = scaled
        store_piece(rank, head, per_piece, mm(qd_ref[head], scaled, NN), slots, send_ref)
    own_ref[...] = slots[0]


def near_kernel(s_ref, low_ref, sg_ref, vg_ref):
    for head in range(low_ref.shape[0]):
        at = head * VDIM
        vg_ref[:, at : at + VDIM] = mm(low_ref[head], sg_ref[:, at : at + VDIM], NN)


def attend_kernel(s_ref, qt_ref, prior_ref, num_ref, inv_ref, w_ref, att_ref, part_ref):
    rank = s_ref[0]
    heads = qt_ref.shape[0]
    per_piece = heads // PLANE
    for head in range(heads):
        at = head * VDIM
        prior = load_piece(rank, head, per_piece, prior_ref)
        total = num_ref[:, at : at + VDIM] + mm(qt_ref[head], prior, NN)
        att_ref[:, at : at + VDIM] = (total * inv_ref[:, head : head + 1]).astype(BF16)
    part_ref[...] = mm(att_ref[...], w_ref[:, columns_of(s_ref, w_ref, 1)], NN).astype(BF16)


def mix_kernel(distance, s_ref, att_ref, w_ref, part_ref):
    weight = w_ref[:, columns_of(s_ref, w_ref, distance)]
    part_ref[...] = mm(att_ref[...], weight, NN).astype(part_ref.dtype)


def last_kernel(s_ref, kt_ref, later_ref, near_ref, part_ref, *refs):
    *other_refs, vg_far, mixed_far, vg_ref, mixed_ref, sems = refs
    rank = s_ref[0]
    heads = kt_ref.shape[0]
    per_piece = heads // PLANE
    copies = []
    for head in range(heads):
        at = head * VDIM
        later = load_piece(rank, head, per_piece, later_ref)
        total = near_ref[:, at : at + VDIM] + mm(kt_ref[head], later, NN)
        vg_ref[:, at : at + VDIM] = total.astype(BF16)
        if head % per_piece == per_piece - 1:
            columns = pl.ds((head + 1 - per_piece) * VDIM, per_piece * VDIM)
            sem = sems.at[head // per_piece]
            copies.append(fetch(vg_ref.at[:, columns], vg_far.at[:, columns], sem))
    deep = part_ref.shape[0] // PLANE
    for step in range(PLANE):
        total = part_ref[step * deep : (step + 1) * deep, :]
        for other_ref in other_refs:
            total = total + other_ref[step * deep : (step + 1) * deep, :].astype(F32)
        mixed_ref[step * deep : (step + 1) * deep, :] = total.astype(BF16)
        rows = pl.ds(step * deep, deep)
        sem = sems.at[PLANE + step]
        copies.append(fetch(mixed_ref.at[rows], mixed_far.at[rows], sem))
    for copy in copies:
        copy.wait()


def shifted(x, axis, by):
    peers = lax.axis_size(axis)
    pairs = [(i, i + by) for i in range(peers) if 0 <= i + by < peers]
    return lax.ppermute(x, axis, pairs)


def after(x, *others):
    return lax.optimization_barrier((x, *others))[0]


def planes_ahead(total, sent, sign, join):
    planes = lax.axis_size("ctx") // PLANE
    received, strides = [], []
    stride = 1
    while stride < planes:
        if (planes // stride) % 4 == 0:
            moved = [swapped(sent, "ctx", j, stride * PLANE) for j in range(1, 4)]
            strides += [(stride, j) for j in range(1, 4)]
            stride = stride * 4
        else:
            moved = [shifted(sent, "ctx", sign * stride * PLANE)]
            strides.append((stride, 0))
            stride = stride * 2
        received += moved
        if stride < planes:
            sent, total = join(total, moved, stride * 2 < planes)
    return received, strides


def swapped(x, axis, distance, stride=1):
    peers = lax.axis_size(axis)
    pairs = [(i, (i // stride ^ distance) * stride + i % stride) for i in range(peers)]
    return lax.ppermute(x, axis, pairs)


def handed_back(pieces):
    back = [swapped(pieces[j], "ctx", j) for j in range(1, PLANE)]
    return jnp.stack([pieces[0]] + back, 0)


def per_device(queries, keys, values, conv_keys, conv_values, out_weight, cotangent):
    tokens = queries.shape[0]
    heads = queries.shape[1] // FEAT
    width = heads * VDIM
    columns = cotangent.shape[1]
    groups = lax.axis_size("head")
    rank = lax.axis_index("ctx") % PLANE
    places = [rank, lax.axis_index("head"), lax.axis_index("ctx") // PLANE]
    scalars = jnp.stack(places).astype(jnp.int32)
    piece_rows = heads // PLANE * ROWS
    message = (piece_rows + 4 * heads, VDIM)
    S = jax.ShapeDtypeStruct
    step = 2 * tokens * ROWS * VDIM * heads
    project_flops = 2 * tokens * width * columns
    dma = pltpu.SemaphoreType.DMA
    vmem = pltpu.VMEM
    slots = vmem((PLANE, piece_rows, VDIM), F32)

    with jax.named_scope("edge"):
        last_rows = pl.pallas_call(
            edge_kernel,
            out_shape=S((CONV - 1, keys.shape[1] + width), BF16),
            in_specs=[pl.BlockSpec(memory_space=pltpu.HBM)] * 2,
            out_specs=pl.BlockSpec(memory_space=vmem),
            scratch_shapes=[vmem((16, keys.shape[1]), BF16), vmem((16, width), BF16), dma((2,))],
            compiler_params=pltpu.CompilerParams(vmem_limit_bytes=VMEM_LIMIT),
        )(in_hbm(keys), in_hbm(values))
        before = shifted(last_rows, "ctx", 1)
    with jax.named_scope("load"):
        arrays = (after(keys, last_rows), values, conv_keys, conv_values)
        near_by = pl.pallas_call(
            load_kernel,
            out_shape=[S(x.shape, x.dtype) for x in arrays],
            in_specs=[pl.BlockSpec(memory_space=pltpu.HBM)] * 4,
            out_specs=[pl.BlockSpec(memory_space=vmem)] * 4,
            scratch_shapes=[dma((4,))],
            compiler_params=pltpu.CompilerParams(vmem_limit_bytes=VMEM_LIMIT),
            cost_estimate=pl.CostEstimate(flops=1 << 20, bytes_accessed=1 << 20, transcendentals=0),
        )(*[in_hbm(x) for x in arrays])
    with jax.named_scope("cotangent"):
        cots = [swapped(cotangent, "head", j) for j in range(1, groups)]
    with jax.named_scope("key_features"):
        outs = [
            S((heads, ROWS, tokens), BF16),
            S((tokens, width), BF16),
            S(message, F32),
            S((PLANE, *message), BF16),
        ]
        ops = (*near_by[:2], before, *near_by[2:])
        kf, vc, own, send = call(key_kernel, scalars, ops, outs, step, scratch=[slots])
    with jax.named_scope("query_features"):
        (qd,) = call(
            query_kernel,
            scalars,
            (after(queries, send),),
            [S((heads, ROWS, tokens), BF16)],
            step,
            far=(0,),
            scratch=[vmem(queries.shape, BF16), dma(())],
        )
    with jax.named_scope("prior_share"):
        got = [swapped(send[j], "ctx", j) for j in range(1, PLANE)]

        def join(norm_at, total, received, more):
            outs = [S(total.shape, BF16), S(total.shape, F32)]
            body = functools.partial(share_kernel, norm_at)
            made = call(body, scalars, (total, *received), outs[: 2 if more else 1], 1 << 20)
            return made if more else (made[0], None)

        more = lax.axis_size("ctx") > 4 * PLANE
        sent, total = join(piece_rows, own, got, more)
    with jax.named_scope("scores"):
        outs = [
            S((heads, tokens, tokens), BF16),
            S((heads, tokens), F32),
            S((tokens, width), F32),
        ]
        low, den, num = call(score_kernel, scalars, (qd, kf, vc), outs, 4 * step)
    with jax.named_scope("prior_planes"):
        sent = after(sent, den)
        norm_join = functools.partial(join, piece_rows)
        moved, strides = planes_ahead(total, sent, 1, norm_join)
    with jax.named_scope("out_grad"):
        ops = (after(cotangent, sent), *cots, out_weight)
        (out_grad,) = call(
            grad_kernel, scalars, ops, [S((tokens, width), F32)], groups * project_flops
        )
    with jax.named_scope("turned"):
        outs = [S((heads, tokens, ROWS), BF16)] * 2
        qt, kt = call(turn_kernel, scalars, (after(qd, out_grad), kf), outs, 1 << 22)
    with jax.named_scope("scaled_grad"):
        outs = [
            S((PLANE, piece_rows, VDIM), BF16),
            S((tokens, heads), F32),
            S((tokens, width), BF16),
            S((piece_rows, VDIM), F32),
            S((PLANE, piece_rows, VDIM), BF16),
        ]
        ops = (den, after(qd, qt), out_grad, own, *got, *moved)
        body = functools.partial(scale_kernel, strides)
        pieces, inverse, scaled, own_later, send_later = call(
            body, scalars, ops, outs, step, scratch=[slots]
        )
        prior = handed_back(pieces)
    with jax.named_scope("later_share"):
        got_later = [swapped(send_later[j], "ctx", j) for j in range(1, PLANE)]
    with jax.named_scope("later_planes"):
        plain_join = functools.partial(join, None)
        sent_later, total_later = plain_join(own_later, got_later, more)
        moved_later, strides = planes_ahead(total_later, sent_later, -1, plain_join)
    with jax.named_scope("attended"):
        outs = [S((tokens, width), BF16), S((tokens, columns), BF16)]
        ops = (qt, prior, after(num, sent_later), inverse, out_weight)
        attended, part = call(attend_kernel, scalars, ops, outs, step + project_flops)
        parts = [swapped(part, "head", 1)]
    with jax.named_scope("near"):
        ops = (low, after(scaled, sent_later))
        (near,) = call(near_kernel, scalars, ops, [S((tokens, width), F32)], 2 * step)
    with jax.named_scope("mixed"):
        for j in list(range(2, groups)) + [0]:
            outs = [S((tokens, columns), BF16 if j else F32)]
            body = functools.partial(mix_kernel, j)
            ops = (after(attended, sent_later), out_weight)
            (part,) = call(body, scalars, ops, outs, 2 * project_flops)
            if j:
                parts.append(swapped(part, "head", j))
    with jax.named_scope("later_back"):
        outs = [S((PLANE, piece_rows, VDIM), BF16)]
        body = functools.partial(piece_kernel, -1, strides)
        ops = (own_later, *got_later, after(moved_later[0], part, near), *moved_later[1:])
        (pieces,) = call(body, scalars, ops, outs, 1 << 20)
        later = handed_back(pieces)
    with jax.named_scope("last"):
        whole = (tokens, columns)
        value_grad, mixed_out = pl.pallas_call(
            last_kernel,
            out_shape=[S((tokens, width), BF16), S(whole, BF16)],
            in_specs=[pl.BlockSpec(memory_space=pltpu.SMEM)]
            + [pl.BlockSpec(memory_space=vmem)] * (4 + len(parts)),
            out_specs=[pl.BlockSpec(memory_space=pltpu.HBM)] * 2,
            scratch_shapes=[
                vmem((tokens, width), BF16),
                vmem(whole, BF16),
                dma((2 * PLANE,)),
            ],
            compiler_params=pltpu.CompilerParams(vmem_limit_bytes=VMEM_LIMIT),
        )(scalars, kt, later, near, part, *parts)
    return mixed_out, value_grad


def solution(mesh):
    in_specs = (
        P("ctx", "head"),
        P("ctx", "head"),
        P("ctx", "head"),
        P(None, "head"),
        P(None, "head"),
        P("head", None),
        P("ctx", "head"),
    )
    out_specs = (P("ctx", "head"), P("ctx", "head"))
    return jax.shard_map(
        per_device, mesh=mesh, in_specs=in_specs, out_specs=out_specs, check_vma=False
    )
```

```python
import functools

import jax
import jax.numpy as jnp
from jax import lax
from jax.experimental import pallas as pl
from jax.experimental.pallas import tpu as pltpu
from jax.sharding import PartitionSpec as P

FEAT = 16
VDIM = 128
CONV = 3
ROWS = 160
VMEM_LIMIT = 14 * 1024 * 1024
PLANE = 4

F32 = jnp.float32
BF16 = jnp.bfloat16
TN = (((0,), (0,)), ((), ()))
NT = (((1,), (1,)), ((), ()))
NN = (((1,), (0,)), ((), ()))


def mm(a, b, dims):
    return lax.dot_general(a, b, dims, preferred_element_type=F32)


def call(body, scalars, operands, out_shape, flops, far=(), scratch=()):
    moved = sum(x.size * x.dtype.itemsize for x in operands)
    moved += sum(x.size * x.dtype.itemsize for x in out_shape)
    vmem = pl.BlockSpec(memory_space=pltpu.VMEM)
    hbm = pl.BlockSpec(memory_space=pltpu.HBM)
    return pl.pallas_call(
        body,
        out_shape=out_shape,
        in_specs=[pl.BlockSpec(memory_space=pltpu.SMEM)]
        + [hbm if i in far else vmem for i in range(len(operands))],
        out_specs=[vmem for _ in out_shape],
        scratch_shapes=list(scratch),
        compiler_params=pltpu.CompilerParams(vmem_limit_bytes=VMEM_LIMIT),
        cost_estimate=pl.CostEstimate(flops=flops, bytes_accessed=moved, transcendentals=0),
    )(scalars, *[in_hbm(x) if i in far else x for i, x in enumerate(operands)])


def in_hbm(x):
    return pltpu.with_memory_space_constraint(x, pltpu.HBM)


def fetch(source, target, sem):
    copy = pltpu.make_async_copy(source, target, sem)
    copy.start()
    return copy


def store_features(out_ref, rows_in, doubled):
    heads = rows_in.shape[0] // FEAT
    tokens = rows_in.shape[1]
    grid = rows_in.reshape(heads, FEAT, tokens) * FEAT ** (-0.25)
    twice = jnp.concatenate([grid, grid], 1)
    out_ref[:, 0:FEAT, :] = grid.astype(BF16)
    half = FEAT // 2
    for turn in range(half):
        square = grid * twice[:, turn : turn + FEAT, :] * 0.5**0.5
        if doubled and turn > 0:
            square = square * 2.0
        out_ref[:, FEAT * (turn + 1) : FEAT * (turn + 2), :] = square.astype(BF16)
    square = grid[:, :half, :] * grid[:, half:, :] * 0.5**0.5
    if doubled:
        square = square * 2.0
    first = lax.broadcasted_iota(jnp.int32, (heads, half, tokens), 1) == 0
    constant = jnp.where(first, 1.0, 0.0)
    out_ref[:, FEAT * (half + 1) :, :] = jnp.concatenate([square, constant], 1).astype(BF16)


def store_piece(rank, head, per_piece, state, own_ref, send_ref):
    slot = rank ^ (head // per_piece)
    at = (head % per_piece) * ROWS
    own_ref[slot, at : at + ROWS, :] = state
    send_ref[slot, at : at + ROWS, :] = state.astype(BF16)


def load_piece(rank, head, per_piece, ref):
    at = (head % per_piece) * ROWS
    return ref[rank ^ (head // per_piece), at : at + ROWS, :]


def edge_kernel(k_far, v_far, edge_ref, k_ref, v_ref, sems):
    tokens, width = k_far.shape
    deep = k_ref.shape[0]
    rows = pl.ds(tokens - deep, deep)
    copies = [fetch(k_far.at[rows], k_ref, sems.at[0]), fetch(v_far.at[rows], v_ref, sems.at[1])]
    last = deep - CONV + 1
    copies[0].wait()
    edge_ref[:, :width] = k_ref[...].astype(F32)[last:].astype(BF16)
    copies[1].wait()
    edge_ref[:, width:] = v_ref[...].astype(F32)[last:].astype(BF16)


def load_kernel(k_far, v_far, ck_far, cv_far, k_ref, v_ref, ck_ref, cv_ref, sems):
    pairs = ((k_far, k_ref), (v_far, v_ref), (ck_far, ck_ref), (cv_far, cv_ref))
    copies = [fetch(a, b, sems.at[i]) for i, (a, b) in enumerate(pairs)]
    for copy in copies:
        copy.wait()


def query_kernel(
    s_ref,
    q_far,
    k_far,
    v_far,
    ck_far,
    cv_far,
    qd_ref,
    k_ref,
    v_ref,
    ck_ref,
    cv_ref,
    q_ref,
    sems,
):
    far = (q_far, k_far, v_far, ck_far, cv_far)
    near = (q_ref, k_ref, v_ref, ck_ref, cv_ref)
    copies = [fetch(a, b, sems.at[i]) for i, (a, b) in enumerate(zip(far, near))]
    copies[0].wait()
    store_features(qd_ref, q_ref[...].astype(F32).T, True)
    for copy in copies[1:]:
        copy.wait()


def columns_of(s_ref, w_ref, distance):
    columns = w_ref.shape[1] // lax.axis_size("head")
    return pl.ds(pl.multiple_of((s_ref[1] ^ distance) * columns, columns), columns)


def turn_kernel(s_ref, qd_ref, kf_ref, qt_ref, kt_ref):
    for head in range(qd_ref.shape[0]):
        qt_ref[head] = qd_ref[head].T
        kt_ref[head] = kf_ref[head].T


def grad_kernel(s_ref, *refs):
    *cots, w_ref, og_ref = refs
    total = None
    for j, cot_ref in enumerate(cots):
        term = mm(cot_ref[...], w_ref[:, columns_of(s_ref, w_ref, j)], NT)
        total = term if total is None else total + term
    og_ref[...] = total


def conv_rows(x, before, taps):
    x = x.astype(F32)
    row = lax.broadcasted_iota(jnp.int32, x.shape, 0)
    running = taps[0:1, :] * x
    for offset in range(1, CONV):
        moved = pltpu.roll(x, offset, 0)
        for at in range(offset):
            source = before[CONV - 1 - offset + at : CONV - offset + at, :]
            moved = jnp.where(row == at, source, moved)
        running = running + taps[offset : offset + 1, :] * moved
    return running


def norm_rows(norm):
    high = norm.astype(BF16).astype(F32)
    middle = (norm - high).astype(BF16).astype(F32)
    rest = norm - high - middle
    parts = (high, middle, rest)
    tail = [x[:, VDIM:] for x in parts]
    filler = jnp.zeros((norm.shape[0], VDIM - 3 * (ROWS - VDIM)), F32)
    tail = jnp.concatenate(tail + [filler], 1)
    return jnp.concatenate([x[:, :VDIM] for x in parts] + [tail], 0)


def norm_values(rows):
    heads = rows.shape[0] // 4
    extra = ROWS - VDIM
    tail = rows[3 * heads :]
    tail = tail[:, :extra] + tail[:, extra : 2 * extra] + tail[:, 2 * extra : 3 * extra]
    main = rows[:heads] + rows[heads : 2 * heads] + rows[2 * heads : 3 * heads]
    return jnp.concatenate([main, tail], 1)


def key_kernel(
    s_ref,
    k_ref,
    v_ref,
    before_ref,
    ck_ref,
    cv_ref,
    kf_ref,
    vc_ref,
    own_ref,
    send_ref,
    slots,
):
    rank = s_ref[0]
    heads = kf_ref.shape[0]
    per_piece = heads // PLANE
    width = k_ref.shape[1]
    before = before_ref[...].astype(F32)
    key_conv = conv_rows(k_ref[...], before[:, :width], ck_ref[...])
    store_features(kf_ref, key_conv.T, False)
    ones = jnp.ones((heads, k_ref.shape[0]), BF16)
    row = lax.broadcasted_iota(jnp.int32, (heads, ROWS), 0)
    norm = jnp.zeros((heads, ROWS), F32)
    for head in range(heads):
        at = head * VDIM
        value = conv_rows(
            v_ref[:, at : at + VDIM],
            before[:, width + at : width + at + VDIM],
            cv_ref[:, at : at + VDIM],
        ).astype(BF16)
        vc_ref[:, at : at + VDIM] = value
        feat = kf_ref[head]
        norm = jnp.where(row == head, mm(ones, feat, NT), norm)
        store_piece(rank, head, per_piece, mm(feat, value, NN), slots, send_ref)
    lines = norm_rows(norm)
    at = per_piece * ROWS
    own_ref[:at, :] = slots[0]
    own_ref[at:, :] = lines
    for slot in range(PLANE):
        send_ref[slot, at:, :] = lines.astype(BF16)


def share_kernel(norm_at, s_ref, own_ref, *refs):
    sent_at = -1 if refs[-1].dtype == BF16 else -2
    got_refs, sent_ref = refs[:sent_at], refs[sent_at]
    total = own_ref[...]
    for got_ref in got_refs:
        total = total + got_ref[...].astype(F32)
    if norm_at is not None:
        lines = norm_rows(norm_values(total[norm_at:]))
        total = jnp.concatenate([total[:norm_at], lines], 0)
    sent_ref[...] = total.astype(BF16)
    if sent_at == -2:
        refs[-1][...] = total


def store_pieces(sign, strides, s_ref, got_refs, moved_refs, pieces_ref):
    rows = pieces_ref.shape[1]

    def masked(ahead, ref):
        return jnp.where(ahead, ref[...].astype(F32), 0.0)

    def is_ahead(other, here):
        return other < here if sign > 0 else other > here

    before = jnp.zeros(got_refs[0].shape, F32)
    for ref, (stride, distance) in zip(moved_refs, strides):
        if distance:
            group = lax.div(s_ref[2], stride)
            before = before + masked(is_ahead(group ^ distance, group), ref)
        else:
            before = before + ref[...].astype(F32)
    rank = s_ref[0]
    extra = None
    for slot in range(PLANE):
        total = before
        for i in range(PLANE):
            if i != slot:
                total = total + masked(is_ahead(rank ^ i, rank ^ slot), got_refs[i])
        pieces_ref[slot] = total[:rows].astype(BF16)
        extra = total[rows:] if slot == 0 else extra
    return extra


def piece_kernel(sign, strides, s_ref, *refs):
    store_pieces(sign, strides, s_ref, refs[:PLANE], refs[PLANE:-1], refs[-1])


def score_kernel(s_ref, qd_ref, kf_ref, vc_ref, low_ref, den_ref, num_ref):
    heads = kf_ref.shape[0]
    tokens = kf_ref.shape[2]
    key_at = lax.broadcasted_iota(jnp.int32, (tokens, tokens), 0)
    query_at = lax.broadcasted_iota(jnp.int32, (tokens, tokens), 1)
    causal = key_at <= query_at
    for head in range(heads):
        scores = jnp.where(causal, mm(kf_ref[head], qd_ref[head], TN), 0.0)
        den_ref[head : head + 1, :] = jnp.sum(scores, 0, keepdims=True)
        low = scores.astype(BF16)
        low_ref[head] = low
        at = head * VDIM
        num_ref[:, at : at + VDIM] = mm(low, vc_ref[:, at : at + VDIM], TN)


def scale_kernel(strides, s_ref, den_ref, qd_ref, og_ref, *refs):
    *refs, pieces_ref, inv_ref, sg_ref, own_ref, send_ref, slots = refs
    rank = s_ref[0]
    heads = qd_ref.shape[0]
    per_piece = heads // PLANE
    lines = store_pieces(1, strides, s_ref, refs[:PLANE], refs[PLANE:], pieces_ref)
    norm = norm_values(lines)
    high = norm.astype(BF16).astype(F32)
    middle = (norm - high).astype(BF16).astype(F32)
    rest = norm - high - middle
    parts = jnp.concatenate([high, middle, rest, jnp.zeros_like(rest)], 0).astype(BF16)
    lines = []
    for head in range(heads):
        terms = mm(parts, qd_ref[head], NN)
        line = den_ref[head : head + 1, :] + terms[head : head + 1, :]
        line = line + terms[heads + head : heads + head + 1, :]
        lines.append(line + terms[2 * heads + head : 2 * heads + head + 1, :])
    inverse = (1.0 / jnp.concatenate(lines, 0)).T
    inv_ref[...] = inverse
    for head in range(heads):
        at = head * VDIM
        scaled = (og_ref[:, at : at + VDIM] * inverse[:, head : head + 1]).astype(BF16)
        sg_ref[:, at : at + VDIM] = scaled
        store_piece(rank, head, per_piece, mm(qd_ref[head], scaled, NN), slots, send_ref)
    own_ref[...] = slots[0]


def near_kernel(s_ref, low_ref, sg_ref, vg_ref):
    for head in range(low_ref.shape[0]):
        at = head * VDIM
        vg_ref[:, at : at + VDIM] = mm(low_ref[head], sg_ref[:, at : at + VDIM], NN)


def attend_kernel(s_ref, qt_ref, prior_ref, num_ref, inv_ref, w_ref, att_ref, part_ref):
    rank = s_ref[0]
    heads = qt_ref.shape[0]
    per_piece = heads // PLANE
    for head in range(heads):
        at = head * VDIM
        prior = load_piece(rank, head, per_piece, prior_ref)
        total = num_ref[:, at : at + VDIM] + mm(qt_ref[head], prior, NN)
        att_ref[:, at : at + VDIM] = (total * inv_ref[:, head : head + 1]).astype(BF16)
    part_ref[...] = mm(att_ref[...], w_ref[:, columns_of(s_ref, w_ref, 1)], NN).astype(BF16)


def mix_kernel(distance, s_ref, att_ref, w_ref, part_ref):
    weight = w_ref[:, columns_of(s_ref, w_ref, distance)]
    part_ref[...] = mm(att_ref[...], weight, NN).astype(part_ref.dtype)


def last_kernel(s_ref, kt_ref, later_ref, near_ref, part_ref, *refs):
    *other_refs, vg_far, mixed_far, vg_ref, mixed_ref, sems = refs
    rank = s_ref[0]
    heads = kt_ref.shape[0]
    per_piece = heads // PLANE
    copies = []
    for head in range(heads):
        at = head * VDIM
        later = load_piece(rank, head, per_piece, later_ref)
        total = near_ref[:, at : at + VDIM] + mm(kt_ref[head], later, NN)
        vg_ref[:, at : at + VDIM] = total.astype(BF16)
        if head % per_piece == per_piece - 1:
            columns = pl.ds((head + 1 - per_piece) * VDIM, per_piece * VDIM)
            sem = sems.at[head // per_piece]
            copies.append(fetch(vg_ref.at[:, columns], vg_far.at[:, columns], sem))
    deep = part_ref.shape[0] // PLANE
    for step in range(PLANE):
        total = part_ref[step * deep : (step + 1) * deep, :]
        for other_ref in other_refs:
            total = total + other_ref[step * deep : (step + 1) * deep, :].astype(F32)
        mixed_ref[step * deep : (step + 1) * deep, :] = total.astype(BF16)
        rows = pl.ds(step * deep, deep)
        sem = sems.at[PLANE + step]
        copies.append(fetch(mixed_ref.at[rows], mixed_far.at[rows], sem))
    for copy in copies:
        copy.wait()


def shifted(x, axis, by):
    peers = lax.axis_size(axis)
    pairs = [(i, i + by) for i in range(peers) if 0 <= i + by < peers]
    return lax.ppermute(x, axis, pairs)


def after(x, *others):
    return lax.optimization_barrier((x, *others))[0]


def planes_ahead(total, sent, sign, join):
    planes = lax.axis_size("ctx") // PLANE
    received, strides = [], []
    stride = 1
    while stride < planes:
        if (planes // stride) % 4 == 0:
            moved = [swapped(sent, "ctx", j, stride * PLANE) for j in range(1, 4)]
            strides += [(stride, j) for j in range(1, 4)]
            stride = stride * 4
        else:
            moved = [shifted(sent, "ctx", sign * stride * PLANE)]
            strides.append((stride, 0))
            stride = stride * 2
        received += moved
        if stride < planes:
            sent, total = join(total, moved, stride * 2 < planes)
    return received, strides


def swapped(x, axis, distance, stride=1):
    peers = lax.axis_size(axis)
    pairs = [(i, (i // stride ^ distance) * stride + i % stride) for i in range(peers)]
    return lax.ppermute(x, axis, pairs)


def handed_back(pieces):
    back = [swapped(pieces[j], "ctx", j) for j in range(1, PLANE)]
    return jnp.stack([pieces[0]] + back, 0)


def per_device(queries, keys, values, conv_keys, conv_values, out_weight, cotangent):
    tokens = queries.shape[0]
    heads = queries.shape[1] // FEAT
    width = heads * VDIM
    columns = cotangent.shape[1]
    groups = lax.axis_size("head")
    rank = lax.axis_index("ctx") % PLANE
    places = [rank, lax.axis_index("head"), lax.axis_index("ctx") // PLANE]
    scalars = jnp.stack(places).astype(jnp.int32)
    piece_rows = heads // PLANE * ROWS
    message = (piece_rows + 4 * heads, VDIM)
    S = jax.ShapeDtypeStruct
    step = 2 * tokens * ROWS * VDIM * heads
    project_flops = 2 * tokens * width * columns
    dma = pltpu.SemaphoreType.DMA
    vmem = pltpu.VMEM
    slots = vmem((PLANE, piece_rows, VDIM), F32)

    with jax.named_scope("edge"):
        last_rows = pl.pallas_call(
            edge_kernel,
            out_shape=S((CONV - 1, keys.shape[1] + width), BF16),
            in_specs=[pl.BlockSpec(memory_space=pltpu.HBM)] * 2,
            out_specs=pl.BlockSpec(memory_space=vmem),
            scratch_shapes=[vmem((16, keys.shape[1]), BF16), vmem((16, width), BF16), dma((2,))],
            compiler_params=pltpu.CompilerParams(vmem_limit_bytes=VMEM_LIMIT),
        )(in_hbm(keys), in_hbm(values))
        before = shifted(last_rows, "ctx", 1)
    with jax.named_scope("query_features"):
        arrays = (keys, values, conv_keys, conv_values)
        qd, *near_by = call(
            query_kernel,
            scalars,
            (after(queries, last_rows), *arrays),
            [S((heads, ROWS, tokens), BF16)] + [S(x.shape, x.dtype) for x in arrays],
            1 << 20,
            far=range(5),
            scratch=[vmem(queries.shape, BF16), dma((5,))],
        )
    with jax.named_scope("key_features"):
        outs = [
            S((heads, ROWS, tokens), BF16),
            S((tokens, width), BF16),
            S(message, F32),
            S((PLANE, *message), BF16),
        ]
        ops = (*near_by[:2], before, *near_by[2:])
        kf, vc, own, send = call(key_kernel, scalars, ops, outs, step, scratch=[slots])
    with jax.named_scope("cotangent"):
        cots = [swapped(after(cotangent, send), "head", j) for j in range(1, groups)]
    with jax.named_scope("prior_share"):
        got = [swapped(send[j], "ctx", j) for j in range(1, PLANE)]

        def join(norm_at, total, received, more):
            outs = [S(total.shape, BF16), S(total.shape, F32)]
            body = functools.partial(share_kernel, norm_at)
            made = call(body, scalars, (total, *received), outs[: 2 if more else 1], 1 << 20)
            return made if more else (made[0], None)

        more = lax.axis_size("ctx") > 4 * PLANE
        sent, total = join(piece_rows, own, got, more)
    with jax.named_scope("scores"):
        outs = [
            S((heads, tokens, tokens), BF16),
            S((heads, tokens), F32),
            S((tokens, width), F32),
        ]
        low, den, num = call(score_kernel, scalars, (qd, kf, vc), outs, 400 * step)
    with jax.named_scope("prior_planes"):
        sent = after(sent, den)
        norm_join = functools.partial(join, piece_rows)
        moved, strides = planes_ahead(total, sent, 1, norm_join)
    with jax.named_scope("turned"):
        outs = [S((heads, tokens, ROWS), BF16)] * 2
        qt, kt = call(turn_kernel, scalars, (after(qd, sent), kf), outs, 1 << 22)
    with jax.named_scope("out_grad"):
        ops = (after(cotangent, qt), *cots, out_weight)
        (out_grad,) = call(
            grad_kernel, scalars, ops, [S((tokens, width), F32)], groups * project_flops
        )
    with jax.named_scope("scaled_grad"):
        outs = [
            S((PLANE, piece_rows, VDIM), BF16),
            S((tokens, heads), F32),
            S((tokens, width), BF16),
            S((piece_rows, VDIM), F32),
            S((PLANE, piece_rows, VDIM), BF16),
        ]
        ops = (den, qd, out_grad, own, *got, *moved)
        body = functools.partial(scale_kernel, strides)
        pieces, inverse, scaled, own_later, send_later = call(
            body, scalars, ops, outs, step, scratch=[slots]
        )
        prior = handed_back(pieces)
    with jax.named_scope("later_share"):
        got_later = [swapped(send_later[j], "ctx", j) for j in range(1, PLANE)]
    with jax.named_scope("later_planes"):
        plain_join = functools.partial(join, None)
        sent_later, total_later = plain_join(own_later, got_later, more)
        moved_later, strides = planes_ahead(total_later, sent_later, -1, plain_join)
    with jax.named_scope("attended"):
        outs = [S((tokens, width), BF16), S((tokens, columns), BF16)]
        ops = (qt, prior, after(num, sent_later), inverse, out_weight)
        attended, part = call(attend_kernel, scalars, ops, outs, step + project_flops)
        parts = [swapped(part, "head", 1)]
    with jax.named_scope("near"):
        ops = (low, after(scaled, sent_later))
        (near,) = call(near_kernel, scalars, ops, [S((tokens, width), F32)], 2 * step)
    with jax.named_scope("mixed"):
        for j in list(range(2, groups)) + [0]:
            outs = [S((tokens, columns), BF16 if j else F32)]
            body = functools.partial(mix_kernel, j)
            ops = (after(attended, sent_later), out_weight)
            (part,) = call(body, scalars, ops, outs, 2 * project_flops)
            if j:
                parts.append(swapped(part, "head", j))
    with jax.named_scope("later_back"):
        outs = [S((PLANE, piece_rows, VDIM), BF16)]
        body = functools.partial(piece_kernel, -1, strides)
        ops = (own_later, *got_later, after(moved_later[0], part, near), *moved_later[1:])
        (pieces,) = call(body, scalars, ops, outs, 1 << 20)
        later = handed_back(pieces)
    with jax.named_scope("last"):
        whole = (tokens, columns)
        value_grad, mixed_out = pl.pallas_call(
            last_kernel,
            out_shape=[S((tokens, width), BF16), S(whole, BF16)],
            in_specs=[pl.BlockSpec(memory_space=pltpu.SMEM)]
            + [pl.BlockSpec(memory_space=vmem)] * (4 + len(parts)),
            out_specs=[pl.BlockSpec(memory_space=pltpu.HBM)] * 2,
            scratch_shapes=[
                vmem((tokens, width), BF16),
                vmem(whole, BF16),
                dma((2 * PLANE,)),
            ],
            compiler_params=pltpu.CompilerParams(vmem_limit_bytes=VMEM_LIMIT),
        )(scalars, kt, later, near, part, *parts)
    return mixed_out, value_grad


def solution(mesh):
    in_specs = (
        P("ctx", "head"),
        P("ctx", "head"),
        P("ctx", "head"),
        P(None, "head"),
        P(None, "head"),
        P("head", None),
        P("ctx", "head"),
    )
    out_specs = (P("ctx", "head"), P("ctx", "head"))
    return jax.shard_map(
        per_device, mesh=mesh, in_specs=in_specs, out_specs=out_specs, check_vma=False
    )
```

```python
import functools

import jax
import jax.numpy as jnp
from jax import lax
from jax.experimental import pallas as pl
from jax.experimental.pallas import tpu as pltpu
from jax.sharding import PartitionSpec as P

FEAT = 16
VDIM = 128
CONV = 3
ROWS = 160
VMEM_LIMIT = 14 * 1024 * 1024
PLANE = 4

F32 = jnp.float32
BF16 = jnp.bfloat16
TN = (((0,), (0,)), ((), ()))
NT = (((1,), (1,)), ((), ()))
NN = (((1,), (0,)), ((), ()))


def mm(a, b, dims):
    return lax.dot_general(a, b, dims, preferred_element_type=F32)


def call(body, operands, out_shape, flops, far=(), scratch=()):
    moved = sum(x.size * x.dtype.itemsize for x in operands)
    moved += sum(x.size * x.dtype.itemsize for x in out_shape)
    vmem = pl.BlockSpec(memory_space=pltpu.VMEM)
    hbm = pl.BlockSpec(memory_space=pltpu.HBM)
    return pl.pallas_call(
        body,
        out_shape=out_shape,
        in_specs=[hbm if i in far else vmem for i in range(len(operands))],
        out_specs=[vmem for _ in out_shape],
        scratch_shapes=list(scratch),
        compiler_params=pltpu.CompilerParams(vmem_limit_bytes=VMEM_LIMIT),
        cost_estimate=pl.CostEstimate(flops=flops, bytes_accessed=moved, transcendentals=0),
    )(*[in_hbm(x) if i in far else x for i, x in enumerate(operands)])


def in_hbm(x):
    return pltpu.with_memory_space_constraint(x, pltpu.HBM)


def fetch(source, target, sem):
    copy = pltpu.make_async_copy(source, target, sem)
    copy.start()
    return copy


def store_features(out_ref, rows_in, doubled):
    heads = rows_in.shape[0] // FEAT
    tokens = rows_in.shape[1]
    grid = rows_in.reshape(heads, FEAT, tokens) * FEAT ** (-0.25)
    twice = jnp.concatenate([grid, grid], 1)
    out_ref[:, 0:FEAT, :] = grid.astype(BF16)
    half = FEAT // 2
    for turn in range(half):
        square = grid * twice[:, turn : turn + FEAT, :] * 0.5**0.5
        if doubled and turn > 0:
            square = square * 2.0
        out_ref[:, FEAT * (turn + 1) : FEAT * (turn + 2), :] = square.astype(BF16)
    square = grid[:, :half, :] * grid[:, half:, :] * 0.5**0.5
    if doubled:
        square = square * 2.0
    first = lax.broadcasted_iota(jnp.int32, (heads, half, tokens), 1) == 0
    constant = jnp.where(first, 1.0, 0.0)
    out_ref[:, FEAT * (half + 1) :, :] = jnp.concatenate([square, constant], 1).astype(BF16)


def store_piece(rank, head, per_piece, state, own_ref, send_ref):
    slot = rank ^ (head // per_piece)
    at = (head % per_piece) * ROWS
    own_ref[slot, at : at + ROWS, :] = state
    send_ref[slot, at : at + ROWS, :] = state.astype(BF16)


def load_piece(rank, head, per_piece, ref):
    at = (head % per_piece) * ROWS
    return ref[rank ^ (head // per_piece), at : at + ROWS, :]


def edge_kernel(k_far, v_far, edge_ref, k_ref, v_ref, sems):
    tokens, width = k_far.shape
    deep = k_ref.shape[0]
    rows = pl.ds(tokens - deep, deep)
    copies = [fetch(k_far.at[rows], k_ref, sems.at[0]), fetch(v_far.at[rows], v_ref, sems.at[1])]
    last = deep - CONV + 1
    copies[0].wait()
    edge_ref[:, :width] = k_ref[...].astype(F32)[last:].astype(BF16)
    copies[1].wait()
    edge_ref[:, width:] = v_ref[...].astype(F32)[last:].astype(BF16)


def load_kernel(k_far, v_far, ck_far, cv_far, k_ref, v_ref, ck_ref, cv_ref, sems):
    pairs = ((k_far, k_ref), (v_far, v_ref), (ck_far, ck_ref), (cv_far, cv_ref))
    copies = [fetch(a, b, sems.at[i]) for i, (a, b) in enumerate(pairs)]
    for copy in copies:
        copy.wait()


def query_kernel(
    q_far,
    k_far,
    v_far,
    ck_far,
    cv_far,
    qd_ref,
    k_ref,
    v_ref,
    ck_ref,
    cv_ref,
    q_ref,
    sems,
):
    far = (q_far, k_far, v_far, ck_far, cv_far)
    near = (q_ref, k_ref, v_ref, ck_ref, cv_ref)
    copies = [fetch(a, b, sems.at[i]) for i, (a, b) in enumerate(zip(far, near))]
    copies[0].wait()
    store_features(qd_ref, q_ref[...].astype(F32).T, True)
    for copy in copies[1:]:
        copy.wait()


def columns_of(w_ref, distance):
    columns = w_ref.shape[1] // lax.axis_size("head")
    return pl.ds(pl.multiple_of((lax.axis_index("head") ^ distance) * columns, columns), columns)


def turn_kernel(qd_ref, kf_ref, qt_ref, kt_ref):
    for head in range(qd_ref.shape[0]):
        qt_ref[head] = qd_ref[head].T
        kt_ref[head] = kf_ref[head].T


def grad_kernel(*refs):
    *cots, w_ref, og_ref = refs
    total = None
    for j, cot_ref in enumerate(cots):
        term = mm(cot_ref[...], w_ref[:, columns_of(w_ref, j)], NT)
        total = term if total is None else total + term
    og_ref[...] = total


def conv_rows(x, before, taps):
    x = x.astype(F32)
    row = lax.broadcasted_iota(jnp.int32, x.shape, 0)
    running = taps[0:1, :] * x
    for offset in range(1, CONV):
        moved = pltpu.roll(x, offset, 0)
        for at in range(offset):
            source = before[CONV - 1 - offset + at : CONV - offset + at, :]
            moved = jnp.where(row == at, source, moved)
        running = running + taps[offset : offset + 1, :] * moved
    return running


def norm_rows(norm):
    high = norm.astype(BF16).astype(F32)
    middle = (norm - high).astype(BF16).astype(F32)
    rest = norm - high - middle
    parts = (high, middle, rest)
    tail = [x[:, VDIM:] for x in parts]
    filler = jnp.zeros((norm.shape[0], VDIM - 3 * (ROWS - VDIM)), F32)
    tail = jnp.concatenate(tail + [filler], 1)
    return jnp.concatenate([x[:, :VDIM] for x in parts] + [tail], 0)


def norm_values(rows):
    heads = rows.shape[0] // 4
    extra = ROWS - VDIM
    tail = rows[3 * heads :]
    tail = tail[:, :extra] + tail[:, extra : 2 * extra] + tail[:, 2 * extra : 3 * extra]
    main = rows[:heads] + rows[heads : 2 * heads] + rows[2 * heads : 3 * heads]
    return jnp.concatenate([main, tail], 1)


def key_kernel(
    k_ref,
    v_ref,
    before_ref,
    ck_ref,
    cv_ref,
    kf_ref,
    vc_ref,
    own_ref,
    send_ref,
    slots,
):
    rank = lax.rem(lax.axis_index("ctx"), PLANE)
    heads = kf_ref.shape[0]
    per_piece = heads // PLANE
    width = k_ref.shape[1]
    before = before_ref[...].astype(F32)
    key_conv = conv_rows(k_ref[...], before[:, :width], ck_ref[...])
    store_features(kf_ref, key_conv.T, False)
    ones = jnp.ones((heads, k_ref.shape[0]), BF16)
    row = lax.broadcasted_iota(jnp.int32, (heads, ROWS), 0)
    norm = jnp.zeros((heads, ROWS), F32)
    for head in range(heads):
        at = head * VDIM
        value = conv_rows(
            v_ref[:, at : at + VDIM],
            before[:, width + at : width + at + VDIM],
            cv_ref[:, at : at + VDIM],
        ).astype(BF16)
        vc_ref[:, at : at + VDIM] = value
        feat = kf_ref[head]
        norm = jnp.where(row == head, mm(ones, feat, NT), norm)
        store_piece(rank, head, per_piece, mm(feat, value, NN), slots, send_ref)
    lines = norm_rows(norm)
    at = per_piece * ROWS
    own_ref[:at, :] = slots[0]
    own_ref[at:, :] = lines
    for slot in range(PLANE):
        send_ref[slot, at:, :] = lines.astype(BF16)


def share_kernel(norm_at, own_ref, *refs):
    sent_at = -1 if refs[-1].dtype == BF16 else -2
    got_refs, sent_ref = refs[:sent_at], refs[sent_at]
    total = own_ref[...]
    for got_ref in got_refs:
        total = total + got_ref[...].astype(F32)
    if norm_at is not None:
        lines = norm_rows(norm_values(total[norm_at:]))
        total = jnp.concatenate([total[:norm_at], lines], 0)
    sent_ref[...] = total.astype(BF16)
    if sent_at == -2:
        refs[-1][...] = total


def store_pieces(sign, strides, got_refs, moved_refs, pieces_ref):
    rows = pieces_ref.shape[1]

    def masked(ahead, ref):
        return jnp.where(ahead, ref[...].astype(F32), 0.0)

    def is_ahead(other, here):
        return other < here if sign > 0 else other > here

    before = jnp.zeros(got_refs[0].shape, F32)
    for ref, (stride, distance) in zip(moved_refs, strides):
        if distance:
            group = lax.div(lax.axis_index("ctx"), PLANE * stride)
            before = before + masked(is_ahead(group ^ distance, group), ref)
        else:
            before = before + ref[...].astype(F32)
    rank = lax.rem(lax.axis_index("ctx"), PLANE)
    extra = None
    for slot in range(PLANE):
        total = before
        for i in range(PLANE):
            if i != slot:
                total = total + masked(is_ahead(rank ^ i, rank ^ slot), got_refs[i])
        pieces_ref[slot] = total[:rows].astype(BF16)
        extra = total[rows:] if slot == 0 else extra
    return extra


def piece_kernel(sign, strides, *refs):
    store_pieces(sign, strides, refs[:PLANE], refs[PLANE:-1], refs[-1])


def score_kernel(qd_ref, kf_ref, vc_ref, low_ref, den_ref, num_ref):
    heads = kf_ref.shape[0]
    tokens = kf_ref.shape[2]
    key_at = lax.broadcasted_iota(jnp.int32, (tokens, tokens), 0)
    query_at = lax.broadcasted_iota(jnp.int32, (tokens, tokens), 1)
    causal = key_at <= query_at
    for head in range(heads):
        scores = jnp.where(causal, mm(kf_ref[head], qd_ref[head], TN), 0.0)
        den_ref[head : head + 1, :] = jnp.sum(scores, 0, keepdims=True)
        low = scores.astype(BF16)
        low_ref[head] = low
        at = head * VDIM
        num_ref[:, at : at + VDIM] = mm(low, vc_ref[:, at : at + VDIM], TN)


def scale_kernel(strides, den_ref, qd_ref, og_ref, *refs):
    *refs, pieces_ref, inv_ref, sg_ref, own_ref, send_ref, slots = refs
    rank = lax.rem(lax.axis_index("ctx"), PLANE)
    heads = qd_ref.shape[0]
    per_piece = heads // PLANE
    lines = store_pieces(1, strides, refs[:PLANE], refs[PLANE:], pieces_ref)
    norm = norm_values(lines)
    high = norm.astype(BF16).astype(F32)
    middle = (norm - high).astype(BF16).astype(F32)
    rest = norm - high - middle
    parts = jnp.concatenate([high, middle, rest, jnp.zeros_like(rest)], 0).astype(BF16)
    lines = []
    for head in range(heads):
        terms = mm(parts, qd_ref[head], NN)
        line = den_ref[head : head + 1, :] + terms[head : head + 1, :]
        line = line + terms[heads + head : heads + head + 1, :]
        lines.append(line + terms[2 * heads + head : 2 * heads + head + 1, :])
    inverse = (1.0 / jnp.concatenate(lines, 0)).T
    inv_ref[...] = inverse
    for head in range(heads):
        at = head * VDIM
        scaled = (og_ref[:, at : at + VDIM] * inverse[:, head : head + 1]).astype(BF16)
        sg_ref[:, at : at + VDIM] = scaled
        store_piece(rank, head, per_piece, mm(qd_ref[head], scaled, NN), slots, send_ref)
    own_ref[...] = slots[0]


def near_kernel(low_ref, sg_ref, vg_ref):
    for head in range(low_ref.shape[0]):
        at = head * VDIM
        vg_ref[:, at : at + VDIM] = mm(low_ref[head], sg_ref[:, at : at + VDIM], NN)


def attend_kernel(qt_ref, prior_ref, num_ref, inv_ref, w_ref, att_ref, part_ref):
    rank = lax.rem(lax.axis_index("ctx"), PLANE)
    heads = qt_ref.shape[0]
    per_piece = heads // PLANE
    for head in range(heads):
        at = head * VDIM
        prior = load_piece(rank, head, per_piece, prior_ref)
        total = num_ref[:, at : at + VDIM] + mm(qt_ref[head], prior, NN)
        att_ref[:, at : at + VDIM] = (total * inv_ref[:, head : head + 1]).astype(BF16)
    part_ref[...] = mm(att_ref[...], w_ref[:, columns_of(w_ref, 1)], NN).astype(BF16)


def mix_kernel(distance, att_ref, w_ref, part_ref):
    weight = w_ref[:, columns_of(w_ref, distance)]
    part_ref[...] = mm(att_ref[...], weight, NN).astype(part_ref.dtype)


def last_kernel(kt_ref, later_ref, near_ref, part_ref, *refs):
    *other_refs, vg_far, mixed_far, vg_ref, mixed_ref, sems = refs
    rank = lax.rem(lax.axis_index("ctx"), PLANE)
    heads = kt_ref.shape[0]
    per_piece = heads // PLANE
    copies = []
    for head in range(heads):
        at = head * VDIM
        later = load_piece(rank, head, per_piece, later_ref)
        total = near_ref[:, at : at + VDIM] + mm(kt_ref[head], later, NN)
        vg_ref[:, at : at + VDIM] = total.astype(BF16)
        if head % per_piece == per_piece - 1:
            columns = pl.ds((head + 1 - per_piece) * VDIM, per_piece * VDIM)
            sem = sems.at[head // per_piece]
            copies.append(fetch(vg_ref.at[:, columns], vg_far.at[:, columns], sem))
    deep = part_ref.shape[0] // PLANE
    for step in range(PLANE):
        total = part_ref[step * deep : (step + 1) * deep, :]
        for other_ref in other_refs:
            total = total + other_ref[step * deep : (step + 1) * deep, :].astype(F32)
        mixed_ref[step * deep : (step + 1) * deep, :] = total.astype(BF16)
        rows = pl.ds(step * deep, deep)
        sem = sems.at[PLANE + step]
        copies.append(fetch(mixed_ref.at[rows], mixed_far.at[rows], sem))
    for copy in copies:
        copy.wait()


def shifted(x, axis, by):
    peers = lax.axis_size(axis)
    pairs = [(i, i + by) for i in range(peers) if 0 <= i + by < peers]
    return lax.ppermute(x, axis, pairs)


def after(x, *others):
    return lax.optimization_barrier((x, *others))[0]


def planes_ahead(total, sent, sign, join):
    planes = lax.axis_size("ctx") // PLANE
    received, strides = [], []
    stride = 1
    while stride < planes:
        if (planes // stride) % 4 == 0:
            moved = [swapped(sent, "ctx", j, stride * PLANE) for j in range(1, 4)]
            strides += [(stride, j) for j in range(1, 4)]
            stride = stride * 4
        else:
            moved = [shifted(sent, "ctx", sign * stride * PLANE)]
            strides.append((stride, 0))
            stride = stride * 2
        received += moved
        if stride < planes:
            sent, total = join(total, moved, stride * 2 < planes)
    return received, strides


def swapped(x, axis, distance, stride=1):
    peers = lax.axis_size(axis)
    pairs = [(i, (i // stride ^ distance) * stride + i % stride) for i in range(peers)]
    return lax.ppermute(x, axis, pairs)


def handed_back(pieces):
    back = [swapped(pieces[j], "ctx", j) for j in range(1, PLANE)]
    return jnp.stack([pieces[0]] + back, 0)


def per_device(queries, keys, values, conv_keys, conv_values, out_weight, cotangent):
    tokens = queries.shape[0]
    heads = queries.shape[1] // FEAT
    width = heads * VDIM
    columns = cotangent.shape[1]
    groups = lax.axis_size("head")
    piece_rows = heads // PLANE * ROWS
    message = (piece_rows + 4 * heads, VDIM)
    S = jax.ShapeDtypeStruct
    step = 2 * tokens * ROWS * VDIM * heads
    project_flops = 2 * tokens * width * columns
    dma = pltpu.SemaphoreType.DMA
    vmem = pltpu.VMEM
    slots = vmem((PLANE, piece_rows, VDIM), F32)

    with jax.named_scope("edge"):
        last_rows = pl.pallas_call(
            edge_kernel,
            out_shape=S((CONV - 1, keys.shape[1] + width), BF16),
            in_specs=[pl.BlockSpec(memory_space=pltpu.HBM)] * 2,
            out_specs=pl.BlockSpec(memory_space=vmem),
            scratch_shapes=[vmem((16, keys.shape[1]), BF16), vmem((16, width), BF16), dma((2,))],
            compiler_params=pltpu.CompilerParams(vmem_limit_bytes=VMEM_LIMIT),
        )(in_hbm(keys), in_hbm(values))
        before = shifted(last_rows, "ctx", 1)
    with jax.named_scope("query_features"):
        arrays = (keys, values, conv_keys, conv_values)
        qd, *near_by = call(
            query_kernel,
            (after(queries, last_rows), *arrays),
            [S((heads, ROWS, tokens), BF16)] + [S(x.shape, x.dtype) for x in arrays],
            1 << 20,
            far=range(5),
            scratch=[vmem(queries.shape, BF16), dma((5,))],
        )
    with jax.named_scope("key_features"):
        outs = [
            S((heads, ROWS, tokens), BF16),
            S((tokens, width), BF16),
            S(message, F32),
            S((PLANE, *message), BF16),
        ]
        ops = (*near_by[:2], before, *near_by[2:])
        kf, vc, own, send = call(key_kernel, ops, outs, step, scratch=[slots])
    with jax.named_scope("cotangent"):
        cots = [swapped(after(cotangent, send), "head", j) for j in range(1, groups)]
    with jax.named_scope("prior_share"):
        got = [swapped(send[j], "ctx", j) for j in range(1, PLANE)]

        def join(norm_at, total, received, more):
            outs = [S(total.shape, BF16), S(total.shape, F32)]
            body = functools.partial(share_kernel, norm_at)
            made = call(body, (total, *received), outs[: 2 if more else 1], 1 << 20)
            return made if more else (made[0], None)

        more = lax.axis_size("ctx") > 4 * PLANE
        sent, total = join(piece_rows, own, got, more)
    with jax.named_scope("scores"):
        outs = [
            S((heads, tokens, tokens), BF16),
            S((heads, tokens), F32),
            S((tokens, width), F32),
        ]
        low, den, num = call(score_kernel, (qd, kf, vc), outs, 400 * step)
    with jax.named_scope("prior_planes"):
        sent = after(sent, den)
        norm_join = functools.partial(join, piece_rows)
        moved, strides = planes_ahead(total, sent, 1, norm_join)
    with jax.named_scope("turned"):
        outs = [S((heads, tokens, ROWS), BF16)] * 2
        qt, kt = call(turn_kernel, (after(qd, sent), kf), outs, 1 << 22)
    with jax.named_scope("out_grad"):
        ops = (after(cotangent, qt), *cots, out_weight)
        (out_grad,) = call(
            grad_kernel, ops, [S((tokens, width), F32)], groups * project_flops
        )
    with jax.named_scope("scaled_grad"):
        outs = [
            S((PLANE, piece_rows, VDIM), BF16),
            S((tokens, heads), F32),
            S((tokens, width), BF16),
            S((piece_rows, VDIM), F32),
            S((PLANE, piece_rows, VDIM), BF16),
        ]
        ops = (den, qd, out_grad, own, *got, *moved)
        body = functools.partial(scale_kernel, strides)
        pieces, inverse, scaled, own_later, send_later = call(
            body, ops, outs, step, scratch=[slots]
        )
        prior = handed_back(pieces)
    with jax.named_scope("later_share"):
        got_later = [swapped(send_later[j], "ctx", j) for j in range(1, PLANE)]
    with jax.named_scope("later_planes"):
        plain_join = functools.partial(join, None)
        sent_later, total_later = plain_join(own_later, got_later, more)
        moved_later, strides = planes_ahead(total_later, sent_later, -1, plain_join)
    with jax.named_scope("attended"):
        outs = [S((tokens, width), BF16), S((tokens, columns), BF16)]
        ops = (qt, prior, after(num, sent_later), inverse, out_weight)
        attended, part = call(attend_kernel, ops, outs, step + project_flops)
        parts = [swapped(part, "head", 1)]
    with jax.named_scope("near"):
        ops = (low, after(scaled, sent_later))
        (near,) = call(near_kernel, ops, [S((tokens, width), F32)], 2 * step)
    with jax.named_scope("mixed"):
        for j in list(range(2, groups)) + [0]:
            outs = [S((tokens, columns), BF16 if j else F32)]
            body = functools.partial(mix_kernel, j)
            ops = (after(attended, sent_later), out_weight)
            (part,) = call(body, ops, outs, 2 * project_flops)
            if j:
                parts.append(swapped(part, "head", j))
    with jax.named_scope("later_back"):
        outs = [S((PLANE, piece_rows, VDIM), BF16)]
        body = functools.partial(piece_kernel, -1, strides)
        ops = (own_later, *got_later, after(moved_later[0], part, near), *moved_later[1:])
        (pieces,) = call(body, ops, outs, 1 << 20)
        later = handed_back(pieces)
    with jax.named_scope("last"):
        whole = (tokens, columns)
        value_grad, mixed_out = pl.pallas_call(
            last_kernel,
            out_shape=[S((tokens, width), BF16), S(whole, BF16)],
            in_specs=[pl.BlockSpec(memory_space=vmem)] * (4 + len(parts)),
            out_specs=[pl.BlockSpec(memory_space=pltpu.HBM)] * 2,
            scratch_shapes=[
                vmem((tokens, width), BF16),
                vmem(whole, BF16),
                dma((2 * PLANE,)),
            ],
            compiler_params=pltpu.CompilerParams(vmem_limit_bytes=VMEM_LIMIT),
        )(kt, later, near, part, *parts)
    return mixed_out, value_grad


def solution(mesh):
    in_specs = (
        P("ctx", "head"),
        P("ctx", "head"),
        P("ctx", "head"),
        P(None, "head"),
        P(None, "head"),
        P("head", None),
        P("ctx", "head"),
    )
    out_specs = (P("ctx", "head"), P("ctx", "head"))
    return jax.shard_map(
        per_device, mesh=mesh, in_specs=in_specs, out_specs=out_specs, check_vma=False
    )
```

```python
import functools

import jax
import jax.numpy as jnp
from jax import lax
from jax.experimental import pallas as pl
from jax.experimental.pallas import tpu as pltpu
from jax.sharding import PartitionSpec as P

FEAT = 16
VDIM = 128
CONV = 3
ROWS = 160
VMEM_LIMIT = 14 * 1024 * 1024
PLANE = 4

F32 = jnp.float32
BF16 = jnp.bfloat16
TN = (((0,), (0,)), ((), ()))
NT = (((1,), (1,)), ((), ()))
NN = (((1,), (0,)), ((), ()))


def mm(a, b, dims):
    return lax.dot_general(a, b, dims, preferred_element_type=F32)


def call(body, operands, out_shape, flops, far=(), scratch=(), out_far=False):
    moved = sum(x.size * x.dtype.itemsize for x in operands)
    moved += sum(x.size * x.dtype.itemsize for x in out_shape)
    vmem = pl.BlockSpec(memory_space=pltpu.VMEM)
    hbm = pl.BlockSpec(memory_space=pltpu.HBM)
    return pl.pallas_call(
        body,
        out_shape=out_shape,
        in_specs=[hbm if i in far else vmem for i in range(len(operands))],
        out_specs=[hbm if out_far else vmem for _ in out_shape],
        scratch_shapes=list(scratch),
        compiler_params=pltpu.CompilerParams(vmem_limit_bytes=VMEM_LIMIT),
        cost_estimate=pl.CostEstimate(flops=flops, bytes_accessed=moved, transcendentals=0),
    )(*[in_hbm(x) if i in far else x for i, x in enumerate(operands)])


def in_hbm(x):
    return pltpu.with_memory_space_constraint(x, pltpu.HBM)


def fetch(source, target, sem):
    copy = pltpu.make_async_copy(source, target, sem)
    copy.start()
    return copy


def store_features(out_ref, rows_in, doubled):
    heads = rows_in.shape[0] // FEAT
    tokens = rows_in.shape[1]
    grid = rows_in.reshape(heads, FEAT, tokens) * FEAT ** (-0.25)
    twice = jnp.concatenate([grid, grid], 1)
    out_ref[:, 0:FEAT, :] = grid.astype(BF16)
    half = FEAT // 2
    for turn in range(half):
        square = grid * twice[:, turn : turn + FEAT, :] * 0.5**0.5
        if doubled and turn > 0:
            square = square * 2.0
        out_ref[:, FEAT * (turn + 1) : FEAT * (turn + 2), :] = square.astype(BF16)
    square = grid[:, :half, :] * grid[:, half:, :] * 0.5**0.5
    if doubled:
        square = square * 2.0
    first = lax.broadcasted_iota(jnp.int32, (heads, half, tokens), 1) == 0
    constant = jnp.where(first, 1.0, 0.0)
    out_ref[:, FEAT * (half + 1) :, :] = jnp.concatenate([square, constant], 1).astype(BF16)


def store_piece(rank, head, per_piece, state, own_ref, send_ref):
    slot = rank ^ (head // per_piece)
    at = (head % per_piece) * ROWS
    own_ref[slot, at : at + ROWS, :] = state
    send_ref[slot, at : at + ROWS, :] = state.astype(BF16)


def load_piece(rank, head, per_piece, ref):
    at = (head % per_piece) * ROWS
    return ref[rank ^ (head // per_piece), at : at + ROWS, :]


def edge_kernel(k_far, v_far, edge_ref, k_ref, v_ref, sems):
    tokens, width = k_far.shape
    deep = k_ref.shape[0]
    rows = pl.ds(tokens - deep, deep)
    copies = [fetch(k_far.at[rows], k_ref, sems.at[0]), fetch(v_far.at[rows], v_ref, sems.at[1])]
    last = deep - CONV + 1
    copies[0].wait()
    edge_ref[:, :width] = k_ref[...].astype(F32)[last:].astype(BF16)
    copies[1].wait()
    edge_ref[:, width:] = v_ref[...].astype(F32)[last:].astype(BF16)


def load_kernel(k_far, v_far, ck_far, cv_far, k_ref, v_ref, ck_ref, cv_ref, sems):
    pairs = ((k_far, k_ref), (v_far, v_ref), (ck_far, ck_ref), (cv_far, cv_ref))
    copies = [fetch(a, b, sems.at[i]) for i, (a, b) in enumerate(pairs)]
    for copy in copies:
        copy.wait()


def query_kernel(
    q_far,
    k_far,
    v_far,
    ck_far,
    cv_far,
    qd_ref,
    k_ref,
    v_ref,
    ck_ref,
    cv_ref,
    q_ref,
    sems,
):
    far = (q_far, k_far, v_far, ck_far, cv_far)
    near = (q_ref, k_ref, v_ref, ck_ref, cv_ref)
    copies = [fetch(a, b, sems.at[i]) for i, (a, b) in enumerate(zip(far, near))]
    copies[0].wait()
    store_features(qd_ref, q_ref[...].astype(F32).T, True)
    for copy in copies[1:]:
        copy.wait()


def columns_of(w_ref, distance):
    columns = w_ref.shape[1] // lax.axis_size("head")
    return pl.ds(pl.multiple_of((lax.axis_index("head") ^ distance) * columns, columns), columns)


def turn_kernel(qd_ref, kf_ref, qt_ref, kt_ref):
    for head in range(qd_ref.shape[0]):
        qt_ref[head] = qd_ref[head].T
        kt_ref[head] = kf_ref[head].T


def grad_kernel(*refs):
    *cots, w_ref, og_ref = refs
    total = None
    for j, cot_ref in enumerate(cots):
        term = mm(cot_ref[...], w_ref[:, columns_of(w_ref, j)], NT)
        total = term if total is None else total + term
    og_ref[...] = total


def masked(wanted, value):
    return jnp.where(wanted, value.astype(F32), 0.0)


def conv_rows(x, before, taps):
    x = x.astype(F32)
    row = lax.broadcasted_iota(jnp.int32, x.shape, 0)
    running = taps[0:1, :] * x
    for offset in range(1, CONV):
        moved = pltpu.roll(x, offset, 0)
        for at in range(offset):
            source = before[CONV - 1 - offset + at : CONV - offset + at, :]
            moved = jnp.where(row == at, source, moved)
        running = running + taps[offset : offset + 1, :] * moved
    return running


def norm_rows(norm):
    high = norm.astype(BF16).astype(F32)
    middle = (norm - high).astype(BF16).astype(F32)
    rest = norm - high - middle
    parts = (high, middle, rest)
    tail = [x[:, VDIM:] for x in parts]
    filler = jnp.zeros((norm.shape[0], VDIM - 3 * (ROWS - VDIM)), F32)
    tail = jnp.concatenate(tail + [filler], 1)
    return jnp.concatenate([x[:, :VDIM] for x in parts] + [tail], 0)


def norm_values(rows):
    heads = rows.shape[0] // 4
    extra = ROWS - VDIM
    tail = rows[3 * heads :]
    tail = tail[:, :extra] + tail[:, extra : 2 * extra] + tail[:, 2 * extra : 3 * extra]
    main = rows[:heads] + rows[heads : 2 * heads] + rows[2 * heads : 3 * heads]
    return jnp.concatenate([main, tail], 1)


def key_kernel(
    k_ref,
    v_ref,
    before_ref,
    ck_ref,
    cv_ref,
    kf_ref,
    vc_ref,
    own_ref,
    send_ref,
    slots,
):
    rank = lax.rem(lax.axis_index("ctx"), PLANE)
    heads = kf_ref.shape[0]
    per_piece = heads // PLANE
    width = k_ref.shape[1]
    before = masked(lax.axis_index("ctx") > 0, before_ref[...])
    key_conv = conv_rows(k_ref[...], before[:, :width], ck_ref[...])
    store_features(kf_ref, key_conv.T, False)
    ones = jnp.ones((heads, k_ref.shape[0]), BF16)
    row = lax.broadcasted_iota(jnp.int32, (heads, ROWS), 0)
    norm = jnp.zeros((heads, ROWS), F32)
    for head in range(heads):
        at = head * VDIM
        value = conv_rows(
            v_ref[:, at : at + VDIM],
            before[:, width + at : width + at + VDIM],
            cv_ref[:, at : at + VDIM],
        ).astype(BF16)
        vc_ref[:, at : at + VDIM] = value
        feat = kf_ref[head]
        norm = jnp.where(row == head, mm(ones, feat, NT), norm)
        store_piece(rank, head, per_piece, mm(feat, value, NN), slots, send_ref)
    lines = norm_rows(norm)
    at = per_piece * ROWS
    own_ref[:at, :] = slots[0]
    own_ref[at:, :] = lines
    for slot in range(PLANE):
        send_ref[slot, at:, :] = lines.astype(BF16)


def share_kernel(norm_at, own_ref, *refs):
    sent_at = -1 if refs[-1].dtype == BF16 else -2
    got_refs, sent_ref = refs[:sent_at], refs[sent_at]
    total = own_ref[...]
    for got_ref in got_refs:
        total = total + got_ref[...].astype(F32)
    if norm_at is not None:
        lines = norm_rows(norm_values(total[norm_at:]))
        total = jnp.concatenate([total[:norm_at], lines], 0)
    sent_ref[...] = total.astype(BF16)
    if sent_at == -2:
        refs[-1][...] = total


def store_pieces(sign, strides, got_refs, moved_refs, pieces_ref):
    rows = pieces_ref.shape[1]

    def is_ahead(other, here):
        return other < here if sign > 0 else other > here

    before = jnp.zeros(got_refs[0].shape, F32)
    for ref, (stride, distance) in zip(moved_refs, strides):
        if distance:
            group = lax.div(lax.axis_index("ctx"), PLANE * stride)
            before = before + masked(is_ahead(group ^ distance, group), ref[...])
        else:
            before = before + ref[...].astype(F32)
    rank = lax.rem(lax.axis_index("ctx"), PLANE)
    extra = None
    for slot in range(PLANE):
        total = before
        for i in range(PLANE):
            if i != slot:
                total = total + masked(is_ahead(rank ^ i, rank ^ slot), got_refs[i][...])
        pieces_ref[slot] = total[:rows].astype(BF16)
        extra = total[rows:] if slot == 0 else extra
    return extra


def piece_kernel(sign, strides, *refs):
    store_pieces(sign, strides, refs[:PLANE], refs[PLANE:-1], refs[-1])


def score_kernel(qd_ref, kf_ref, vc_ref, low_ref, den_ref, num_ref):
    heads = kf_ref.shape[0]
    tokens = kf_ref.shape[2]
    key_at = lax.broadcasted_iota(jnp.int32, (tokens, tokens), 0)
    query_at = lax.broadcasted_iota(jnp.int32, (tokens, tokens), 1)
    causal = key_at <= query_at
    for head in range(heads):
        scores = jnp.where(causal, mm(kf_ref[head], qd_ref[head], TN), 0.0)
        den_ref[head : head + 1, :] = jnp.sum(scores, 0, keepdims=True)
        low = scores.astype(BF16)
        low_ref[head] = low
        at = head * VDIM
        num_ref[:, at : at + VDIM] = mm(low, vc_ref[:, at : at + VDIM], TN)


def scale_kernel(strides, den_ref, qd_ref, og_ref, *refs):
    *refs, pieces_ref, inv_ref, sg_ref, own_ref, send_ref, slots = refs
    rank = lax.rem(lax.axis_index("ctx"), PLANE)
    heads = qd_ref.shape[0]
    per_piece = heads // PLANE
    lines = store_pieces(1, strides, refs[:PLANE], refs[PLANE:], pieces_ref)
    norm = norm_values(lines)
    high = norm.astype(BF16).astype(F32)
    middle = (norm - high).astype(BF16).astype(F32)
    rest = norm - high - middle
    parts = jnp.concatenate([high, middle, rest, jnp.zeros_like(rest)], 0).astype(BF16)
    lines = []
    for head in range(heads):
        terms = mm(parts, qd_ref[head], NN)
        line = den_ref[head : head + 1, :] + terms[head : head + 1, :]
        line = line + terms[heads + head : heads + head + 1, :]
        lines.append(line + terms[2 * heads + head : 2 * heads + head + 1, :])
    inverse = (1.0 / jnp.concatenate(lines, 0)).T
    inv_ref[...] = inverse
    for head in range(heads):
        at = head * VDIM
        scaled = (og_ref[:, at : at + VDIM] * inverse[:, head : head + 1]).astype(BF16)
        sg_ref[:, at : at + VDIM] = scaled
        store_piece(rank, head, per_piece, mm(qd_ref[head], scaled, NN), slots, send_ref)
    own_ref[...] = slots[0]


def near_kernel(low_ref, sg_ref, vg_ref):
    for head in range(low_ref.shape[0]):
        at = head * VDIM
        vg_ref[:, at : at + VDIM] = mm(low_ref[head], sg_ref[:, at : at + VDIM], NN)


def attend_kernel(qt_ref, prior_ref, num_ref, inv_ref, w_ref, att_ref, part_ref):
    rank = lax.rem(lax.axis_index("ctx"), PLANE)
    heads = qt_ref.shape[0]
    per_piece = heads // PLANE
    for head in range(heads):
        at = head * VDIM
        prior = load_piece(rank, head, per_piece, prior_ref)
        total = num_ref[:, at : at + VDIM] + mm(qt_ref[head], prior, NN)
        att_ref[:, at : at + VDIM] = (total * inv_ref[:, head : head + 1]).astype(BF16)
    part_ref[...] = mm(att_ref[...], w_ref[:, columns_of(w_ref, 1)], NN).astype(BF16)


def mix_kernel(distance, att_ref, w_ref, part_ref):
    weight = w_ref[:, columns_of(w_ref, distance)]
    part_ref[...] = mm(att_ref[...], weight, NN).astype(part_ref.dtype)


def far_block(distance, kt_ref, near_ref, later_ref):
    per_piece = kt_ref.shape[0] // PLANE
    first = (lax.rem(lax.axis_index("ctx"), PLANE) ^ distance) * per_piece
    blocks = []
    for i in range(per_piece):
        columns = pl.ds(pl.multiple_of((first + i) * VDIM, VDIM), VDIM)
        later = later_ref[i * ROWS : (i + 1) * ROWS, :]
        total = near_ref[:, columns] + mm(kt_ref[first + i], later, NN)
        blocks.append(total.astype(BF16))
    return jnp.concatenate(blocks, 1)


def early_kernel(kt_ref, near_ref, *refs):
    *later_refs, block_ref = refs
    for distance, later_ref in enumerate(later_refs):
        block_ref[distance] = far_block(distance, kt_ref, near_ref, later_ref)


def late_kernel(kt_ref, near_ref, early_ref, *refs):
    *later_refs, vg_far, block_ref, sems = refs
    early, columns = early_ref.shape[0], early_ref.shape[2]
    rank = lax.rem(lax.axis_index("ctx"), PLANE)

    def send(distance, ref):
        start = pl.multiple_of((rank ^ distance) * columns, columns)
        return fetch(ref, vg_far.at[:, pl.ds(start, columns)], sems.at[distance])

    copies = [send(distance, early_ref.at[distance]) for distance in range(early)]
    for i, later_ref in enumerate(later_refs):
        block_ref[i] = far_block(early + i, kt_ref, near_ref, later_ref)
        copies.append(send(early + i, block_ref.at[i]))
    for copy in copies:
        copy.wait()


def sum_kernel(part_ref, *refs):
    *other_refs, mixed_far, mixed_ref, sems = refs
    copies = []
    deep = part_ref.shape[0] // PLANE
    for step in range(PLANE):
        rows = pl.ds(step * deep, deep)
        total = part_ref[rows, :]
        for other_ref in other_refs:
            total = total + other_ref[rows, :].astype(F32)
        mixed_ref[rows, :] = total.astype(BF16)
        copies.append(fetch(mixed_ref.at[rows], mixed_far.at[rows], sems.at[step]))
    for copy in copies:
        copy.wait()


def shifted(x, axis, by):
    peers = lax.axis_size(axis)
    pairs = [(i, i + by) for i in range(peers) if 0 <= i + by < peers]
    return lax.ppermute(x, axis, pairs)


def after(x, *others):
    return lax.optimization_barrier((x, *others))[0]


def planes_ahead(total, sent, sign, join):
    planes = lax.axis_size("ctx") // PLANE
    received, strides = [], []
    stride = 1
    while stride < planes:
        if (planes // stride) % 4 == 0:
            moved = [swapped(sent, "ctx", j, stride * PLANE) for j in range(1, 4)]
            strides += [(stride, j) for j in range(1, 4)]
            stride = stride * 4
        else:
            moved = [shifted(sent, "ctx", sign * stride * PLANE)]
            strides.append((stride, 0))
            stride = stride * 2
        received += moved
        if stride < planes:
            sent, total = join(total, moved, stride * 2 < planes)
    return received, strides


def swapped(x, axis, distance, stride=1):
    peers = lax.axis_size(axis)
    pairs = [(i, (i // stride ^ distance) * stride + i % stride) for i in range(peers)]
    return lax.ppermute(x, axis, pairs)


def handed_back(pieces):
    back = [swapped(pieces[j], "ctx", j) for j in range(1, PLANE)]
    return jnp.stack([pieces[0]] + back, 0)


def per_device(queries, keys, values, conv_keys, conv_values, out_weight, cotangent):
    tokens = queries.shape[0]
    heads = queries.shape[1] // FEAT
    width = heads * VDIM
    columns = cotangent.shape[1]
    groups = lax.axis_size("head")
    piece_rows = heads // PLANE * ROWS
    message = (piece_rows + 4 * heads, VDIM)
    S = jax.ShapeDtypeStruct
    step = 2 * tokens * ROWS * VDIM * heads
    project_flops = 2 * tokens * width * columns
    dma = pltpu.SemaphoreType.DMA
    vmem = pltpu.VMEM
    slots = vmem((PLANE, piece_rows, VDIM), F32)

    with jax.named_scope("edge"):
        last_rows = pl.pallas_call(
            edge_kernel,
            out_shape=S((CONV - 1, keys.shape[1] + width), BF16),
            in_specs=[pl.BlockSpec(memory_space=pltpu.HBM)] * 2,
            out_specs=pl.BlockSpec(memory_space=vmem),
            scratch_shapes=[vmem((16, keys.shape[1]), BF16), vmem((16, width), BF16), dma((2,))],
            compiler_params=pltpu.CompilerParams(vmem_limit_bytes=VMEM_LIMIT),
        )(in_hbm(keys), in_hbm(values))
        slabs = lax.axis_size("ctx")
        before = lax.ppermute(last_rows, "ctx", [(i, (i + 1) % slabs) for i in range(slabs)])
    with jax.named_scope("query_features"):
        arrays = (keys, values, conv_keys, conv_values)
        qd, *near_by = call(
            query_kernel,
            (after(queries, last_rows), *arrays),
            [S((heads, ROWS, tokens), BF16)] + [S(x.shape, x.dtype) for x in arrays],
            1 << 20,
            far=range(5),
            scratch=[vmem(queries.shape, BF16), dma((5,))],
        )
    with jax.named_scope("key_features"):
        outs = [
            S((heads, ROWS, tokens), BF16),
            S((tokens, width), BF16),
            S(message, F32),
            S((PLANE, *message), BF16),
        ]
        ops = (*near_by[:2], before, *near_by[2:])
        kf, vc, own, send = call(key_kernel, ops, outs, step, scratch=[slots])
    with jax.named_scope("cotangent"):
        cots = [swapped(after(cotangent, send), "head", j) for j in range(1, groups)]
    with jax.named_scope("prior_share"):
        got = [swapped(send[j], "ctx", j) for j in range(1, PLANE)]

        def join(norm_at, total, received, more):
            outs = [S(total.shape, BF16), S(total.shape, F32)]
            body = functools.partial(share_kernel, norm_at)
            made = call(body, (total, *received), outs[: 2 if more else 1], 1 << 20)
            return made if more else (made[0], None)

        more = lax.axis_size("ctx") > 4 * PLANE
        sent, total = join(piece_rows, own, got, more)
    with jax.named_scope("scores"):
        outs = [
            S((heads, tokens, tokens), BF16),
            S((heads, tokens), F32),
            S((tokens, width), F32),
        ]
        low, den, num = call(score_kernel, (qd, kf, vc), outs, 400 * step)
    with jax.named_scope("prior_planes"):
        sent = after(sent, den)
        norm_join = functools.partial(join, piece_rows)
        moved, strides = planes_ahead(total, sent, 1, norm_join)
    with jax.named_scope("turned"):
        outs = [S((heads, tokens, ROWS), BF16)] * 2
        qt, kt = call(turn_kernel, (after(qd, sent), kf), outs, 1 << 22)
    with jax.named_scope("out_grad"):
        ops = (after(cotangent, qt), *cots, out_weight)
        (out_grad,) = call(
            grad_kernel, ops, [S((tokens, width), F32)], groups * project_flops
        )
    with jax.named_scope("scaled_grad"):
        outs = [
            S((PLANE, piece_rows, VDIM), BF16),
            S((tokens, heads), F32),
            S((tokens, width), BF16),
            S((piece_rows, VDIM), F32),
            S((PLANE, piece_rows, VDIM), BF16),
        ]
        ops = (den, qd, out_grad, own, *got, *moved)
        body = functools.partial(scale_kernel, strides)
        pieces, inverse, scaled, own_later, send_later = call(
            body, ops, outs, step, scratch=[slots]
        )
        prior = handed_back(pieces)
    with jax.named_scope("later_share"):
        got_later = [swapped(send_later[j], "ctx", j) for j in range(1, PLANE)]
    with jax.named_scope("later_planes"):
        plain_join = functools.partial(join, None)
        sent_later, total_later = plain_join(own_later, got_later, more)
        moved_later, strides = planes_ahead(total_later, sent_later, -1, plain_join)
    with jax.named_scope("attended"):
        outs = [S((tokens, width), BF16), S((tokens, columns), BF16)]
        ops = (qt, prior, after(num, sent_later), inverse, out_weight)
        attended, part = call(attend_kernel, ops, outs, step + project_flops)
        parts = [swapped(part, "head", 1)]
    with jax.named_scope("near"):
        ops = (low, after(scaled, sent_later))
        (near,) = call(near_kernel, ops, [S((tokens, width), F32)], 2 * step)
    with jax.named_scope("mixed"):
        for j in list(range(2, groups)) + [0]:
            outs = [S((tokens, columns), BF16 if j else F32)]
            body = functools.partial(mix_kernel, j)
            ops = (after(attended, sent_later), out_weight)
            (part,) = call(body, ops, outs, 2 * project_flops)
            if j:
                parts.append(swapped(part, "head", j))
    with jax.named_scope("later_back"):
        outs = [S((PLANE, piece_rows, VDIM), BF16)]
        body = functools.partial(piece_kernel, -1, strides)
        ops = (own_later, *got_later, after(moved_later[0], part), *moved_later[1:])
        (pieces,) = call(body, ops, outs, 1 << 20)
        later = [pieces[0]] + [swapped(pieces[j], "ctx", j) for j in range(1, PLANE)]
    with jax.named_scope("near"):
        ops = (low, after(scaled, sent_later))
        (near,) = call(near_kernel, ops, [S((tokens, width), F32)], 2 * step)
    with jax.named_scope("mixed"):
        for j in list(range(2, groups)) + [0]:
            outs = [S((tokens, columns), BF16 if j else F32)]
            body = functools.partial(mix_kernel, j)
            ops = (after(attended, sent_later), out_weight)
            (part,) = call(body, ops, outs, 2 * project_flops)
            if j:
                parts.append(swapped(part, "head", j))
    with jax.named_scope("later_back"):
        outs = [S((PLANE, piece_rows, VDIM), BF16)]
        body = functools.partial(piece_kernel, -1, strides)
        ops = (own_later, *got_later, after(moved_later[0], part, near), *moved_later[1:])
        (pieces,) = call(body, ops, outs, 1 << 20)
        later = handed_back(pieces)
    with jax.named_scope("far_grad"):
        block = (tokens, width // PLANE)
        outs = [S((2, *block), BF16)]
        (early,) = call(early_kernel, (kt, near, *later[:2]), outs, 16 * step)
        (value_grad,) = call(
            late_kernel,
            (kt, near, early, *later[2:]),
            [S((tokens, width), BF16)],
            16 * step,
            scratch=[vmem((PLANE - 2, *block), BF16), dma((PLANE,))],
            out_far=True,
        )
    with jax.named_scope("mixed_out"):
        (mixed_out,) = call(
            sum_kernel,
            (part, *[after(x, value_grad) for x in parts]),
            [S((tokens, columns), BF16)],
            1 << 20,
            scratch=[vmem((tokens, columns), BF16), dma((PLANE,))],
            out_far=True,
        )
    return mixed_out, value_grad


def solution(mesh):
    in_specs = (
        P("ctx", "head"),
        P("ctx", "head"),
        P("ctx", "head"),
        P(None, "head"),
        P(None, "head"),
        P("head", None),
        P("ctx", "head"),
    )
    out_specs = (P("ctx", "head"), P("ctx", "head"))
    return jax.shard_map(
        per_device, mesh=mesh, in_specs=in_specs, out_specs=out_specs, check_vma=False
    )
```

```python
import functools

import jax
import jax.numpy as jnp
from jax import lax
from jax.experimental import pallas as pl
from jax.experimental.pallas import tpu as pltpu
from jax.sharding import PartitionSpec as P

FEAT = 16
VDIM = 128
CONV = 3
ROWS = 160
VMEM_LIMIT = 14 * 1024 * 1024
SPARE = 7
PLANE = 4

F32 = jnp.float32
BF16 = jnp.bfloat16
TN = (((0,), (0,)), ((), ()))
NT = (((1,), (1,)), ((), ()))
NN = (((1,), (0,)), ((), ()))


def mm(a, b, dims):
    return lax.dot_general(a, b, dims, preferred_element_type=F32)


def call(body, operands, out_shape, flops, far=(), scratch=(), out_far=False):
    moved = sum(x.size * x.dtype.itemsize for x in operands)
    moved += sum(x.size * x.dtype.itemsize for x in out_shape)
    vmem = pl.BlockSpec(memory_space=pltpu.VMEM)
    hbm = pl.BlockSpec(memory_space=pltpu.HBM)
    return pl.pallas_call(
        body,
        out_shape=out_shape,
        in_specs=[hbm if i in far else vmem for i in range(len(operands))],
        out_specs=[hbm if out_far else vmem for _ in out_shape],
        scratch_shapes=list(scratch),
        compiler_params=pltpu.CompilerParams(vmem_limit_bytes=VMEM_LIMIT),
        cost_estimate=pl.CostEstimate(flops=flops, bytes_accessed=moved, transcendentals=0),
    )(*[in_hbm(x) if i in far else x for i, x in enumerate(operands)])


def in_hbm(x):
    return pltpu.with_memory_space_constraint(x, pltpu.HBM)


def fetch(source, target, sem):
    copy = pltpu.make_async_copy(source, target, sem)
    copy.start()
    return copy


def store_features(out_ref, rows_in, doubled):
    heads = rows_in.shape[0] // FEAT
    tokens = rows_in.shape[1]
    grid = rows_in.reshape(heads, FEAT, tokens) * FEAT ** (-0.25)
    twice = jnp.concatenate([grid, grid], 1)
    out_ref[:, 0:FEAT, :] = grid.astype(BF16)
    half = FEAT // 2
    for turn in range(half):
        square = grid * twice[:, turn : turn + FEAT, :] * 0.5**0.5
        if doubled and turn > 0:
            square = square * 2.0
        out_ref[:, FEAT * (turn + 1) : FEAT * (turn + 2), :] = square.astype(BF16)
    square = grid[:, :half, :] * grid[:, half:, :] * 0.5**0.5
    if doubled:
        square = square * 2.0
    first = lax.broadcasted_iota(jnp.int32, (heads, half, tokens), 1) == 0
    constant = jnp.where(first, 1.0, 0.0)
    out_ref[:, FEAT * (half + 1) :, :] = jnp.concatenate([square, constant], 1).astype(BF16)


def store_piece(rank, head, per_piece, state, own_ref, send_ref):
    slot = rank ^ (head // per_piece)
    at = (head % per_piece) * ROWS
    own_ref[slot, at : at + ROWS, :] = state
    send_ref[slot, at : at + ROWS, :] = state.astype(BF16)


def load_piece(rank, head, per_piece, ref):
    at = (head % per_piece) * ROWS
    return ref[rank ^ (head // per_piece), at : at + ROWS, :]


def edge_kernel(k_far, v_far, edge_ref, k_ref, v_ref, sems):
    tokens, width = k_far.shape
    deep = k_ref.shape[0]
    rows = pl.ds(tokens - deep, deep)
    copies = [fetch(k_far.at[rows], k_ref, sems.at[0]), fetch(v_far.at[rows], v_ref, sems.at[1])]
    last = deep - CONV + 1
    copies[0].wait()
    edge_ref[:, :width] = k_ref[...].astype(F32)[last:].astype(BF16)
    copies[1].wait()
    edge_ref[:, width:] = v_ref[...].astype(F32)[last:].astype(BF16)


def load_kernel(k_far, v_far, ck_far, cv_far, k_ref, v_ref, ck_ref, cv_ref, sems):
    pairs = ((k_far, k_ref), (v_far, v_ref), (ck_far, ck_ref), (cv_far, cv_ref))
    copies = [fetch(a, b, sems.at[i]) for i, (a, b) in enumerate(pairs)]
    for copy in copies:
        copy.wait()


def query_kernel(
    q_far,
    k_far,
    v_far,
    ck_far,
    cv_far,
    qd_ref,
    k_ref,
    v_ref,
    ck_ref,
    cv_ref,
    q_ref,
    sems,
):
    far = (q_far, k_far, v_far, ck_far, cv_far)
    near = (q_ref, k_ref, v_ref, ck_ref, cv_ref)
    copies = [fetch(a, b, sems.at[i]) for i, (a, b) in enumerate(zip(far, near))]
    copies[0].wait()
    store_features(qd_ref, q_ref[...].astype(F32).T, True)
    for copy in copies[1:]:
        copy.wait()


def columns_of(w_ref, distance):
    columns = w_ref.shape[1] // lax.axis_size("head")
    return pl.ds(pl.multiple_of((lax.axis_index("head") ^ distance) * columns, columns), columns)


def turn_kernel(qd_ref, kf_ref, qt_ref, kt_ref):
    for head in range(qd_ref.shape[0]):
        qt_ref[head] = qd_ref[head].T
        kt_ref[head] = kf_ref[head].T


def grad_kernel(*refs):
    *cots, w_ref, og_ref = refs
    total = None
    for j, cot_ref in enumerate(cots):
        term = mm(cot_ref[...], w_ref[:, columns_of(w_ref, j)], NT)
        total = term if total is None else total + term
    og_ref[...] = total


def masked(wanted, value):
    return jnp.where(wanted, value.astype(F32), 0.0)


def conv_rows(x, before, taps):
    x = x.astype(F32)
    row = lax.broadcasted_iota(jnp.int32, x.shape, 0)
    running = taps[0:1, :] * x
    for offset in range(1, CONV):
        moved = pltpu.roll(x, offset, 0)
        for at in range(offset):
            source = before[CONV - 1 - offset + at : CONV - offset + at, :]
            moved = jnp.where(row == at, source, moved)
        running = running + taps[offset : offset + 1, :] * moved
    return running


def norm_rows(norm):
    high = norm.astype(BF16).astype(F32)
    middle = (norm - high).astype(BF16).astype(F32)
    parts = jnp.concatenate([high, middle, norm - high - middle], 0)
    deep = parts.shape[0] // 4
    tail = [parts[i * deep : (i + 1) * deep, VDIM:] for i in range(4)]
    return jnp.concatenate([parts[:, :VDIM], jnp.concatenate(tail, 1)], 0)


def norm_values(lines):
    heads = lines.shape[0] * 4 // 15
    wide = ROWS - VDIM
    tail = [lines[3 * heads :, i * wide : (i + 1) * wide] for i in range(4)]
    parts = jnp.concatenate([lines[: 3 * heads], jnp.concatenate(tail, 0)], 1)
    return parts[:heads] + parts[heads : 2 * heads] + parts[2 * heads :]


def with_lines(state, lines, rows):
    pieces, used = [], 0
    for first in range(0, state.shape[0], ROWS):
        free = min(SPARE, lines.shape[0] - used)
        last = jnp.concatenate(
            [
                state[first + ROWS - SPARE - 1 : first + ROWS - SPARE],
                lines[used : used + free],
                jnp.zeros((SPARE - free, VDIM), F32),
            ][: 3 if free < SPARE else 2],
            0,
        )
        pieces += [state[first : first + ROWS - SPARE - 1], last]
        used += free
    left = rows - state.shape[0]
    blank = left - (lines.shape[0] - used)
    if left > 0:
        pieces.append(lines[used:])
        if blank > 0:
            pieces.append(jnp.zeros((blank, VDIM), F32))
    return jnp.concatenate(pieces, 0)


def lines_in(state, piece_rows):
    count = 15 * (piece_rows // ROWS * PLANE) // 4
    found, used = [], 0
    for first in range(0, piece_rows, ROWS):
        free = min(SPARE, count - used)
        found.append(state[first + ROWS - SPARE : first + ROWS - SPARE + free])
        used += free
    return jnp.concatenate(found + [state[piece_rows : piece_rows + count - used]], 0)


def key_kernel(
    k_ref,
    v_ref,
    before_ref,
    ck_ref,
    cv_ref,
    kf_ref,
    vc_ref,
    own_ref,
    send_ref,
    slots,
):
    rank = lax.rem(lax.axis_index("ctx"), PLANE)
    heads = kf_ref.shape[0]
    per_piece = heads // PLANE
    width = k_ref.shape[1]
    before = masked(lax.axis_index("ctx") > 0, before_ref[...])
    key_conv = conv_rows(k_ref[...], before[:, :width], ck_ref[...])
    store_features(kf_ref, key_conv.T, False)
    ones = jnp.ones((heads, k_ref.shape[0]), BF16)
    row = lax.broadcasted_iota(jnp.int32, (heads, ROWS), 0)
    norm = jnp.zeros((heads, ROWS), F32)
    for head in range(heads):
        at = head * VDIM
        value = conv_rows(
            v_ref[:, at : at + VDIM],
            before[:, width + at : width + at + VDIM],
            cv_ref[:, at : at + VDIM],
        ).astype(BF16)
        vc_ref[:, at : at + VDIM] = value
        feat = kf_ref[head]
        norm = jnp.where(row == head, mm(ones, feat, NT), norm)
        first = (head % per_piece) * ROWS
        slots[rank ^ (head // per_piece), first : first + ROWS, :] = mm(feat, value, NN)
    lines = norm_rows(norm)
    for slot in range(PLANE):
        piece = with_lines(slots[slot], lines, own_ref.shape[0])
        if slot == 0:
            own_ref[...] = piece
        else:
            send_ref[slot] = piece.astype(BF16)


def share_kernel(norm_at, own_ref, *refs):
    sent_at = -1 if refs[-1].dtype == BF16 else -2
    got_refs, sent_ref = refs[:sent_at], refs[sent_at]
    total = own_ref[...]
    for got_ref in got_refs:
        total = total + got_ref[...].astype(F32)
    if norm_at is not None:
        lines = norm_rows(norm_values(lines_in(total, norm_at)))
        total = with_lines(total[:norm_at], lines, total.shape[0])
    sent_ref[...] = total.astype(BF16)
    if sent_at == -2:
        refs[-1][...] = total


def store_pieces(sign, strides, got_refs, moved_refs, pieces_ref):
    rows = pieces_ref.shape[1]

    def is_ahead(other, here):
        return other < here if sign > 0 else other > here

    before = jnp.zeros(got_refs[0].shape, F32)
    for ref, (stride, distance) in zip(moved_refs, strides):
        if distance:
            group = lax.div(lax.axis_index("ctx"), PLANE * stride)
            before = before + masked(is_ahead(group ^ distance, group), ref[...])
        else:
            before = before + ref[...].astype(F32)
    rank = lax.rem(lax.axis_index("ctx"), PLANE)
    extra = None
    for slot in range(PLANE):
        total = before
        for i in range(PLANE):
            if i != slot:
                total = total + masked(is_ahead(rank ^ i, rank ^ slot), got_refs[i][...])
        pieces_ref[slot] = total[:rows].astype(BF16)
        extra = total if slot == 0 else extra
    return extra


def piece_kernel(sign, strides, *refs):
    store_pieces(sign, strides, refs[:PLANE], refs[PLANE:-1], refs[-1])


def score_kernel(qd_ref, kf_ref, vc_ref, low_ref, den_ref, num_ref):
    heads = kf_ref.shape[0]
    tokens = kf_ref.shape[2]
    key_at = lax.broadcasted_iota(jnp.int32, (tokens, tokens), 0)
    query_at = lax.broadcasted_iota(jnp.int32, (tokens, tokens), 1)
    causal = key_at <= query_at
    for head in range(heads):
        scores = jnp.where(causal, mm(kf_ref[head], qd_ref[head], TN), 0.0)
        den_ref[head : head + 1, :] = jnp.sum(scores, 0, keepdims=True)
        low = scores.astype(BF16)
        low_ref[head] = low
        at = head * VDIM
        num_ref[:, at : at + VDIM] = mm(low, vc_ref[:, at : at + VDIM], TN)


def scale_kernel(strides, den_ref, qd_ref, og_ref, *refs):
    *refs, pieces_ref, inv_ref, sg_ref, own_ref, send_ref, slots = refs
    rank = lax.rem(lax.axis_index("ctx"), PLANE)
    heads = qd_ref.shape[0]
    per_piece = heads // PLANE
    lines = store_pieces(1, strides, refs[:PLANE], refs[PLANE:], pieces_ref)
    norm = norm_values(lines_in(lines, pieces_ref.shape[1]))
    high = norm.astype(BF16).astype(F32)
    middle = (norm - high).astype(BF16).astype(F32)
    rest = norm - high - middle
    parts = jnp.concatenate([high, middle, rest, jnp.zeros_like(rest)], 0).astype(BF16)
    lines = []
    for head in range(heads):
        terms = mm(parts, qd_ref[head], NN)
        line = den_ref[head : head + 1, :] + terms[head : head + 1, :]
        line = line + terms[heads + head : heads + head + 1, :]
        lines.append(line + terms[2 * heads + head : 2 * heads + head + 1, :])
    inverse = (1.0 / jnp.concatenate(lines, 0)).T
    inv_ref[...] = inverse
    for head in range(heads):
        at = head * VDIM
        scaled = (og_ref[:, at : at + VDIM] * inverse[:, head : head + 1]).astype(BF16)
        sg_ref[:, at : at + VDIM] = scaled
        store_piece(rank, head, per_piece, mm(qd_ref[head], scaled, NN), slots, send_ref)
    own_ref[...] = slots[0]


def near_kernel(low_ref, sg_ref, vg_ref):
    for head in range(low_ref.shape[0]):
        at = head * VDIM
        vg_ref[:, at : at + VDIM] = mm(low_ref[head], sg_ref[:, at : at + VDIM], NN)


def attend_kernel(qt_ref, prior_ref, num_ref, inv_ref, w_ref, att_ref, part_ref):
    rank = lax.rem(lax.axis_index("ctx"), PLANE)
    heads = qt_ref.shape[0]
    per_piece = heads // PLANE
    for head in range(heads):
        at = head * VDIM
        prior = load_piece(rank, head, per_piece, prior_ref)
        total = num_ref[:, at : at + VDIM] + mm(qt_ref[head], prior, NN)
        att_ref[:, at : at + VDIM] = (total * inv_ref[:, head : head + 1]).astype(BF16)
    part_ref[...] = mm(att_ref[...], w_ref[:, columns_of(w_ref, 1)], NN).astype(BF16)


def mix_kernel(distance, att_ref, w_ref, part_ref):
    weight = w_ref[:, columns_of(w_ref, distance)]
    part_ref[...] = mm(att_ref[...], weight, NN).astype(part_ref.dtype)


def far_block(distance, kt_ref, near_ref, later_ref):
    per_piece = kt_ref.shape[0] // PLANE
    first = (lax.rem(lax.axis_index("ctx"), PLANE) ^ distance) * per_piece
    blocks = []
    for i in range(per_piece):
        columns = pl.ds(pl.multiple_of((first + i) * VDIM, VDIM), VDIM)
        later = later_ref[i * ROWS : (i + 1) * ROWS, :]
        total = near_ref[:, columns] + mm(kt_ref[first + i], later, NN)
        blocks.append(total.astype(BF16))
    return jnp.concatenate(blocks, 1)


def early_kernel(kt_ref, near_ref, *refs):
    *later_refs, block_ref = refs
    for distance, later_ref in enumerate(later_refs):
        block_ref[distance] = far_block(distance, kt_ref, near_ref, later_ref)


def late_kernel(kt_ref, near_ref, early_ref, *refs):
    *later_refs, vg_far, block_ref, sems = refs
    early, columns = early_ref.shape[0], early_ref.shape[2]
    rank = lax.rem(lax.axis_index("ctx"), PLANE)

    def send(distance, ref):
        start = pl.multiple_of((rank ^ distance) * columns, columns)
        return fetch(ref, vg_far.at[:, pl.ds(start, columns)], sems.at[distance])

    copies = [send(distance, early_ref.at[distance]) for distance in range(early)]
    for i, later_ref in enumerate(later_refs):
        block_ref[i] = far_block(early + i, kt_ref, near_ref, later_ref)
        copies.append(send(early + i, block_ref.at[i]))
    for copy in copies:
        copy.wait()


def sum_kernel(part_ref, *refs):
    *other_refs, mixed_far, mixed_ref, sems = refs
    copies = []
    deep = part_ref.shape[0] // PLANE
    for step in range(PLANE):
        rows = pl.ds(step * deep, deep)
        total = part_ref[rows, :]
        for other_ref in other_refs:
            total = total + other_ref[rows, :].astype(F32)
        mixed_ref[rows, :] = total.astype(BF16)
        copies.append(fetch(mixed_ref.at[rows], mixed_far.at[rows], sems.at[step]))
    for copy in copies:
        copy.wait()


def shifted(x, axis, by):
    peers = lax.axis_size(axis)
    pairs = [(i, i + by) for i in range(peers) if 0 <= i + by < peers]
    return lax.ppermute(x, axis, pairs)


def after(x, *others):
    return lax.optimization_barrier((x, *others))[0]


def planes_ahead(total, sent, sign, join):
    planes = lax.axis_size("ctx") // PLANE
    received, strides = [], []
    stride = 1
    while stride < planes:
        if (planes // stride) % 4 == 0:
            moved = [swapped(sent, "ctx", j, stride * PLANE) for j in range(1, 4)]
            strides += [(stride, j) for j in range(1, 4)]
            stride = stride * 4
        else:
            moved = [shifted(sent, "ctx", sign * stride * PLANE)]
            strides.append((stride, 0))
            stride = stride * 2
        received += moved
        if stride < planes:
            sent, total = join(total, moved, stride * 2 < planes)
    return received, strides


def swapped(x, axis, distance, stride=1):
    peers = lax.axis_size(axis)
    pairs = [(i, (i // stride ^ distance) * stride + i % stride) for i in range(peers)]
    return lax.ppermute(x, axis, pairs)


def handed_back(pieces):
    back = [swapped(pieces[j], "ctx", j) for j in range(1, PLANE)]
    return jnp.stack([pieces[0]] + back, 0)


def per_device(queries, keys, values, conv_keys, conv_values, out_weight, cotangent):
    tokens = queries.shape[0]
    heads = queries.shape[1] // FEAT
    width = heads * VDIM
    columns = cotangent.shape[1]
    groups = lax.axis_size("head")
    piece_rows = heads // PLANE * ROWS
    extra = max(0, 15 * heads // 4 - SPARE * heads // PLANE)
    message = (piece_rows + -(-extra // 16) * 16, VDIM)
    S = jax.ShapeDtypeStruct
    step = 2 * tokens * ROWS * VDIM * heads
    project_flops = 2 * tokens * width * columns
    dma = pltpu.SemaphoreType.DMA
    vmem = pltpu.VMEM
    slots = vmem((PLANE, piece_rows, VDIM), F32)

    with jax.named_scope("edge"):
        last_rows = pl.pallas_call(
            edge_kernel,
            out_shape=S((CONV - 1, keys.shape[1] + width), BF16),
            in_specs=[pl.BlockSpec(memory_space=pltpu.HBM)] * 2,
            out_specs=pl.BlockSpec(memory_space=vmem),
            scratch_shapes=[vmem((16, keys.shape[1]), BF16), vmem((16, width), BF16), dma((2,))],
            compiler_params=pltpu.CompilerParams(vmem_limit_bytes=VMEM_LIMIT),
        )(in_hbm(keys), in_hbm(values))
        slabs = lax.axis_size("ctx")
        before = lax.ppermute(last_rows, "ctx", [(i, (i + 1) % slabs) for i in range(slabs)])
    with jax.named_scope("query_features"):
        arrays = (keys, values, conv_keys, conv_values)
        qd, *near_by = call(
            query_kernel,
            (after(queries, last_rows), *arrays),
            [S((heads, ROWS, tokens), BF16)] + [S(x.shape, x.dtype) for x in arrays],
            1 << 20,
            far=range(5),
            scratch=[vmem(queries.shape, BF16), dma((5,))],
        )
    with jax.named_scope("key_features"):
        outs = [
            S((heads, ROWS, tokens), BF16),
            S((tokens, width), BF16),
            S(message, F32),
            S((PLANE, *message), BF16),
        ]
        ops = (*near_by[:2], before, *near_by[2:])
        kf, vc, own, send = call(key_kernel, ops, outs, step, scratch=[slots])
    with jax.named_scope("cotangent"):
        cots = [swapped(after(cotangent, last_rows), "head", j) for j in range(1, groups)]
    with jax.named_scope("prior_share"):
        got = [swapped(send[j], "ctx", j) for j in range(1, PLANE)]

        def join(norm_at, total, received, more):
            outs = [S(total.shape, BF16), S(total.shape, F32)]
            body = functools.partial(share_kernel, norm_at)
            made = call(body, (total, *received), outs[: 2 if more else 1], 1 << 20)
            return made if more else (made[0], None)

        more = lax.axis_size("ctx") > 4 * PLANE
        sent, total = join(piece_rows, own, got, more)
    with jax.named_scope("scores"):
        outs = [
            S((heads, tokens, tokens), BF16),
            S((heads, tokens), F32),
            S((tokens, width), F32),
        ]
        low, den, num = call(score_kernel, (qd, kf, vc), outs, 400 * step)
    with jax.named_scope("prior_planes"):
        sent = after(sent, den)
        norm_join = functools.partial(join, piece_rows)
        moved, strides = planes_ahead(total, sent, 1, norm_join)
    with jax.named_scope("turned"):
        outs = [S((heads, tokens, ROWS), BF16)] * 2
        qt, kt = call(turn_kernel, (after(qd, sent), kf), outs, 1 << 22)
    with jax.named_scope("out_grad"):
        ops = (after(cotangent, qt), *cots, out_weight)
        (out_grad,) = call(
            grad_kernel, ops, [S((tokens, width), F32)], groups * project_flops
        )
    with jax.named_scope("scaled_grad"):
        outs = [
            S((PLANE, piece_rows, VDIM), BF16),
            S((tokens, heads), F32),
            S((tokens, width), BF16),
            S((piece_rows, VDIM), F32),
            S((PLANE, piece_rows, VDIM), BF16),
        ]
        ops = (den, qd, out_grad, own, *got, *moved)
        body = functools.partial(scale_kernel, strides)
        pieces, inverse, scaled, own_later, send_later = call(
            body, ops, outs, step, scratch=[slots]
        )
        prior = handed_back(pieces)
    with jax.named_scope("later_share"):
        got_later = [swapped(send_later[j], "ctx", j) for j in range(1, PLANE)]
    with jax.named_scope("later_planes"):
        plain_join = functools.partial(join, None)
        sent_later, total_later = plain_join(own_later, got_later, more)
        moved_later, strides = planes_ahead(total_later, sent_later, -1, plain_join)
    with jax.named_scope("attended"):
        outs = [S((tokens, width), BF16), S((tokens, columns), BF16)]
        ops = (qt, prior, after(num, sent_later), inverse, out_weight)
        attended, part = call(attend_kernel, ops, outs, step + project_flops)
        parts = [swapped(part, "head", 1)]
    with jax.named_scope("near"):
        ops = (low, after(scaled, sent_later))
        (near,) = call(near_kernel, ops, [S((tokens, width), F32)], 2 * step)
    with jax.named_scope("mixed"):
        for j in list(range(2, groups)) + [0]:
            outs = [S((tokens, columns), BF16 if j else F32)]
            body = functools.partial(mix_kernel, j)
            ops = (after(attended, sent_later), out_weight)
            (part,) = call(body, ops, outs, 2 * project_flops)
            if j:
                parts.append(swapped(part, "head", j))
    with jax.named_scope("later_back"):
        outs = [S((PLANE, piece_rows, VDIM), BF16)]
        body = functools.partial(piece_kernel, -1, strides)
        ops = (own_later, *got_later, after(moved_later[0], part), *moved_later[1:])
        (pieces,) = call(body, ops, outs, 1 << 20)
        later = [pieces[0]] + [swapped(pieces[j], "ctx", j) for j in range(1, PLANE)]
    with jax.named_scope("near"):
        ops = (low, after(scaled, sent_later))
        (near,) = call(near_kernel, ops, [S((tokens, width), F32)], 2 * step)
    with jax.named_scope("mixed"):
        for j in list(range(2, groups)) + [0]:
            outs = [S((tokens, columns), BF16 if j else F32)]
            body = functools.partial(mix_kernel, j)
            ops = (after(attended, sent_later), out_weight)
            (part,) = call(body, ops, outs, 2 * project_flops)
            if j:
                parts.append(swapped(part, "head", j))
    with jax.named_scope("later_back"):
        outs = [S((PLANE, piece_rows, VDIM), BF16)]
        body = functools.partial(piece_kernel, -1, strides)
        ops = (own_later, *got_later, after(moved_later[0], part, near), *moved_later[1:])
        (pieces,) = call(body, ops, outs, 1 << 20)
        later = handed_back(pieces)
    with jax.named_scope("far_grad"):
        block = (tokens, width // PLANE)
        outs = [S((2, *block), BF16)]
        (early,) = call(early_kernel, (kt, near, *later[:2]), outs, 16 * step)
        (value_grad,) = call(
            late_kernel,
            (kt, near, early, *later[2:]),
            [S((tokens, width), BF16)],
            16 * step,
            scratch=[vmem((PLANE - 2, *block), BF16), dma((PLANE,))],
            out_far=True,
        )
    with jax.named_scope("mixed_out"):
        (mixed_out,) = call(
            sum_kernel,
            (part, *[after(x, value_grad) for x in parts]),
            [S((tokens, columns), BF16)],
            1 << 20,
            scratch=[vmem((tokens, columns), BF16), dma((PLANE,))],
            out_far=True,
        )
    return mixed_out, value_grad


def solution(mesh):
    in_specs = (
        P("ctx", "head"),
        P("ctx", "head"),
        P("ctx", "head"),
        P(None, "head"),
        P(None, "head"),
        P("head", None),
        P("ctx", "head"),
    )
    out_specs = (P("ctx", "head"), P("ctx", "head"))
    return jax.shard_map(
        per_device, mesh=mesh, in_specs=in_specs, out_specs=out_specs, check_vma=False
    )
```

```python
import functools

import jax
import jax.numpy as jnp
from jax import lax
from jax.experimental import pallas as pl
from jax.experimental.pallas import tpu as pltpu
from jax.sharding import PartitionSpec as P

FEAT = 16
VDIM = 128
CONV = 3
ROWS = 160
VMEM_LIMIT = 14 * 1024 * 1024
SPARE = 7
PLANE = 4

F32 = jnp.float32
BF16 = jnp.bfloat16
TN = (((0,), (0,)), ((), ()))
NT = (((1,), (1,)), ((), ()))
NN = (((1,), (0,)), ((), ()))


def mm(a, b, dims):
    return lax.dot_general(a, b, dims, preferred_element_type=F32)


def call(body, operands, out_shape, flops, far=(), scratch=(), out_far=False):
    moved = sum(x.size * x.dtype.itemsize for x in operands)
    moved += sum(x.size * x.dtype.itemsize for x in out_shape)
    vmem = pl.BlockSpec(memory_space=pltpu.VMEM)
    hbm = pl.BlockSpec(memory_space=pltpu.HBM)
    return pl.pallas_call(
        body,
        out_shape=out_shape,
        in_specs=[hbm if i in far else vmem for i in range(len(operands))],
        out_specs=[hbm if out_far else vmem for _ in out_shape],
        scratch_shapes=list(scratch),
        compiler_params=pltpu.CompilerParams(vmem_limit_bytes=VMEM_LIMIT),
        cost_estimate=pl.CostEstimate(flops=flops, bytes_accessed=moved, transcendentals=0),
    )(*[in_hbm(x) if i in far else x for i, x in enumerate(operands)])


def in_hbm(x):
    return pltpu.with_memory_space_constraint(x, pltpu.HBM)


def fetch(source, target, sem):
    copy = pltpu.make_async_copy(source, target, sem)
    copy.start()
    return copy


def store_features(out_ref, rows_in, doubled):
    heads = rows_in.shape[0] // FEAT
    tokens = rows_in.shape[1]
    grid = rows_in.reshape(heads, FEAT, tokens) * FEAT ** (-0.25)
    twice = jnp.concatenate([grid, grid], 1)
    out_ref[:, 0:FEAT, :] = grid.astype(BF16)
    half = FEAT // 2
    for turn in range(half):
        square = grid * twice[:, turn : turn + FEAT, :] * 0.5**0.5
        if doubled and turn > 0:
            square = square * 2.0
        out_ref[:, FEAT * (turn + 1) : FEAT * (turn + 2), :] = square.astype(BF16)
    square = grid[:, :half, :] * grid[:, half:, :] * 0.5**0.5
    if doubled:
        square = square * 2.0
    first = lax.broadcasted_iota(jnp.int32, (heads, half, tokens), 1) == 0
    constant = jnp.where(first, 1.0, 0.0)
    out_ref[:, FEAT * (half + 1) :, :] = jnp.concatenate([square, constant], 1).astype(BF16)


def store_piece(rank, head, per_piece, state, own_ref, send_ref):
    slot = rank ^ (head // per_piece)
    at = (head % per_piece) * ROWS
    own_ref[slot, at : at + ROWS, :] = state
    send_ref[slot, at : at + ROWS, :] = state.astype(BF16)


def load_piece(rank, head, per_piece, ref):
    at = (head % per_piece) * ROWS
    return ref[rank ^ (head // per_piece), at : at + ROWS, :]


def edge_kernel(k_far, v_far, edge_ref, k_ref, v_ref, sems):
    tokens, width = k_far.shape
    deep = k_ref.shape[0]
    rows = pl.ds(tokens - deep, deep)
    copies = [fetch(k_far.at[rows], k_ref, sems.at[0]), fetch(v_far.at[rows], v_ref, sems.at[1])]
    last = deep - CONV + 1
    copies[0].wait()
    edge_ref[:, :width] = k_ref[...].astype(F32)[last:].astype(BF16)
    copies[1].wait()
    edge_ref[:, width:] = v_ref[...].astype(F32)[last:].astype(BF16)


def load_kernel(k_far, v_far, ck_far, cv_far, k_ref, v_ref, ck_ref, cv_ref, sems):
    pairs = ((k_far, k_ref), (v_far, v_ref), (ck_far, ck_ref), (cv_far, cv_ref))
    copies = [fetch(a, b, sems.at[i]) for i, (a, b) in enumerate(pairs)]
    for copy in copies:
        copy.wait()


def query_kernel(
    q_far,
    k_far,
    v_far,
    ck_far,
    cv_far,
    qd_ref,
    k_ref,
    v_ref,
    ck_ref,
    cv_ref,
    q_ref,
    sems,
):
    far = (q_far, k_far, v_far, ck_far, cv_far)
    near = (q_ref, k_ref, v_ref, ck_ref, cv_ref)
    copies = [fetch(a, b, sems.at[i]) for i, (a, b) in enumerate(zip(far, near))]
    copies[0].wait()
    store_features(qd_ref, q_ref[...].astype(F32).T, True)
    for copy in copies[1:]:
        copy.wait()


def columns_of(w_ref, distance):
    columns = w_ref.shape[1] // lax.axis_size("head")
    return pl.ds(pl.multiple_of((lax.axis_index("head") ^ distance) * columns, columns), columns)


def turn_kernel(qd_ref, kf_ref, qt_ref, kt_ref):
    for head in range(qd_ref.shape[0]):
        qt_ref[head] = qd_ref[head].T
        kt_ref[head] = kf_ref[head].T


def grad_kernel(*refs):
    *cots, w_ref, og_ref = refs
    total = None
    for j, cot_ref in enumerate(cots):
        term = mm(cot_ref[...], w_ref[:, columns_of(w_ref, j)], NT)
        total = term if total is None else total + term
    og_ref[...] = total


def masked(wanted, value):
    return jnp.where(wanted, value.astype(F32), 0.0)


def conv_rows(x, before, taps):
    x = x.astype(F32)
    row = lax.broadcasted_iota(jnp.int32, x.shape, 0)
    running = taps[0:1, :] * x
    for offset in range(1, CONV):
        moved = pltpu.roll(x, offset, 0)
        for at in range(offset):
            source = before[CONV - 1 - offset + at : CONV - offset + at, :]
            moved = jnp.where(row == at, source, moved)
        running = running + taps[offset : offset + 1, :] * moved
    return running


def norm_rows(norm):
    high = norm.astype(BF16).astype(F32)
    middle = (norm - high).astype(BF16).astype(F32)
    parts = jnp.concatenate([high, middle, norm - high - middle], 0)
    deep = parts.shape[0] // 4
    tail = [parts[i * deep : (i + 1) * deep, VDIM:] for i in range(4)]
    return jnp.concatenate([parts[:, :VDIM], jnp.concatenate(tail, 1)], 0)


def norm_values(lines):
    heads = lines.shape[0] * 4 // 15
    wide = ROWS - VDIM
    tail = [lines[3 * heads :, i * wide : (i + 1) * wide] for i in range(4)]
    parts = jnp.concatenate([lines[: 3 * heads], jnp.concatenate(tail, 0)], 1)
    return parts[:heads] + parts[heads : 2 * heads] + parts[2 * heads :]


def with_lines(state, lines, rows):
    pieces, used = [], 0
    for first in range(0, state.shape[0], ROWS):
        free = min(SPARE, lines.shape[0] - used)
        last = jnp.concatenate(
            [
                state[first + ROWS - SPARE - 1 : first + ROWS - SPARE],
                lines[used : used + free],
                jnp.zeros((SPARE - free, VDIM), F32),
            ][: 3 if free < SPARE else 2],
            0,
        )
        pieces += [state[first : first + ROWS - SPARE - 1], last]
        used += free
    left = rows - state.shape[0]
    blank = left - (lines.shape[0] - used)
    if left > 0:
        pieces.append(lines[used:])
        if blank > 0:
            pieces.append(jnp.zeros((blank, VDIM), F32))
    return jnp.concatenate(pieces, 0)


def lines_in(state, piece_rows):
    count = 15 * (piece_rows // ROWS * PLANE) // 4
    found, used = [], 0
    for first in range(0, piece_rows, ROWS):
        free = min(SPARE, count - used)
        found.append(state[first + ROWS - SPARE - 1 : first + ROWS, :][1 : 1 + free].astype(F32))
        used += free
    rest = state[piece_rows:, :][: count - used].astype(F32)
    return jnp.concatenate(found + [rest], 0)


def key_kernel(
    k_ref,
    v_ref,
    before_ref,
    ck_ref,
    cv_ref,
    kf_ref,
    vc_ref,
    own_ref,
    send_ref,
    slots,
):
    rank = lax.rem(lax.axis_index("ctx"), PLANE)
    heads = kf_ref.shape[0]
    per_piece = heads // PLANE
    width = k_ref.shape[1]
    before = masked(lax.axis_index("ctx") > 0, before_ref[...])
    key_conv = conv_rows(k_ref[...], before[:, :width], ck_ref[...])
    store_features(kf_ref, key_conv.T, False)
    ones = jnp.ones((heads, k_ref.shape[0]), BF16)
    row = lax.broadcasted_iota(jnp.int32, (heads, ROWS), 0)
    norm = jnp.zeros((heads, ROWS), F32)
    for head in range(heads):
        at = head * VDIM
        value = conv_rows(
            v_ref[:, at : at + VDIM],
            before[:, width + at : width + at + VDIM],
            cv_ref[:, at : at + VDIM],
        ).astype(BF16)
        vc_ref[:, at : at + VDIM] = value
        feat = kf_ref[head]
        norm = jnp.where(row == head, mm(ones, feat, NT), norm)
        first = (head % per_piece) * ROWS
        slots[rank ^ (head // per_piece), first : first + ROWS, :] = mm(feat, value, NN)
    lines = norm_rows(norm)
    for slot in range(PLANE):
        piece = with_lines(slots[slot], lines, own_ref.shape[0])
        if slot == 0:
            own_ref[...] = piece
        else:
            send_ref[slot] = piece.astype(BF16)


def share_kernel(piece_rows, own_ref, *refs):
    got_refs, out_refs = refs[: PLANE - 1], refs[PLANE - 1 :]
    total = own_ref[...]
    for got_ref in got_refs:
        total = total + got_ref[...].astype(F32)
    half = piece_rows // 2
    lines = norm_rows(norm_values(lines_in(total, piece_rows)))
    parts = (with_tail(total[:half], lines, out_refs[0].shape[0]), total[half:piece_rows])
    for ref, part in zip(out_refs, parts):
        ref[...] = part.astype(BF16)
    for ref, part in zip(out_refs[2:], parts):
        ref[...] = part


def with_tail(state, lines, rows):
    blank = jnp.zeros((rows - state.shape[0] - lines.shape[0], VDIM), F32)
    return jnp.concatenate([state, lines, blank], 0)


def join_kernel(tail, total_ref, *refs):
    out_at = -1 if refs[-1].dtype == BF16 else -2
    total = total_ref[...]
    for got_ref in refs[:out_at]:
        total = total + got_ref[...].astype(F32)
    if tail is not None:
        lines = norm_rows(norm_values(total[tail[0] : tail[1]]))
        total = with_tail(total[: tail[0]], lines, total.shape[0])
    refs[out_at][...] = total.astype(BF16)
    if out_at == -2:
        refs[-1][...] = total


def is_ahead(sign, other, here):
    return other < here if sign > 0 else other > here


def before_plane(sign, strides, refs, rows):
    total = 0.0
    for ref, (stride, distance) in zip(refs, strides):
        if distance:
            group = lax.div(lax.axis_index("ctx"), PLANE * stride)
            total = total + masked(is_ahead(sign, group ^ distance, group), ref[rows, :])
        else:
            total = total + ref[rows, :].astype(F32)
    return total


def piece_kernel(sign, strides, *refs):
    got_refs, moved_refs, pieces_ref = refs[:PLANE], refs[PLANE:-1], refs[-1]
    rank = lax.rem(lax.axis_index("ctx"), PLANE)
    count = len(strides)
    parts = len(moved_refs) // count
    deep = pieces_ref.shape[1] // parts
    for part in range(parts):
        refs = moved_refs[part * count : (part + 1) * count]
        before = before_plane(sign, strides, refs, pl.ds(0, deep))
        rows = pl.ds(part * deep, deep)
        for slot in range(PLANE):
            total = before
            for i in range(PLANE):
                if i != slot:
                    ahead = is_ahead(sign, rank ^ i, rank ^ slot)
                    total = total + masked(ahead, got_refs[i][rows, :])
            pieces_ref[slot, rows, :] = total.astype(BF16)


def score_kernel(qd_ref, kf_ref, vc_ref, low_ref, den_ref, num_ref):
    heads = kf_ref.shape[0]
    tokens = kf_ref.shape[2]
    key_at = lax.broadcasted_iota(jnp.int32, (tokens, tokens), 0)
    query_at = lax.broadcasted_iota(jnp.int32, (tokens, tokens), 1)
    causal = key_at <= query_at
    for head in range(heads):
        scores = jnp.where(causal, mm(kf_ref[head], qd_ref[head], TN), 0.0)
        den_ref[head : head + 1, :] = jnp.sum(scores, 0, keepdims=True)
        low = scores.astype(BF16)
        low_ref[head] = low
        at = head * VDIM
        num_ref[:, at : at + VDIM] = mm(low, vc_ref[:, at : at + VDIM], TN)


def scale_kernel(strides, den_ref, qd_ref, og_ref, *refs):
    *refs, inv_ref, sg_ref, own_ref, send_ref, slots = refs
    got_refs, moved_refs = refs[:PLANE], refs[PLANE:]
    rank = lax.rem(lax.axis_index("ctx"), PLANE)
    heads = qd_ref.shape[0]
    per_piece = heads // PLANE
    piece_rows = per_piece * ROWS
    lines = before_plane(1, strides, moved_refs, pl.ds(piece_rows // 2, 15 * heads // 4))
    for i in range(1, PLANE):
        here = lines_in(got_refs[i], piece_rows)
        lines = lines + masked(is_ahead(1, rank ^ i, rank), here)
    norm = norm_values(lines)
    high = norm.astype(BF16).astype(F32)
    middle = (norm - high).astype(BF16).astype(F32)
    rest = norm - high - middle
    parts = jnp.concatenate([high, middle, rest, jnp.zeros_like(rest)], 0).astype(BF16)
    lines = []
    for head in range(heads):
        terms = mm(parts, qd_ref[head], NN)
        line = den_ref[head : head + 1, :] + terms[head : head + 1, :]
        line = line + terms[heads + head : heads + head + 1, :]
        lines.append(line + terms[2 * heads + head : 2 * heads + head + 1, :])
    inverse = (1.0 / jnp.concatenate(lines, 0)).T
    inv_ref[...] = inverse
    for head in range(heads):
        at = head * VDIM
        scaled = (og_ref[:, at : at + VDIM] * inverse[:, head : head + 1]).astype(BF16)
        sg_ref[:, at : at + VDIM] = scaled
        store_piece(rank, head, per_piece, mm(qd_ref[head], scaled, NN), slots, send_ref)
    own_ref[...] = slots[0]


def near_kernel(low_ref, sg_ref, vg_ref):
    for head in range(low_ref.shape[0]):
        at = head * VDIM
        vg_ref[:, at : at + VDIM] = mm(low_ref[head], sg_ref[:, at : at + VDIM], NN)


def attend_kernel(qt_ref, prior_ref, num_ref, inv_ref, w_ref, att_ref, part_ref):
    rank = lax.rem(lax.axis_index("ctx"), PLANE)
    heads = qt_ref.shape[0]
    per_piece = heads // PLANE
    for head in range(heads):
        at = head * VDIM
        prior = load_piece(rank, head, per_piece, prior_ref)
        total = num_ref[:, at : at + VDIM] + mm(qt_ref[head], prior, NN)
        att_ref[:, at : at + VDIM] = (total * inv_ref[:, head : head + 1]).astype(BF16)
    part_ref[...] = mm(att_ref[...], w_ref[:, columns_of(w_ref, 1)], NN).astype(BF16)


def mix_kernel(distance, att_ref, w_ref, part_ref):
    weight = w_ref[:, columns_of(w_ref, distance)]
    part_ref[...] = mm(att_ref[...], weight, NN).astype(part_ref.dtype)


def far_block(distance, kt_ref, near_ref, later_ref):
    per_piece = kt_ref.shape[0] // PLANE
    first = (lax.rem(lax.axis_index("ctx"), PLANE) ^ distance) * per_piece
    blocks = []
    for i in range(per_piece):
        columns = pl.ds(pl.multiple_of((first + i) * VDIM, VDIM), VDIM)
        later = later_ref[i * ROWS : (i + 1) * ROWS, :]
        total = near_ref[:, columns] + mm(kt_ref[first + i], later, NN)
        blocks.append(total.astype(BF16))
    return jnp.concatenate(blocks, 1)


def early_kernel(kt_ref, near_ref, *refs):
    *later_refs, block_ref = refs
    for distance, later_ref in enumerate(later_refs):
        block_ref[distance] = far_block(distance, kt_ref, near_ref, later_ref)


def late_kernel(kt_ref, near_ref, early_ref, *refs):
    *later_refs, vg_far, block_ref, sems = refs
    early, columns = early_ref.shape[0], early_ref.shape[2]
    rank = lax.rem(lax.axis_index("ctx"), PLANE)

    def send(distance, ref):
        start = pl.multiple_of((rank ^ distance) * columns, columns)
        return fetch(ref, vg_far.at[:, pl.ds(start, columns)], sems.at[distance])

    copies = [send(distance, early_ref.at[distance]) for distance in range(early)]
    for i, later_ref in enumerate(later_refs):
        block_ref[i] = far_block(early + i, kt_ref, near_ref, later_ref)
        copies.append(send(early + i, block_ref.at[i]))
    for copy in copies:
        copy.wait()


def sum_kernel(part_ref, *refs):
    *other_refs, mixed_far, mixed_ref, sems = refs
    copies = []
    deep = part_ref.shape[0] // PLANE
    for step in range(PLANE):
        rows = pl.ds(step * deep, deep)
        total = part_ref[rows, :]
        for other_ref in other_refs:
            total = total + other_ref[rows, :].astype(F32)
        mixed_ref[rows, :] = total.astype(BF16)
        copies.append(fetch(mixed_ref.at[rows], mixed_far.at[rows], sems.at[step]))
    for copy in copies:
        copy.wait()


def shifted(x, axis, by):
    peers = lax.axis_size(axis)
    pairs = [(i, i + by) for i in range(peers) if 0 <= i + by < peers]
    return lax.ppermute(x, axis, pairs)


def after(x, *others):
    return lax.optimization_barrier((x, *others))[0]


def planes_ahead(total, sent, sign, join):
    planes = lax.axis_size("ctx") // PLANE
    received, strides = [], []
    stride = 1
    while stride < planes:
        if (planes // stride) % 4 == 0:
            moved = [swapped(sent, "ctx", j, stride * PLANE) for j in range(1, 4)]
            strides += [(stride, j) for j in range(1, 4)]
            stride = stride * 4
        else:
            moved = [shifted(sent, "ctx", sign * stride * PLANE)]
            strides.append((stride, 0))
            stride = stride * 2
        received += moved
        if stride < planes:
            sent, total = join(total, moved, stride * 2 < planes)
    return received, strides


def swapped(x, axis, distance, stride=1):
    peers = lax.axis_size(axis)
    pairs = [(i, (i // stride ^ distance) * stride + i % stride) for i in range(peers)]
    return lax.ppermute(x, axis, pairs)


def handed_back(pieces):
    back = [swapped(pieces[j], "ctx", j) for j in range(1, PLANE)]
    return jnp.stack([pieces[0]] + back, 0)


def per_device(queries, keys, values, conv_keys, conv_values, out_weight, cotangent):
    tokens = queries.shape[0]
    heads = queries.shape[1] // FEAT
    width = heads * VDIM
    columns = cotangent.shape[1]
    groups = lax.axis_size("head")
    piece_rows = heads // PLANE * ROWS
    extra = max(0, 15 * heads // 4 - SPARE * heads // PLANE)
    message = (piece_rows + -(-extra // 16) * 16, VDIM)
    S = jax.ShapeDtypeStruct
    step = 2 * tokens * ROWS * VDIM * heads
    project_flops = 2 * tokens * width * columns
    dma = pltpu.SemaphoreType.DMA
    vmem = pltpu.VMEM
    slots = vmem((PLANE, piece_rows, VDIM), F32)

    with jax.named_scope("edge"):
        last_rows = pl.pallas_call(
            edge_kernel,
            out_shape=S((CONV - 1, keys.shape[1] + width), BF16),
            in_specs=[pl.BlockSpec(memory_space=pltpu.HBM)] * 2,
            out_specs=pl.BlockSpec(memory_space=vmem),
            scratch_shapes=[vmem((16, keys.shape[1]), BF16), vmem((16, width), BF16), dma((2,))],
            compiler_params=pltpu.CompilerParams(vmem_limit_bytes=VMEM_LIMIT),
        )(in_hbm(keys), in_hbm(values))
        slabs = lax.axis_size("ctx")
        before = lax.ppermute(last_rows, "ctx", [(i, (i + 1) % slabs) for i in range(slabs)])
    with jax.named_scope("query_features"):
        arrays = (keys, values, conv_keys, conv_values)
        qd, *near_by = call(
            query_kernel,
            (after(queries, last_rows), *arrays),
            [S((heads, ROWS, tokens), BF16)] + [S(x.shape, x.dtype) for x in arrays],
            1 << 20,
            far=range(5),
            scratch=[vmem(queries.shape, BF16), dma((5,))],
        )
    with jax.named_scope("key_features"):
        outs = [
            S((heads, ROWS, tokens), BF16),
            S((tokens, width), BF16),
            S(message, F32),
            S((PLANE, *message), BF16),
        ]
        ops = (*near_by[:2], before, *near_by[2:])
        kf, vc, own, send = call(key_kernel, ops, outs, step, scratch=[slots])
    with jax.named_scope("cotangent"):
        cots = [swapped(after(cotangent, last_rows), "head", j) for j in range(1, groups)]
    with jax.named_scope("prior_share"):
        got = [swapped(send[j], "ctx", j) for j in range(1, PLANE)]

        more = lax.axis_size("ctx") > 4 * PLANE
        half = piece_rows // 2
        count = 15 * heads // 4
        shapes = [(half + -(-count // 16) * 16, VDIM), (half, VDIM)]
        outs = [S(x, BF16) for x in shapes] + [S(x, F32) for x in shapes]
        body = functools.partial(share_kernel, piece_rows)
        sent = call(body, (own, *got), outs[: 4 if more else 2], 1 << 20)
        total = sent[2:] if more else (None, None)
        got = [own] + got

        def join(tail, total, received, more):
            outs = [S(total.shape, BF16), S(total.shape, F32)]
            body = functools.partial(join_kernel, tail)
            made = call(body, (total, *received[::-1]), outs[: 2 if more else 1], 1 << 20)
            return made if more else (made[0], None)

    with jax.named_scope("scores"):
        outs = [
            S((heads, tokens, tokens), BF16),
            S((heads, tokens), F32),
            S((tokens, width), F32),
        ]
        low, den, num = call(score_kernel, (qd, kf, vc), outs, 400 * step)
    with jax.named_scope("turned"):
        outs = [S((heads, tokens, ROWS), BF16)] * 2
        qt, kt = call(turn_kernel, (after(qd, den), kf), outs, 1 << 22)
    with jax.named_scope("prior_planes"):
        sent = lax.optimization_barrier((*sent[:2], qt))[:2]
        norm_join = functools.partial(join, (half, half + count))
        rest, strides = planes_ahead(total[1], sent[1], 1, functools.partial(join, None))
        moved, _ = planes_ahead(total[0], sent[0], 1, norm_join)
    with jax.named_scope("out_grad"):
        ops = (after(cotangent, *sent), *cots, out_weight)
        (out_grad,) = call(
            grad_kernel, ops, [S((tokens, width), F32)], groups * project_flops
        )
    with jax.named_scope("scaled_grad"):
        outs = [
            S((tokens, heads), F32),
            S((tokens, width), BF16),
            S((piece_rows, VDIM), F32),
            S((PLANE, piece_rows, VDIM), BF16),
        ]
        ops = (den, qd, out_grad, *got, *moved)
        body = functools.partial(scale_kernel, strides)
        inverse, scaled, own_later, send_later = call(body, ops, outs, step, scratch=[slots])
    with jax.named_scope("later_share"):
        got_later = [swapped(send_later[j], "ctx", j) for j in range(1, PLANE)]
    with jax.named_scope("prior_back"):
        body = functools.partial(piece_kernel, 1, strides)
        ops = (*got, *moved, after(rest[0], scaled), *rest[1:])
        (pieces,) = call(body, ops, [S((PLANE, piece_rows, VDIM), BF16)], 1 << 20)
        prior = handed_back(pieces)
    with jax.named_scope("later_planes"):
        plain_join = functools.partial(join, None)
        sent_later, total_later = plain_join(own_later, got_later, more)
        moved_later, strides = planes_ahead(total_later, sent_later, -1, plain_join)
    with jax.named_scope("attended"):
        outs = [S((tokens, width), BF16), S((tokens, columns), BF16)]
        ops = (qt, prior, after(num, sent_later), inverse, out_weight)
        attended, part = call(attend_kernel, ops, outs, step + project_flops)
        parts = [swapped(part, "head", 1)]
    with jax.named_scope("near"):
        ops = (low, after(scaled, sent_later))
        (near,) = call(near_kernel, ops, [S((tokens, width), F32)], 2 * step)
    with jax.named_scope("mixed"):
        for j in list(range(2, groups)) + [0]:
            outs = [S((tokens, columns), BF16 if j else F32)]
            body = functools.partial(mix_kernel, j)
            ops = (after(attended, sent_later), out_weight)
            (part,) = call(body, ops, outs, 2 * project_flops)
            if j:
                parts.append(swapped(part, "head", j))
    with jax.named_scope("later_back"):
        outs = [S((PLANE, piece_rows, VDIM), BF16)]
        body = functools.partial(piece_kernel, -1, strides)
        ops = (own_later, *got_later, after(moved_later[0], part), *moved_later[1:])
        (pieces,) = call(body, ops, outs, 1 << 20)
        later = [pieces[0]] + [swapped(pieces[j], "ctx", j) for j in range(1, PLANE)]
    with jax.named_scope("near"):
        ops = (low, after(scaled, sent_later))
        (near,) = call(near_kernel, ops, [S((tokens, width), F32)], 2 * step)
    with jax.named_scope("mixed"):
        for j in list(range(2, groups)) + [0]:
            outs = [S((tokens, columns), BF16 if j else F32)]
            body = functools.partial(mix_kernel, j)
            ops = (after(attended, sent_later), out_weight)
            (part,) = call(body, ops, outs, 2 * project_flops)
            if j:
                parts.append(swapped(part, "head", j))
    with jax.named_scope("later_back"):
        outs = [S((PLANE, piece_rows, VDIM), BF16)]
        body = functools.partial(piece_kernel, -1, strides)
        ops = (own_later, *got_later, after(moved_later[0], part, near), *moved_later[1:])
        (pieces,) = call(body, ops, outs, 1 << 20)
        later = handed_back(pieces)
    with jax.named_scope("far_grad"):
        block = (tokens, width // PLANE)
        outs = [S((2, *block), BF16)]
        (early,) = call(early_kernel, (kt, near, *later[:2]), outs, 16 * step)
        (value_grad,) = call(
            late_kernel,
            (kt, near, early, *later[2:]),
            [S((tokens, width), BF16)],
            16 * step,
            scratch=[vmem((PLANE - 2, *block), BF16), dma((PLANE,))],
            out_far=True,
        )
    with jax.named_scope("mixed_out"):
        (mixed_out,) = call(
            sum_kernel,
            (part, *[after(x, value_grad) for x in parts]),
            [S((tokens, columns), BF16)],
            1 << 20,
            scratch=[vmem((tokens, columns), BF16), dma((PLANE,))],
            out_far=True,
        )
    return mixed_out, value_grad


def solution(mesh):
    in_specs = (
        P("ctx", "head"),
        P("ctx", "head"),
        P("ctx", "head"),
        P(None, "head"),
        P(None, "head"),
        P("head", None),
        P("ctx", "head"),
    )
    out_specs = (P("ctx", "head"), P("ctx", "head"))
    return jax.shard_map(
        per_device, mesh=mesh, in_specs=in_specs, out_specs=out_specs, check_vma=False
    )
```

```python
import functools

import jax
import jax.numpy as jnp
from jax import lax
from jax.experimental import pallas as pl
from jax.experimental.pallas import tpu as pltpu
from jax.sharding import PartitionSpec as P

FEAT = 16
VDIM = 128
CONV = 3
ROWS = 160
VMEM_LIMIT = 14 * 1024 * 1024
SPARE = 7
PLANE = 4

F32 = jnp.float32
BF16 = jnp.bfloat16
TN = (((0,), (0,)), ((), ()))
NT = (((1,), (1,)), ((), ()))
NN = (((1,), (0,)), ((), ()))


def mm(a, b, dims):
    return lax.dot_general(a, b, dims, preferred_element_type=F32)


def call(body, operands, out_shape, flops, far=(), scratch=(), out_far=False):
    moved = sum(x.size * x.dtype.itemsize for x in operands)
    moved += sum(x.size * x.dtype.itemsize for x in out_shape)
    vmem = pl.BlockSpec(memory_space=pltpu.VMEM)
    hbm = pl.BlockSpec(memory_space=pltpu.HBM)
    return pl.pallas_call(
        body,
        out_shape=out_shape,
        in_specs=[hbm if i in far else vmem for i in range(len(operands))],
        out_specs=[hbm if out_far else vmem for _ in out_shape],
        scratch_shapes=list(scratch),
        compiler_params=pltpu.CompilerParams(vmem_limit_bytes=VMEM_LIMIT),
        cost_estimate=pl.CostEstimate(flops=flops, bytes_accessed=moved, transcendentals=0),
    )(*[in_hbm(x) if i in far else x for i, x in enumerate(operands)])


def in_hbm(x):
    return pltpu.with_memory_space_constraint(x, pltpu.HBM)


def fetch(source, target, sem):
    copy = pltpu.make_async_copy(source, target, sem)
    copy.start()
    return copy


def store_features(out_ref, rows_in, doubled):
    heads = rows_in.shape[0] // FEAT
    tokens = rows_in.shape[1]
    grid = rows_in.reshape(heads, FEAT, tokens) * FEAT ** (-0.25)
    twice = jnp.concatenate([grid, grid], 1)
    out_ref[:, 0:FEAT, :] = grid.astype(BF16)
    half = FEAT // 2
    for turn in range(half):
        square = grid * twice[:, turn : turn + FEAT, :] * 0.5**0.5
        if doubled and turn > 0:
            square = square * 2.0
        out_ref[:, FEAT * (turn + 1) : FEAT * (turn + 2), :] = square.astype(BF16)
    square = grid[:, :half, :] * grid[:, half:, :] * 0.5**0.5
    if doubled:
        square = square * 2.0
    first = lax.broadcasted_iota(jnp.int32, (heads, half, tokens), 1) == 0
    constant = jnp.where(first, 1.0, 0.0)
    out_ref[:, FEAT * (half + 1) :, :] = jnp.concatenate([square, constant], 1).astype(BF16)


def store_piece(rank, head, per_piece, state, own_ref, send_ref):
    slot = rank ^ (head // per_piece)
    at = (head % per_piece) * ROWS
    own_ref[slot, at : at + ROWS, :] = state
    send_ref[slot, at : at + ROWS, :] = state.astype(BF16)


def load_piece(rank, head, per_piece, ref):
    at = (head % per_piece) * ROWS
    return ref[lax.rem(PLANE - (rank ^ (head // per_piece)), PLANE), at : at + ROWS, :]


def edge_kernel(k_far, v_far, edge_ref, k_ref, v_ref, sems):
    tokens, width = k_far.shape
    deep = k_ref.shape[0]
    rows = pl.ds(tokens - deep, deep)
    copies = [fetch(k_far.at[rows], k_ref, sems.at[0]), fetch(v_far.at[rows], v_ref, sems.at[1])]
    last = deep - CONV + 1
    copies[0].wait()
    edge_ref[:, :width] = k_ref[...].astype(F32)[last:].astype(BF16)
    copies[1].wait()
    edge_ref[:, width:] = v_ref[...].astype(F32)[last:].astype(BF16)


def load_kernel(k_far, v_far, ck_far, cv_far, k_ref, v_ref, ck_ref, cv_ref, sems):
    pairs = ((k_far, k_ref), (v_far, v_ref), (ck_far, ck_ref), (cv_far, cv_ref))
    copies = [fetch(a, b, sems.at[i]) for i, (a, b) in enumerate(pairs)]
    for copy in copies:
        copy.wait()


def query_kernel(
    q_far,
    k_far,
    v_far,
    ck_far,
    cv_far,
    qd_ref,
    k_ref,
    v_ref,
    ck_ref,
    cv_ref,
    q_ref,
    sems,
):
    far = (q_far, k_far, v_far, ck_far, cv_far)
    near = (q_ref, k_ref, v_ref, ck_ref, cv_ref)
    copies = [fetch(a, b, sems.at[i]) for i, (a, b) in enumerate(zip(far, near))]
    copies[0].wait()
    store_features(qd_ref, q_ref[...].astype(F32).T, True)
    for copy in copies[1:]:
        copy.wait()


def columns_of(w_ref, distance):
    columns = w_ref.shape[1] // lax.axis_size("head")
    return pl.ds(pl.multiple_of((lax.axis_index("head") ^ distance) * columns, columns), columns)


def turn_kernel(qd_ref, kf_ref, qt_ref, kt_ref):
    for head in range(qd_ref.shape[0]):
        qt_ref[head] = qd_ref[head].T
        kt_ref[head] = kf_ref[head].T


def grad_kernel(*refs):
    *cots, w_ref, og_ref = refs
    total = None
    for j, cot_ref in enumerate(cots):
        term = mm(cot_ref[...], w_ref[:, columns_of(w_ref, j)], NT)
        total = term if total is None else total + term
    og_ref[...] = total


def masked(wanted, value):
    return jnp.where(wanted, value.astype(F32), 0.0)


def conv_rows(x, before, taps):
    x = x.astype(F32)
    row = lax.broadcasted_iota(jnp.int32, x.shape, 0)
    running = taps[0:1, :] * x
    for offset in range(1, CONV):
        moved = pltpu.roll(x, offset, 0)
        for at in range(offset):
            source = before[CONV - 1 - offset + at : CONV - offset + at, :]
            moved = jnp.where(row == at, source, moved)
        running = running + taps[offset : offset + 1, :] * moved
    return running


def norm_rows(norm):
    high = norm.astype(BF16).astype(F32)
    middle = (norm - high).astype(BF16).astype(F32)
    parts = jnp.concatenate([high, middle, norm - high - middle], 0)
    deep = parts.shape[0] // 4
    tail = [parts[i * deep : (i + 1) * deep, VDIM:] for i in range(4)]
    return jnp.concatenate([parts[:, :VDIM], jnp.concatenate(tail, 1)], 0)


def norm_values(lines):
    heads = lines.shape[0] * 4 // 15
    wide = ROWS - VDIM
    tail = [lines[3 * heads :, i * wide : (i + 1) * wide] for i in range(4)]
    parts = jnp.concatenate([lines[: 3 * heads], jnp.concatenate(tail, 0)], 1)
    return parts[:heads] + parts[heads : 2 * heads] + parts[2 * heads :]


def with_lines(state, lines, rows):
    pieces, used = [], 0
    for first in range(0, state.shape[0], ROWS):
        free = min(SPARE, lines.shape[0] - used)
        last = jnp.concatenate(
            [
                state[first + ROWS - SPARE - 1 : first + ROWS - SPARE],
                lines[used : used + free],
                jnp.zeros((SPARE - free, VDIM), F32),
            ][: 3 if free < SPARE else 2],
            0,
        )
        pieces += [state[first : first + ROWS - SPARE - 1], last]
        used += free
    left = rows - state.shape[0]
    blank = left - (lines.shape[0] - used)
    if left > 0:
        pieces.append(lines[used:])
        if blank > 0:
            pieces.append(jnp.zeros((blank, VDIM), F32))
    return jnp.concatenate(pieces, 0)


def lines_in(state, piece_rows):
    count = 15 * (piece_rows // ROWS * PLANE) // 4
    found, used = [], 0
    for first in range(0, piece_rows, ROWS):
        free = min(SPARE, count - used)
        found.append(state[first + ROWS - SPARE - 1 : first + ROWS, :][1 : 1 + free].astype(F32))
        used += free
    rest = state[piece_rows:, :][: count - used].astype(F32)
    return jnp.concatenate(found + [rest], 0)


def key_kernel(
    k_ref,
    v_ref,
    before_ref,
    ck_ref,
    cv_ref,
    kf_ref,
    vc_ref,
    own_ref,
    send_ref,
    slots,
):
    rank = lax.rem(lax.axis_index("ctx"), PLANE)
    heads = kf_ref.shape[0]
    per_piece = heads // PLANE
    width = k_ref.shape[1]
    before = masked(lax.axis_index("ctx") > 0, before_ref[...])
    key_conv = conv_rows(k_ref[...], before[:, :width], ck_ref[...])
    store_features(kf_ref, key_conv.T, False)
    ones = jnp.ones((heads, k_ref.shape[0]), BF16)
    row = lax.broadcasted_iota(jnp.int32, (heads, ROWS), 0)
    norm = jnp.zeros((heads, ROWS), F32)
    for head in range(heads):
        at = head * VDIM
        value = conv_rows(
            v_ref[:, at : at + VDIM],
            before[:, width + at : width + at + VDIM],
            cv_ref[:, at : at + VDIM],
        ).astype(BF16)
        vc_ref[:, at : at + VDIM] = value
        feat = kf_ref[head]
        norm = jnp.where(row == head, mm(ones, feat, NT), norm)
        first = (head % per_piece) * ROWS
        slots[rank ^ (head // per_piece), first : first + ROWS, :] = mm(feat, value, NN)
    lines = norm_rows(norm)
    for slot in range(PLANE):
        piece = with_lines(slots[slot], lines, own_ref.shape[0])
        if slot == 0:
            own_ref[...] = piece
        else:
            send_ref[slot] = piece.astype(BF16)


def share_kernel(piece_rows, own_ref, *refs):
    got_refs, out_refs = refs[: PLANE - 1], refs[PLANE - 1 :]
    total = own_ref[...]
    for got_ref in got_refs:
        total = total + got_ref[...].astype(F32)
    half = piece_rows // 2
    lines = norm_rows(norm_values(lines_in(total, piece_rows)))
    parts = (with_tail(total[:half], lines, out_refs[0].shape[0]), total[half:piece_rows])
    for ref, part in zip(out_refs, parts):
        ref[...] = part.astype(BF16)
    for ref, part in zip(out_refs[2:], parts):
        ref[...] = part


def with_tail(state, lines, rows):
    blank = jnp.zeros((rows - state.shape[0] - lines.shape[0], VDIM), F32)
    return jnp.concatenate([state, lines, blank], 0)


def join_kernel(tail, total_ref, *refs):
    out_at = -1 if refs[-1].dtype == BF16 else -2
    total = total_ref[...]
    for got_ref in refs[:out_at]:
        total = total + got_ref[...].astype(F32)
    if tail is not None:
        lines = norm_rows(norm_values(total[tail[0] : tail[1]]))
        total = with_tail(total[: tail[0]], lines, total.shape[0])
    refs[out_at][...] = total.astype(BF16)
    if out_at == -2:
        refs[-1][...] = total


def is_ahead(sign, other, here):
    return other < here if sign > 0 else other > here


def before_plane(sign, strides, refs, rows):
    total = 0.0
    for ref, (stride, distance) in zip(refs, strides):
        if distance:
            group = lax.div(lax.axis_index("ctx"), PLANE * stride)
            total = total + masked(is_ahead(sign, group ^ distance, group), ref[rows, :])
        else:
            total = total + ref[rows, :].astype(F32)
    return total


def piece_kernel(sign, strides, *refs):
    got_refs, moved_refs, pieces_ref = refs[:PLANE][::-1], refs[PLANE:-1], refs[-1]
    rank = lax.rem(lax.axis_index("ctx"), PLANE)
    count = len(strides)
    parts = len(moved_refs) // count
    deep = pieces_ref.shape[1] // parts
    for part in range(parts):
        refs = moved_refs[part * count : (part + 1) * count]
        before = before_plane(sign, strides, refs, pl.ds(0, deep))
        rows = pl.ds(part * deep, deep)
        for slot in range(PLANE):
            total = before
            for i in range(PLANE):
                if i != slot:
                    ahead = is_ahead(sign, rank ^ i, rank ^ slot)
                    total = total + masked(ahead, got_refs[i][rows, :])
            pieces_ref[slot, rows, :] = total.astype(BF16)


def score_kernel(qd_ref, kf_ref, vc_ref, low_ref, den_ref, num_ref):
    heads = kf_ref.shape[0]
    tokens = kf_ref.shape[2]
    key_at = lax.broadcasted_iota(jnp.int32, (tokens, tokens), 0)
    query_at = lax.broadcasted_iota(jnp.int32, (tokens, tokens), 1)
    causal = key_at <= query_at
    for head in range(heads):
        scores = jnp.where(causal, mm(kf_ref[head], qd_ref[head], TN), 0.0)
        den_ref[head : head + 1, :] = jnp.sum(scores, 0, keepdims=True)
        low = scores.astype(BF16)
        low_ref[head] = low
        at = head * VDIM
        num_ref[:, at : at + VDIM] = mm(low, vc_ref[:, at : at + VDIM], TN)


def scale_kernel(strides, den_ref, qd_ref, og_ref, *refs):
    *refs, inv_ref, sg_ref, own_ref, send_ref, slots = refs
    got_refs, moved_refs = refs[:PLANE][::-1], refs[PLANE:]
    rank = lax.rem(lax.axis_index("ctx"), PLANE)
    heads = qd_ref.shape[0]
    per_piece = heads // PLANE
    piece_rows = per_piece * ROWS
    lines = before_plane(1, strides, moved_refs, pl.ds(piece_rows // 2, 15 * heads // 4))
    for i in range(1, PLANE):
        here = lines_in(got_refs[i], piece_rows)
        lines = lines + masked(is_ahead(1, rank ^ i, rank), here)
    norm = norm_values(lines)
    high = norm.astype(BF16).astype(F32)
    middle = (norm - high).astype(BF16).astype(F32)
    rest = norm - high - middle
    parts = jnp.concatenate([high, middle, rest, jnp.zeros_like(rest)], 0).astype(BF16)
    lines = []
    for head in range(heads):
        terms = mm(parts, qd_ref[head], NN)
        line = den_ref[head : head + 1, :] + terms[head : head + 1, :]
        line = line + terms[heads + head : heads + head + 1, :]
        lines.append(line + terms[2 * heads + head : 2 * heads + head + 1, :])
    inverse = (1.0 / jnp.concatenate(lines, 0)).T
    inv_ref[...] = inverse
    for head in range(heads):
        at = head * VDIM
        scaled = (og_ref[:, at : at + VDIM] * inverse[:, head : head + 1]).astype(BF16)
        sg_ref[:, at : at + VDIM] = scaled
        store_piece(rank, head, per_piece, mm(qd_ref[head], scaled, NN), slots, send_ref)
    own_ref[...] = slots[0]


def near_kernel(low_ref, sg_ref, vg_ref):
    for head in range(low_ref.shape[0]):
        at = head * VDIM
        vg_ref[:, at : at + VDIM] = mm(low_ref[head], sg_ref[:, at : at + VDIM], NN)


def attend_kernel(qt_ref, prior_ref, num_ref, inv_ref, w_ref, att_ref, part_ref):
    rank = lax.rem(lax.axis_index("ctx"), PLANE)
    heads = qt_ref.shape[0]
    per_piece = heads // PLANE
    for head in range(heads):
        at = head * VDIM
        prior = load_piece(rank, head, per_piece, prior_ref)
        total = num_ref[:, at : at + VDIM] + mm(qt_ref[head], prior, NN)
        att_ref[:, at : at + VDIM] = (total * inv_ref[:, head : head + 1]).astype(BF16)
    part_ref[...] = mm(att_ref[...], w_ref[:, columns_of(w_ref, 1)], NN).astype(BF16)


def mix_kernel(distance, att_ref, w_ref, part_ref):
    weight = w_ref[:, columns_of(w_ref, distance)]
    part_ref[...] = mm(att_ref[...], weight, NN).astype(part_ref.dtype)


def far_block(distance, kt_ref, near_ref, later_ref):
    per_piece = kt_ref.shape[0] // PLANE
    first = (lax.rem(lax.axis_index("ctx"), PLANE) ^ distance) * per_piece
    blocks = []
    for i in range(per_piece):
        columns = pl.ds(pl.multiple_of((first + i) * VDIM, VDIM), VDIM)
        later = later_ref[i * ROWS : (i + 1) * ROWS, :]
        total = near_ref[:, columns] + mm(kt_ref[first + i], later, NN)
        blocks.append(total.astype(BF16))
    return jnp.concatenate(blocks, 1)


def early_kernel(kt_ref, near_ref, *refs):
    *later_refs, block_ref = refs
    for distance, later_ref in enumerate(later_refs):
        block_ref[distance] = far_block(distance, kt_ref, near_ref, later_ref)


def late_kernel(kt_ref, near_ref, early_ref, *refs):
    *later_refs, vg_far, block_ref, sems = refs
    early, columns = early_ref.shape[0], early_ref.shape[2]
    rank = lax.rem(lax.axis_index("ctx"), PLANE)

    def send(distance, ref):
        start = pl.multiple_of((rank ^ distance) * columns, columns)
        return fetch(ref, vg_far.at[:, pl.ds(start, columns)], sems.at[distance])

    copies = [send(distance, early_ref.at[distance]) for distance in range(early)]
    for i, later_ref in enumerate(later_refs):
        block_ref[i] = far_block(early + i, kt_ref, near_ref, later_ref)
        copies.append(send(early + i, block_ref.at[i]))
    for copy in copies:
        copy.wait()


def sum_kernel(part_ref, *refs):
    *other_refs, mixed_far, mixed_ref, sems = refs
    copies = []
    deep = part_ref.shape[0] // PLANE
    for step in range(PLANE):
        rows = pl.ds(step * deep, deep)
        total = part_ref[rows, :]
        for other_ref in other_refs:
            total = total + other_ref[rows, :].astype(F32)
        mixed_ref[rows, :] = total.astype(BF16)
        copies.append(fetch(mixed_ref.at[rows], mixed_far.at[rows], sems.at[step]))
    for copy in copies:
        copy.wait()


def shifted(x, axis, by):
    peers = lax.axis_size(axis)
    pairs = [(i, i + by) for i in range(peers) if 0 <= i + by < peers]
    return lax.ppermute(x, axis, pairs)


def after(x, *others):
    return lax.optimization_barrier((x, *others))[0]


def planes_ahead(total, sent, sign, join, last=None):
    planes = lax.axis_size("ctx") // PLANE
    received, strides = [], []
    stride = 1
    while stride < planes:
        if (planes // stride) % 4 == 0:
            near = sent if last is None else after(sent, last)
            moved = [swapped(near if j == 1 else sent, "ctx", j, stride * PLANE) for j in range(1, 4)]
            strides += [(stride, j) for j in range(1, 4)]
            stride = stride * 4
        else:
            moved = [shifted(sent, "ctx", sign * stride * PLANE)]
            strides.append((stride, 0))
            stride = stride * 2
        received += moved
        if stride < planes:
            sent, total = join(total, moved, stride * 2 < planes)
    return received, strides


def swapped(x, axis, distance, stride=1):
    peers = lax.axis_size(axis)
    pairs = [(i, (i // stride ^ distance) * stride + i % stride) for i in range(peers)]
    return lax.ppermute(x, axis, pairs)


def handed_back(pieces):
    return [pieces[0]] + [swapped(pieces[j], "ctx", j) for j in range(1, PLANE)]


def per_device(queries, keys, values, conv_keys, conv_values, out_weight, cotangent):
    tokens = queries.shape[0]
    heads = queries.shape[1] // FEAT
    width = heads * VDIM
    columns = cotangent.shape[1]
    groups = lax.axis_size("head")
    piece_rows = heads // PLANE * ROWS
    extra = max(0, 15 * heads // 4 - SPARE * heads // PLANE)
    message = (piece_rows + -(-extra // 16) * 16, VDIM)
    S = jax.ShapeDtypeStruct
    step = 2 * tokens * ROWS * VDIM * heads
    project_flops = 2 * tokens * width * columns
    dma = pltpu.SemaphoreType.DMA
    vmem = pltpu.VMEM
    slots = vmem((PLANE, piece_rows, VDIM), F32)

    with jax.named_scope("edge"):
        last_rows = pl.pallas_call(
            edge_kernel,
            out_shape=S((CONV - 1, keys.shape[1] + width), BF16),
            in_specs=[pl.BlockSpec(memory_space=pltpu.HBM)] * 2,
            out_specs=pl.BlockSpec(memory_space=vmem),
            scratch_shapes=[vmem((16, keys.shape[1]), BF16), vmem((16, width), BF16), dma((2,))],
            compiler_params=pltpu.CompilerParams(vmem_limit_bytes=VMEM_LIMIT),
        )(in_hbm(keys), in_hbm(values))
        slabs = lax.axis_size("ctx")
        before = lax.ppermute(last_rows, "ctx", [(i, (i + 1) % slabs) for i in range(slabs)])
    with jax.named_scope("query_features"):
        arrays = (keys, values, conv_keys, conv_values)
        qd, *near_by = call(
            query_kernel,
            (after(queries, last_rows), *arrays),
            [S((heads, ROWS, tokens), BF16)] + [S(x.shape, x.dtype) for x in arrays],
            1 << 20,
            far=range(5),
            scratch=[vmem(queries.shape, BF16), dma((5,))],
        )
    with jax.named_scope("key_features"):
        outs = [
            S((heads, ROWS, tokens), BF16),
            S((tokens, width), BF16),
            S(message, F32),
            S((PLANE, *message), BF16),
        ]
        ops = (*near_by[:2], before, *near_by[2:])
        kf, vc, own, send = call(key_kernel, ops, outs, step, scratch=[slots])
    with jax.named_scope("cotangent"):
        cots = [swapped(after(cotangent, last_rows), "head", j) for j in range(1, groups)]
    with jax.named_scope("prior_share"):
        got = [swapped(send[j], "ctx", j) for j in range(1, PLANE)]

        more = lax.axis_size("ctx") > 4 * PLANE
        half = piece_rows // 2
        count = 15 * heads // 4
        shapes = [(half + -(-count // 16) * 16, VDIM), (half, VDIM)]
        outs = [S(x, BF16) for x in shapes] + [S(x, F32) for x in shapes]
        body = functools.partial(share_kernel, piece_rows)
        sent = call(body, (own, *got[::-1]), outs[: 4 if more else 2], 1 << 20)
        total = sent[2:] if more else (None, None)
        got = [own] + got

        def join(tail, total, received, more):
            outs = [S(total.shape, BF16), S(total.shape, F32)]
            body = functools.partial(join_kernel, tail)
            made = call(body, (total, *received[::-1]), outs[: 2 if more else 1], 1 << 20)
            return made if more else (made[0], None)

    with jax.named_scope("scores"):
        outs = [
            S((heads, tokens, tokens), BF16),
            S((heads, tokens), F32),
            S((tokens, width), F32),
        ]
        low, den, num = call(score_kernel, (qd, kf, vc), outs, 400 * step)
    with jax.named_scope("turned"):
        outs = [S((heads, tokens, ROWS), BF16)] * 2
        qt, kt = call(turn_kernel, (after(qd, den), kf), outs, 1 << 22)
    with jax.named_scope("prior_planes"):
        sent = lax.optimization_barrier((*sent[:2], qt))[:2]
        norm_join = functools.partial(join, (half, half + count))
        rest, strides = planes_ahead(total[1], sent[1], 1, functools.partial(join, None))
        moved, _ = planes_ahead(total[0], sent[0], 1, norm_join)
    with jax.named_scope("out_grad"):
        ops = (after(cotangent, moved[0]), *cots, out_weight)
        (out_grad,) = call(
            grad_kernel, ops, [S((tokens, width), F32)], groups * project_flops
        )
    with jax.named_scope("scaled_grad"):
        outs = [
            S((tokens, heads), F32),
            S((tokens, width), BF16),
            S((piece_rows, VDIM), F32),
            S((PLANE, piece_rows, VDIM), BF16),
        ]
        ops = (den, qd, out_grad, *got[::-1], *moved)
        body = functools.partial(scale_kernel, strides)
        inverse, scaled, own_later, send_later = call(body, ops, outs, step, scratch=[slots])
    with jax.named_scope("later_share"):
        got_later = [swapped(send_later[j], "ctx", j) for j in range(1, PLANE)]
    with jax.named_scope("prior_back"):
        body = functools.partial(piece_kernel, 1, strides)
        ops = (*got[::-1], *moved, after(rest[0], scaled), *rest[1:])
        (pieces,) = call(body, ops, [S((PLANE, piece_rows, VDIM), BF16)], 1 << 20)
        prior = handed_back(pieces)
        prior = jnp.stack([prior[0]] + prior[:0:-1], 0)
    with jax.named_scope("later_planes"):
        plain_join = functools.partial(join, None)
        sent_later, total_later = plain_join(own_later, got_later, more)
    with jax.named_scope("attended"):
        outs = [S((tokens, width), BF16), S((tokens, columns), BF16)]
        ops = (qt, prior, after(num, sent_later), inverse, out_weight)
        attended, part = call(attend_kernel, ops, outs, step + project_flops)
        parts = [swapped(part, "head", 1)]
    with jax.named_scope("later_planes"):
        moved_later, strides = planes_ahead(total_later, sent_later, -1, plain_join, part)
    with jax.named_scope("near"):
        ops = (low, after(scaled, sent_later))
        (near,) = call(near_kernel, ops, [S((tokens, width), F32)], 2 * step)
    with jax.named_scope("mixed"):
        for j in list(range(2, groups)) + [0]:
            outs = [S((tokens, columns), BF16 if j else F32)]
            body = functools.partial(mix_kernel, j)
            ops = (after(attended, sent_later), out_weight)
            (part,) = call(body, ops, outs, 2 * project_flops)
            if j:
                parts.append(swapped(part, "head", j))
    with jax.named_scope("later_back"):
        outs = [S((PLANE, piece_rows, VDIM), BF16)]
        body = functools.partial(piece_kernel, -1, strides)
        ops = (*got_later[::-1], own_later, after(moved_later[0], part, near), *moved_later[1:])
        (pieces,) = call(body, ops, outs, 1 << 20)
        later = handed_back(pieces)
    with jax.named_scope("far_grad"):
        block = (tokens, width // PLANE)
        outs = [S((2, *block), BF16)]
        (early,) = call(early_kernel, (kt, near, *later[:2]), outs, 16 * step)
        (value_grad,) = call(
            late_kernel,
            (kt, near, early, *later[2:]),
            [S((tokens, width), BF16)],
            16 * step,
            scratch=[vmem((PLANE - 2, *block), BF16), dma((PLANE,))],
            out_far=True,
        )
    with jax.named_scope("mixed_out"):
        (mixed_out,) = call(
            sum_kernel,
            (part, *[after(x, value_grad) for x in parts]),
            [S((tokens, columns), BF16)],
            1 << 20,
            scratch=[vmem((tokens, columns), BF16), dma((PLANE,))],
            out_far=True,
        )
    return mixed_out, value_grad


def solution(mesh):
    in_specs = (
        P("ctx", "head"),
        P("ctx", "head"),
        P("ctx", "head"),
        P(None, "head"),
        P(None, "head"),
        P("head", None),
        P("ctx", "head"),
    )
    out_specs = (P("ctx", "head"), P("ctx", "head"))
    return jax.shard_map(
        per_device, mesh=mesh, in_specs=in_specs, out_specs=out_specs, check_vma=False
    )
```

```python
import functools

import jax
import jax.numpy as jnp
from jax import lax
from jax.experimental import pallas as pl
from jax.experimental.pallas import tpu as pltpu
from jax.sharding import PartitionSpec as P

FEAT = 16
VDIM = 128
CONV = 3
ROWS = 160
VMEM_LIMIT = 14 * 1024 * 1024
SPARE = 7
PLANE = 4

F32 = jnp.float32
BF16 = jnp.bfloat16
TN = (((0,), (0,)), ((), ()))
NT = (((1,), (1,)), ((), ()))
NN = (((1,), (0,)), ((), ()))


def mm(a, b, dims):
    return lax.dot_general(a, b, dims, preferred_element_type=F32)


def call(body, operands, out_shape, flops, far=(), scratch=(), out_far=False):
    moved = sum(x.size * x.dtype.itemsize for x in operands)
    moved += sum(x.size * x.dtype.itemsize for x in out_shape)
    vmem = pl.BlockSpec(memory_space=pltpu.VMEM)
    hbm = pl.BlockSpec(memory_space=pltpu.HBM)
    return pl.pallas_call(
        body,
        out_shape=out_shape,
        in_specs=[hbm if i in far else vmem for i in range(len(operands))],
        out_specs=[hbm if out_far else vmem for _ in out_shape],
        scratch_shapes=list(scratch),
        compiler_params=pltpu.CompilerParams(vmem_limit_bytes=VMEM_LIMIT),
        cost_estimate=pl.CostEstimate(flops=flops, bytes_accessed=moved, transcendentals=0),
    )(*[in_hbm(x) if i in far else x for i, x in enumerate(operands)])


def in_hbm(x):
    return pltpu.with_memory_space_constraint(x, pltpu.HBM)


def fetch(source, target, sem):
    copy = pltpu.make_async_copy(source, target, sem)
    copy.start()
    return copy


def store_features(out_ref, rows_in, doubled):
    heads = rows_in.shape[0] // FEAT
    tokens = rows_in.shape[1]
    grid = rows_in.reshape(heads, FEAT, tokens) * FEAT ** (-0.25)
    twice = jnp.concatenate([grid, grid], 1)
    out_ref[:, 0:FEAT, :] = grid.astype(BF16)
    half = FEAT // 2
    for turn in range(half):
        square = grid * twice[:, turn : turn + FEAT, :] * 0.5**0.5
        if doubled and turn > 0:
            square = square * 2.0
        out_ref[:, FEAT * (turn + 1) : FEAT * (turn + 2), :] = square.astype(BF16)
    square = grid[:, :half, :] * grid[:, half:, :] * 0.5**0.5
    if doubled:
        square = square * 2.0
    first = lax.broadcasted_iota(jnp.int32, (heads, half, tokens), 1) == 0
    constant = jnp.where(first, 1.0, 0.0)
    out_ref[:, FEAT * (half + 1) :, :] = jnp.concatenate([square, constant], 1).astype(BF16)


def store_piece(rank, head, per_piece, state, own_ref, send_ref):
    slot = rank ^ (head // per_piece)
    at = (head % per_piece) * ROWS
    own_ref[slot, at : at + ROWS, :] = state
    send_ref[slot, at : at + ROWS, :] = state.astype(BF16)


def load_piece(rank, head, per_piece, ref):
    at = (head % per_piece) * ROWS
    return ref[lax.rem(PLANE - (rank ^ (head // per_piece)), PLANE), at : at + ROWS, :]


def edge_kernel(k_far, v_far, edge_ref, k_ref, v_ref, sems):
    tokens, width = k_far.shape
    deep = k_ref.shape[0]
    rows = pl.ds(tokens - deep, deep)
    copies = [fetch(k_far.at[rows], k_ref, sems.at[0]), fetch(v_far.at[rows], v_ref, sems.at[1])]
    last = deep - CONV + 1
    copies[0].wait()
    edge_ref[:, :width] = k_ref[...].astype(F32)[last:].astype(BF16)
    copies[1].wait()
    edge_ref[:, width:] = v_ref[...].astype(F32)[last:].astype(BF16)


def load_kernel(k_far, v_far, ck_far, cv_far, k_ref, v_ref, ck_ref, cv_ref, sems):
    pairs = ((k_far, k_ref), (v_far, v_ref), (ck_far, ck_ref), (cv_far, cv_ref))
    copies = [fetch(a, b, sems.at[i]) for i, (a, b) in enumerate(pairs)]
    for copy in copies:
        copy.wait()


def query_kernel(
    q_far,
    k_far,
    v_far,
    ck_far,
    cv_far,
    qd_ref,
    k_ref,
    v_ref,
    ck_ref,
    cv_ref,
    q_ref,
    sems,
):
    far = (q_far, k_far, v_far, ck_far, cv_far)
    near = (q_ref, k_ref, v_ref, ck_ref, cv_ref)
    copies = [fetch(a, b, sems.at[i]) for i, (a, b) in enumerate(zip(far, near))]
    copies[0].wait()
    store_features(qd_ref, q_ref[...].astype(F32).T, True)
    for copy in copies[1:]:
        copy.wait()


def columns_of(w_ref, distance):
    columns = w_ref.shape[1] // lax.axis_size("head")
    return pl.ds(pl.multiple_of((lax.axis_index("head") ^ distance) * columns, columns), columns)


def turn_kernel(qd_ref, kf_ref, qt_ref, kt_ref):
    for head in range(qd_ref.shape[0]):
        qt_ref[head] = qd_ref[head].T
        kt_ref[head] = kf_ref[head].T


def own_grad_kernel(cot_ref, w_ref, og_ref):
    og_ref[...] = mm(cot_ref[...], w_ref[:, columns_of(w_ref, 0)], NT)


def grad_kernel(before_ref, *refs):
    *cots, w_ref, og_ref = refs
    total = before_ref[...]
    for j, cot_ref in enumerate(cots):
        total = total + mm(cot_ref[...], w_ref[:, columns_of(w_ref, j + 1)], NT)
    og_ref[...] = total


def masked(wanted, value):
    return jnp.where(wanted, value.astype(F32), 0.0)


def conv_rows(x, before, taps):
    x = x.astype(F32)
    row = lax.broadcasted_iota(jnp.int32, x.shape, 0)
    running = taps[0:1, :] * x
    for offset in range(1, CONV):
        moved = pltpu.roll(x, offset, 0)
        for at in range(offset):
            source = before[CONV - 1 - offset + at : CONV - offset + at, :]
            moved = jnp.where(row == at, source, moved)
        running = running + taps[offset : offset + 1, :] * moved
    return running


def norm_rows(norm):
    high = norm.astype(BF16).astype(F32)
    middle = (norm - high).astype(BF16).astype(F32)
    parts = jnp.concatenate([high, middle, norm - high - middle], 0)
    deep = parts.shape[0] // 4
    tail = [parts[i * deep : (i + 1) * deep, VDIM:] for i in range(4)]
    return jnp.concatenate([parts[:, :VDIM], jnp.concatenate(tail, 1)], 0)


def norm_values(lines):
    heads = lines.shape[0] * 4 // 15
    wide = ROWS - VDIM
    tail = [lines[3 * heads :, i * wide : (i + 1) * wide] for i in range(4)]
    parts = jnp.concatenate([lines[: 3 * heads], jnp.concatenate(tail, 0)], 1)
    return parts[:heads] + parts[heads : 2 * heads] + parts[2 * heads :]


def with_lines(state, lines, rows):
    pieces, used = [], 0
    for first in range(0, state.shape[0], ROWS):
        free = min(SPARE, lines.shape[0] - used)
        last = jnp.concatenate(
            [
                state[first + ROWS - SPARE - 1 : first + ROWS - SPARE],
                lines[used : used + free],
                jnp.zeros((SPARE - free, VDIM), F32),
            ][: 3 if free < SPARE else 2],
            0,
        )
        pieces += [state[first : first + ROWS - SPARE - 1], last]
        used += free
    left = rows - state.shape[0]
    blank = left - (lines.shape[0] - used)
    if left > 0:
        pieces.append(lines[used:])
        if blank > 0:
            pieces.append(jnp.zeros((blank, VDIM), F32))
    return jnp.concatenate(pieces, 0)


def lines_in(state, piece_rows):
    count = 15 * (piece_rows // ROWS * PLANE) // 4
    found, used = [], 0
    for first in range(0, piece_rows, ROWS):
        free = min(SPARE, count - used)
        tile = state[first + ROWS - 16 : first + ROWS, :].astype(F32)
        found.append(tile[16 - SPARE : 16 - SPARE + free])
        used += free
    rest = state[piece_rows:, :].astype(F32)
    return jnp.concatenate(found + [rest[: count - used]], 0)


def key_kernel(
    k_ref,
    v_ref,
    before_ref,
    ck_ref,
    cv_ref,
    kf_ref,
    vc_ref,
    own_ref,
    send_ref,
    slots,
):
    rank = lax.rem(lax.axis_index("ctx"), PLANE)
    heads = kf_ref.shape[0]
    per_piece = heads // PLANE
    width = k_ref.shape[1]
    before = masked(lax.axis_index("ctx") > 0, before_ref[...])
    key_conv = conv_rows(k_ref[...], before[:, :width], ck_ref[...])
    store_features(kf_ref, key_conv.T, False)
    ones = jnp.ones((heads, k_ref.shape[0]), BF16)
    row = lax.broadcasted_iota(jnp.int32, (heads, ROWS), 0)
    norm = jnp.zeros((heads, ROWS), F32)
    for head in range(heads):
        at = head * VDIM
        value = conv_rows(
            v_ref[:, at : at + VDIM],
            before[:, width + at : width + at + VDIM],
            cv_ref[:, at : at + VDIM],
        ).astype(BF16)
        vc_ref[:, at : at + VDIM] = value
        feat = kf_ref[head]
        norm = jnp.where(row == head, mm(ones, feat, NT), norm)
        first = (head % per_piece) * ROWS
        slots[rank ^ (head // per_piece), first : first + ROWS, :] = mm(feat, value, NN)
    lines = norm_rows(norm)
    for slot in range(PLANE):
        piece = with_lines(slots[slot], lines, own_ref.shape[0])
        if slot == 0:
            own_ref[...] = piece
        else:
            send_ref[slot] = piece.astype(BF16)


def share_kernel(piece_rows, own_ref, *refs):
    got_refs, out_refs = refs[: PLANE - 1], refs[PLANE - 1 :]
    total = own_ref[...]
    for got_ref in got_refs:
        total = total + got_ref[...].astype(F32)
    half = piece_rows // 2
    lines = norm_rows(norm_values(lines_in(total, piece_rows)))
    parts = (with_tail(total[:half], lines, out_refs[0].shape[0]), total[half:piece_rows])
    for ref, part in zip(out_refs, parts):
        ref[...] = part.astype(BF16)
    for ref, part in zip(out_refs[2:], parts):
        ref[...] = part


def with_tail(state, lines, rows):
    blank = jnp.zeros((rows - state.shape[0] - lines.shape[0], VDIM), F32)
    return jnp.concatenate([state, lines, blank], 0)


def join_kernel(tail, total_ref, *refs):
    out_at = -1 if refs[-1].dtype == BF16 else -2
    total = total_ref[...]
    for got_ref in refs[:out_at]:
        total = total + got_ref[...].astype(F32)
    if tail is not None:
        lines = norm_rows(norm_values(total[tail[0] : tail[1]]))
        total = with_tail(total[: tail[0]], lines, total.shape[0])
    refs[out_at][...] = total.astype(BF16)
    if out_at == -2:
        refs[-1][...] = total


def is_ahead(sign, other, here):
    return other < here if sign > 0 else other > here


def before_plane(sign, strides, refs, rows):
    total = 0.0
    for ref, (stride, distance) in zip(refs, strides):
        if distance:
            group = lax.div(lax.axis_index("ctx"), PLANE * stride)
            total = total + masked(is_ahead(sign, group ^ distance, group), ref[rows, :])
        else:
            total = total + ref[rows, :].astype(F32)
    return total


def piece_kernel(sign, strides, *refs):
    got_refs, moved_refs, pieces_ref = refs[:PLANE][::-1], refs[PLANE:-1], refs[-1]
    rank = lax.rem(lax.axis_index("ctx"), PLANE)
    count = len(strides)
    parts = len(moved_refs) // count
    deep = pieces_ref.shape[1] // parts
    for part in range(parts):
        refs = moved_refs[part * count : (part + 1) * count]
        before = before_plane(sign, strides, refs, pl.ds(0, deep))
        rows = pl.ds(part * deep, deep)
        for slot in range(PLANE):
            total = before
            for i in range(PLANE):
                if i != slot:
                    ahead = is_ahead(sign, rank ^ i, rank ^ slot)
                    total = total + masked(ahead, got_refs[i][rows, :])
            pieces_ref[slot, rows, :] = total.astype(BF16)


def score_kernel(qd_ref, kf_ref, vc_ref, low_ref, den_ref, num_ref):
    heads = kf_ref.shape[0]
    tokens = kf_ref.shape[2]
    key_at = lax.broadcasted_iota(jnp.int32, (tokens, tokens), 0)
    query_at = lax.broadcasted_iota(jnp.int32, (tokens, tokens), 1)
    causal = key_at <= query_at
    for head in range(heads):
        scores = jnp.where(causal, mm(kf_ref[head], qd_ref[head], TN), 0.0)
        den_ref[head : head + 1, :] = jnp.sum(scores, 0, keepdims=True)
        low = scores.astype(BF16)
        low_ref[head] = low
        at = head * VDIM
        num_ref[:, at : at + VDIM] = mm(low, vc_ref[:, at : at + VDIM], TN)


def scale_kernel(strides, den_ref, qd_ref, og_ref, *refs):
    *refs, inv_ref, sg_ref, own_ref, send_ref, slots = refs
    got_refs, moved_refs = refs[:PLANE][::-1], refs[PLANE:]
    rank = lax.rem(lax.axis_index("ctx"), PLANE)
    heads = qd_ref.shape[0]
    per_piece = heads // PLANE
    piece_rows = per_piece * ROWS
    half = piece_rows // 2
    lines = before_plane(1, strides, moved_refs, pl.ds(half, moved_refs[0].shape[0] - half))
    lines = lines[: 15 * heads // 4]
    for i in range(1, PLANE):
        here = lines_in(got_refs[i], piece_rows)
        lines = lines + masked(is_ahead(1, rank ^ i, rank), here)
    norm = norm_values(lines)
    high = norm.astype(BF16).astype(F32)
    middle = (norm - high).astype(BF16).astype(F32)
    rest = norm - high - middle
    parts = jnp.concatenate([high, middle, rest, jnp.zeros_like(rest)], 0).astype(BF16)
    lines = []
    for head in range(heads):
        terms = mm(parts, qd_ref[head], NN)
        line = den_ref[head : head + 1, :] + terms[head : head + 1, :]
        line = line + terms[heads + head : heads + head + 1, :]
        lines.append(line + terms[2 * heads + head : 2 * heads + head + 1, :])
    inverse = (1.0 / jnp.concatenate(lines, 0)).T
    inv_ref[...] = inverse
    for head in range(heads):
        at = head * VDIM
        scaled = (og_ref[:, at : at + VDIM] * inverse[:, head : head + 1]).astype(BF16)
        sg_ref[:, at : at + VDIM] = scaled
        store_piece(rank, head, per_piece, mm(qd_ref[head], scaled, NN), slots, send_ref)
    own_ref[...] = slots[0]


def near_kernel(low_ref, sg_ref, vg_ref):
    for head in range(low_ref.shape[0]):
        at = head * VDIM
        vg_ref[:, at : at + VDIM] = mm(low_ref[head], sg_ref[:, at : at + VDIM], NN)


def attend_kernel(qt_ref, prior_ref, num_ref, inv_ref, w_ref, att_ref, part_ref):
    rank = lax.rem(lax.axis_index("ctx"), PLANE)
    heads = qt_ref.shape[0]
    per_piece = heads // PLANE
    for head in range(heads):
        at = head * VDIM
        prior = load_piece(rank, head, per_piece, prior_ref)
        total = num_ref[:, at : at + VDIM] + mm(qt_ref[head], prior, NN)
        att_ref[:, at : at + VDIM] = (total * inv_ref[:, head : head + 1]).astype(BF16)
    part_ref[...] = mm(att_ref[...], w_ref[:, columns_of(w_ref, 1)], NN).astype(BF16)


def mix_kernel(distance, att_ref, w_ref, part_ref):
    weight = w_ref[:, columns_of(w_ref, distance)]
    part_ref[...] = mm(att_ref[...], weight, NN).astype(part_ref.dtype)


def far_block(distance, kt_ref, near_ref, later_ref):
    per_piece = kt_ref.shape[0] // PLANE
    first = (lax.rem(lax.axis_index("ctx"), PLANE) ^ distance) * per_piece
    blocks = []
    for i in range(per_piece):
        columns = pl.ds(pl.multiple_of((first + i) * VDIM, VDIM), VDIM)
        later = later_ref[i * ROWS : (i + 1) * ROWS, :]
        total = near_ref[:, columns] + mm(kt_ref[first + i], later, NN)
        blocks.append(total.astype(BF16))
    return jnp.concatenate(blocks, 1)


def early_kernel(kt_ref, near_ref, *refs):
    *later_refs, block_ref = refs
    for distance, later_ref in enumerate(later_refs):
        block_ref[distance] = far_block(distance, kt_ref, near_ref, later_ref)


def late_kernel(kt_ref, near_ref, early_ref, *refs):
    *later_refs, vg_far, block_ref, sems = refs
    early, columns = early_ref.shape[0], early_ref.shape[2]
    rank = lax.rem(lax.axis_index("ctx"), PLANE)

    def send(distance, ref):
        start = pl.multiple_of((rank ^ distance) * columns, columns)
        return fetch(ref, vg_far.at[:, pl.ds(start, columns)], sems.at[distance])

    copies = [send(distance, early_ref.at[distance]) for distance in range(early)]
    for i, later_ref in enumerate(later_refs):
        block_ref[i] = far_block(early + i, kt_ref, near_ref, later_ref)
        copies.append(send(early + i, block_ref.at[i]))
    for copy in copies:
        copy.wait()


def sum_kernel(part_ref, *refs):
    *other_refs, mixed_far, mixed_ref, sems = refs
    copies = []
    deep = part_ref.shape[0] // PLANE
    for step in range(PLANE):
        rows = pl.ds(step * deep, deep)
        total = part_ref[rows, :]
        for other_ref in other_refs:
            total = total + other_ref[rows, :].astype(F32)
        mixed_ref[rows, :] = total.astype(BF16)
        copies.append(fetch(mixed_ref.at[rows], mixed_far.at[rows], sems.at[step]))
    for copy in copies:
        copy.wait()


def shifted(x, axis, by):
    peers = lax.axis_size(axis)
    pairs = [(i, i + by) for i in range(peers) if 0 <= i + by < peers]
    return lax.ppermute(x, axis, pairs)


def after(x, *others):
    return lax.optimization_barrier((x, *others))[0]


def planes_ahead(total, sent, sign, join, last=None):
    planes = lax.axis_size("ctx") // PLANE
    received, strides = [], []
    stride = 1
    while stride < planes:
        if (planes // stride) % 4 == 0:
            near = sent if last is None else after(sent, last)
            moved = [swapped(near if j == 1 else sent, "ctx", j, stride * PLANE) for j in range(1, 4)]
            strides += [(stride, j) for j in range(1, 4)]
            stride = stride * 4
        else:
            moved = [shifted(sent, "ctx", sign * stride * PLANE)]
            strides.append((stride, 0))
            stride = stride * 2
        received += moved
        if stride < planes:
            sent, total = join(total, moved, stride * 2 < planes)
    return received, strides


def swapped(x, axis, distance, stride=1):
    peers = lax.axis_size(axis)
    pairs = [(i, (i // stride ^ distance) * stride + i % stride) for i in range(peers)]
    return lax.ppermute(x, axis, pairs)


def handed_back(pieces):
    return [pieces[0]] + [swapped(pieces[j], "ctx", j) for j in range(1, PLANE)]


def per_device(queries, keys, values, conv_keys, conv_values, out_weight, cotangent):
    tokens = queries.shape[0]
    heads = queries.shape[1] // FEAT
    width = heads * VDIM
    columns = cotangent.shape[1]
    groups = lax.axis_size("head")
    piece_rows = heads // PLANE * ROWS
    extra = max(0, 15 * heads // 4 - SPARE * heads // PLANE)
    message = (piece_rows + -(-extra // 16) * 16, VDIM)
    S = jax.ShapeDtypeStruct
    step = 2 * tokens * ROWS * VDIM * heads
    project_flops = 2 * tokens * width * columns
    dma = pltpu.SemaphoreType.DMA
    vmem = pltpu.VMEM
    slots = vmem((PLANE, piece_rows, VDIM), F32)

    with jax.named_scope("edge"):
        last_rows = pl.pallas_call(
            edge_kernel,
            out_shape=S((CONV - 1, keys.shape[1] + width), BF16),
            in_specs=[pl.BlockSpec(memory_space=pltpu.HBM)] * 2,
            out_specs=pl.BlockSpec(memory_space=vmem),
            scratch_shapes=[vmem((16, keys.shape[1]), BF16), vmem((16, width), BF16), dma((2,))],
            compiler_params=pltpu.CompilerParams(vmem_limit_bytes=VMEM_LIMIT),
        )(in_hbm(keys), in_hbm(values))
        slabs = lax.axis_size("ctx")
        before = lax.ppermute(last_rows, "ctx", [(i, (i + 1) % slabs) for i in range(slabs)])
    with jax.named_scope("query_features"):
        arrays = (keys, values, conv_keys, conv_values)
        qd, *near_by = call(
            query_kernel,
            (after(queries, last_rows), *arrays),
            [S((heads, ROWS, tokens), BF16)] + [S(x.shape, x.dtype) for x in arrays],
            1 << 20,
            far=range(5),
            scratch=[vmem(queries.shape, BF16), dma((5,))],
        )
    with jax.named_scope("key_features"):
        outs = [
            S((heads, ROWS, tokens), BF16),
            S((tokens, width), BF16),
            S(message, F32),
            S((PLANE, *message), BF16),
        ]
        ops = (*near_by[:2], before, *near_by[2:])
        kf, vc, own, send = call(key_kernel, ops, outs, step, scratch=[slots])
    with jax.named_scope("cotangent"):
        cots = [swapped(after(cotangent, last_rows), "head", j) for j in range(1, groups)]
    with jax.named_scope("prior_share"):
        got = [swapped(send[j], "ctx", j) for j in range(1, PLANE)]

        more = lax.axis_size("ctx") > 4 * PLANE
        half = piece_rows // 2
        count = 15 * heads // 4
        shapes = [(half + -(-count // 16) * 16, VDIM), (half, VDIM)]
        outs = [S(x, BF16) for x in shapes] + [S(x, F32) for x in shapes]
        body = functools.partial(share_kernel, piece_rows)
        sent = call(body, (own, *got[::-1]), outs[: 4 if more else 2], 1 << 20)
        total = sent[2:] if more else (None, None)
        got = [own] + got

        def join(tail, total, received, more):
            outs = [S(total.shape, BF16), S(total.shape, F32)]
            body = functools.partial(join_kernel, tail)
            made = call(body, (total, *received[::-1]), outs[: 2 if more else 1], 1 << 20)
            return made if more else (made[0], None)

    with jax.named_scope("scores"):
        outs = [
            S((heads, tokens, tokens), BF16),
            S((heads, tokens), F32),
            S((tokens, width), F32),
        ]
        low, den, num = call(score_kernel, (qd, kf, vc), outs, 400 * step)
    with jax.named_scope("turned"):
        outs = [S((heads, tokens, ROWS), BF16)] * 2
        qt, kt = call(turn_kernel, (after(qd, den), kf), outs, 1 << 22)
    with jax.named_scope("own_grad"):
        ops = (after(cotangent, den), out_weight)
        outs = [S((tokens, width), F32)]
        (own_grad,) = call(own_grad_kernel, ops, outs, project_flops)
    with jax.named_scope("prior_planes"):
        sent = lax.optimization_barrier((*sent[:2], qt, own_grad))[:2]
        norm_join = functools.partial(join, (half, half + count))
        rest, strides = planes_ahead(total[1], sent[1], 1, functools.partial(join, None))
        moved, _ = planes_ahead(total[0], sent[0], 1, norm_join)
    with jax.named_scope("out_grad"):
        ops = (after(own_grad, moved[0]), *cots, out_weight)
        (out_grad,) = call(
            grad_kernel, ops, [S((tokens, width), F32)], (groups - 1) * project_flops
        )
    with jax.named_scope("scaled_grad"):
        outs = [
            S((tokens, heads), F32),
            S((tokens, width), BF16),
            S((piece_rows, VDIM), F32),
            S((PLANE, piece_rows, VDIM), BF16),
        ]
        ops = (den, qd, out_grad, *got[::-1], *moved)
        body = functools.partial(scale_kernel, strides)
        inverse, scaled, own_later, send_later = call(body, ops, outs, step, scratch=[slots])
    with jax.named_scope("later_share"):
        got_later = [swapped(send_later[j], "ctx", j) for j in range(1, PLANE)]
    with jax.named_scope("prior_back"):
        body = functools.partial(piece_kernel, 1, strides)
        ops = (*got[::-1], *moved, after(rest[0], scaled), *rest[1:])
        (pieces,) = call(body, ops, [S((PLANE, piece_rows, VDIM), BF16)], 1 << 20)
        prior = handed_back(pieces)
        prior = jnp.stack([prior[0]] + prior[:0:-1], 0)
    with jax.named_scope("later_planes"):
        plain_join = functools.partial(join, None)
        sent_later, total_later = plain_join(own_later, got_later, more)
    with jax.named_scope("attended"):
        outs = [S((tokens, width), BF16), S((tokens, columns), BF16)]
        ops = (qt, prior, after(num, sent_later), inverse, out_weight)
        attended, part = call(attend_kernel, ops, outs, step + project_flops)
        parts = [swapped(part, "head", 1)]
    with jax.named_scope("later_planes"):
        moved_later, strides = planes_ahead(total_later, sent_later, -1, plain_join, part)
    with jax.named_scope("near"):
        ops = (low, after(scaled, sent_later))
        (near,) = call(near_kernel, ops, [S((tokens, width), F32)], 2 * step)
    with jax.named_scope("mixed"):
        for j in list(range(2, groups)) + [0]:
            outs = [S((tokens, columns), BF16 if j else F32)]
            body = functools.partial(mix_kernel, j)
            ops = (after(attended, sent_later), out_weight)
            (part,) = call(body, ops, outs, 2 * project_flops)
            if j:
                parts.append(swapped(part, "head", j))
    with jax.named_scope("later_back"):
        outs = [S((PLANE, piece_rows, VDIM), BF16)]
        body = functools.partial(piece_kernel, -1, strides)
        ops = (*got_later[::-1], own_later, after(moved_later[0], part, near), *moved_later[1:])
        (pieces,) = call(body, ops, outs, 1 << 20)
        later = handed_back(pieces)
    with jax.named_scope("far_grad"):
        block = (tokens, width // PLANE)
        outs = [S((2, *block), BF16)]
        (early,) = call(early_kernel, (kt, near, *later[:2]), outs, 16 * step)
        (value_grad,) = call(
            late_kernel,
            (kt, near, early, *later[2:]),
            [S((tokens, width), BF16)],
            16 * step,
            scratch=[vmem((PLANE - 2, *block), BF16), dma((PLANE,))],
            out_far=True,
        )
    with jax.named_scope("mixed_out"):
        (mixed_out,) = call(
            sum_kernel,
            (part, *[after(x, value_grad) for x in parts]),
            [S((tokens, columns), BF16)],
            1 << 20,
            scratch=[vmem((tokens, columns), BF16), dma((PLANE,))],
            out_far=True,
        )
    return mixed_out, value_grad


def solution(mesh):
    in_specs = (
        P("ctx", "head"),
        P("ctx", "head"),
        P("ctx", "head"),
        P(None, "head"),
        P(None, "head"),
        P("head", None),
        P("ctx", "head"),
    )
    out_specs = (P("ctx", "head"), P("ctx", "head"))
    return jax.shard_map(
        per_device, mesh=mesh, in_specs=in_specs, out_specs=out_specs, check_vma=False
    )
```

```python
import functools

import jax
import jax.numpy as jnp
from jax import lax
from jax.experimental import pallas as pl
from jax.experimental.pallas import tpu as pltpu
from jax.sharding import PartitionSpec as P

FEAT = 16
VDIM = 128
CONV = 3
ROWS = 160
VMEM_LIMIT = 14 * 1024 * 1024
SPARE = 7
FIRST = 4
PLANE = 4

F32 = jnp.float32
BF16 = jnp.bfloat16
TN = (((0,), (0,)), ((), ()))
NT = (((1,), (1,)), ((), ()))
NN = (((1,), (0,)), ((), ()))


def mm(a, b, dims):
    return lax.dot_general(a, b, dims, preferred_element_type=F32)


def call(body, operands, out_shape, flops, far=(), scratch=(), out_far=False):
    moved = sum(x.size * x.dtype.itemsize for x in operands)
    moved += sum(x.size * x.dtype.itemsize for x in out_shape)
    vmem = pl.BlockSpec(memory_space=pltpu.VMEM)
    hbm = pl.BlockSpec(memory_space=pltpu.HBM)
    return pl.pallas_call(
        body,
        out_shape=out_shape,
        in_specs=[hbm if i in far else vmem for i in range(len(operands))],
        out_specs=[hbm if out_far else vmem for _ in out_shape],
        scratch_shapes=list(scratch),
        compiler_params=pltpu.CompilerParams(vmem_limit_bytes=VMEM_LIMIT),
        cost_estimate=pl.CostEstimate(flops=flops, bytes_accessed=moved, transcendentals=0),
    )(*[in_hbm(x) if i in far else x for i, x in enumerate(operands)])


def in_hbm(x):
    return pltpu.with_memory_space_constraint(x, pltpu.HBM)


def fetch(source, target, sem):
    copy = pltpu.make_async_copy(source, target, sem)
    copy.start()
    return copy


def store_features(out_ref, rows_in, doubled):
    heads = rows_in.shape[0] // FEAT
    tokens = rows_in.shape[1]
    grid = rows_in.reshape(heads, FEAT, tokens) * FEAT ** (-0.25)
    twice = jnp.concatenate([grid, grid], 1)
    out_ref[:, 0:FEAT, :] = grid.astype(BF16)
    half = FEAT // 2
    for turn in range(half):
        square = grid * twice[:, turn : turn + FEAT, :] * 0.5**0.5
        if doubled and turn > 0:
            square = square * 2.0
        out_ref[:, FEAT * (turn + 1) : FEAT * (turn + 2), :] = square.astype(BF16)
    square = grid[:, :half, :] * grid[:, half:, :] * 0.5**0.5
    if doubled:
        square = square * 2.0
    first = lax.broadcasted_iota(jnp.int32, (heads, half, tokens), 1) == 0
    constant = jnp.where(first, 1.0, 0.0)
    out_ref[:, FEAT * (half + 1) :, :] = jnp.concatenate([square, constant], 1).astype(BF16)


def store_piece(rank, head, per_piece, state, own_ref, send_ref):
    slot = rank ^ (head // per_piece)
    at = (head % per_piece) * ROWS
    own_ref[slot, at : at + ROWS, :] = state
    send_ref[slot, at : at + ROWS, :] = state.astype(BF16)


def load_piece(rank, head, per_piece, ref):
    at = (head % per_piece) * ROWS
    return ref[lax.rem(PLANE - (rank ^ (head // per_piece)), PLANE), at : at + ROWS, :]


def edge_kernel(k_far, v_far, edge_ref, k_ref, v_ref, sems):
    tokens, width = k_far.shape
    deep = k_ref.shape[0]
    rows = pl.ds(tokens - deep, deep)
    copies = [fetch(k_far.at[rows], k_ref, sems.at[0]), fetch(v_far.at[rows], v_ref, sems.at[1])]
    last = deep - CONV + 1
    copies[0].wait()
    edge_ref[:, :width] = k_ref[...].astype(F32)[last:].astype(BF16)
    copies[1].wait()
    edge_ref[:, width:] = v_ref[...].astype(F32)[last:].astype(BF16)


def load_kernel(k_far, v_far, ck_far, cv_far, k_ref, v_ref, ck_ref, cv_ref, sems):
    pairs = ((k_far, k_ref), (v_far, v_ref), (ck_far, ck_ref), (cv_far, cv_ref))
    copies = [fetch(a, b, sems.at[i]) for i, (a, b) in enumerate(pairs)]
    for copy in copies:
        copy.wait()


def query_kernel(
    q_far,
    k_far,
    v_far,
    ck_far,
    cv_far,
    qd_ref,
    k_ref,
    v_ref,
    ck_ref,
    cv_ref,
    q_ref,
    sems,
):
    far = (q_far, k_far, v_far, ck_far, cv_far)
    near = (q_ref, k_ref, v_ref, ck_ref, cv_ref)
    copies = [fetch(a, b, sems.at[i]) for i, (a, b) in enumerate(zip(far, near))]
    copies[0].wait()
    store_features(qd_ref, q_ref[...].astype(F32).T, True)
    for copy in copies[1:]:
        copy.wait()


def columns_of(w_ref, distance):
    columns = w_ref.shape[1] // lax.axis_size("head")
    return pl.ds(pl.multiple_of((lax.axis_index("head") ^ distance) * columns, columns), columns)


def turn_kernel(qd_ref, kf_ref, qt_ref, kt_ref):
    for head in range(qd_ref.shape[0]):
        qt_ref[head] = qd_ref[head].T
        kt_ref[head] = kf_ref[head].T


def own_grad_kernel(cot_ref, w_ref, og_ref):
    og_ref[...] = mm(cot_ref[...], w_ref[:, columns_of(w_ref, 0)], NT)


def grad_kernel(before_ref, *refs):
    *cots, w_ref, og_ref = refs
    total = before_ref[...]
    for j, cot_ref in enumerate(cots):
        total = total + mm(cot_ref[...], w_ref[:, columns_of(w_ref, j + 1)], NT)
    og_ref[...] = total


def masked(wanted, value):
    return jnp.where(wanted, value.astype(F32), 0.0)


def conv_rows(x, before, taps):
    x = x.astype(F32)
    row = lax.broadcasted_iota(jnp.int32, x.shape, 0)
    running = taps[0:1, :] * x
    for offset in range(1, CONV):
        moved = pltpu.roll(x, offset, 0)
        for at in range(offset):
            source = before[CONV - 1 - offset + at : CONV - offset + at, :]
            moved = jnp.where(row == at, source, moved)
        running = running + taps[offset : offset + 1, :] * moved
    return running


def norm_rows(norm):
    high = norm.astype(BF16).astype(F32)
    middle = (norm - high).astype(BF16).astype(F32)
    parts = jnp.concatenate([high, middle, norm - high - middle], 0)
    deep = parts.shape[0] // 4
    tail = [parts[i * deep : (i + 1) * deep, VDIM:] for i in range(4)]
    return jnp.concatenate([parts[:, :VDIM], jnp.concatenate(tail, 1)], 0)


def norm_values(lines):
    heads = lines.shape[0] * 4 // 15
    wide = ROWS - VDIM
    tail = [lines[3 * heads :, i * wide : (i + 1) * wide] for i in range(4)]
    parts = jnp.concatenate([lines[: 3 * heads], jnp.concatenate(tail, 0)], 1)
    return parts[:heads] + parts[heads : 2 * heads] + parts[2 * heads :]


def with_lines(state, lines, rows):
    pieces, used = [], 0
    for first in range(0, state.shape[0], ROWS):
        free = min(SPARE, lines.shape[0] - used)
        last = jnp.concatenate(
            [
                state[first + ROWS - SPARE - 1 : first + ROWS - SPARE],
                lines[used : used + free],
                jnp.zeros((SPARE - free, VDIM), F32),
            ][: 3 if free < SPARE else 2],
            0,
        )
        pieces += [state[first : first + ROWS - SPARE - 1], last]
        used += free
    left = rows - state.shape[0]
    blank = left - (lines.shape[0] - used)
    if left > 0:
        pieces.append(lines[used:])
        if blank > 0:
            pieces.append(jnp.zeros((blank, VDIM), F32))
    return jnp.concatenate(pieces, 0)


def lines_in(state, piece_rows):
    count = 15 * (piece_rows // ROWS * PLANE) // 4
    found, used = [], 0
    for first in range(0, piece_rows, ROWS):
        free = min(SPARE, count - used)
        tile = state[first + ROWS - 16 : first + ROWS, :].astype(F32)
        found.append(tile[16 - SPARE : 16 - SPARE + free])
        used += free
    rest = state[piece_rows:, :].astype(F32)
    return jnp.concatenate(found + [rest[: count - used]], 0)


def key_kernel(
    k_ref,
    v_ref,
    before_ref,
    ck_ref,
    cv_ref,
    kf_ref,
    vc_ref,
    own_ref,
    send_ref,
    slots,
):
    rank = lax.rem(lax.axis_index("ctx"), PLANE)
    heads = kf_ref.shape[0]
    per_piece = heads // PLANE
    width = k_ref.shape[1]
    before = masked(lax.axis_index("ctx") > 0, before_ref[...])
    key_conv = conv_rows(k_ref[...], before[:, :width], ck_ref[...])
    store_features(kf_ref, key_conv.T, False)
    ones = jnp.ones((heads, k_ref.shape[0]), BF16)
    row = lax.broadcasted_iota(jnp.int32, (heads, ROWS), 0)
    norm = jnp.zeros((heads, ROWS), F32)
    for head in range(heads):
        at = head * VDIM
        value = conv_rows(
            v_ref[:, at : at + VDIM],
            before[:, width + at : width + at + VDIM],
            cv_ref[:, at : at + VDIM],
        ).astype(BF16)
        vc_ref[:, at : at + VDIM] = value
        feat = kf_ref[head]
        norm = jnp.where(row == head, mm(ones, feat, NT), norm)
        first = (head % per_piece) * ROWS
        slots[rank ^ (head // per_piece), first : first + ROWS, :] = mm(feat, value, NN)
    lines = norm_rows(norm)
    for slot in range(PLANE):
        piece = with_lines(slots[slot], lines, own_ref.shape[0])
        if slot == 0:
            own_ref[...] = piece
        else:
            send_ref[slot] = piece.astype(BF16)


def share_kernel(piece_rows, own_ref, *refs):
    got_refs, out_refs = refs[: PLANE - 1], refs[PLANE - 1 :]
    total = own_ref[...]
    for got_ref in got_refs:
        total = total + got_ref[...].astype(F32)
    half = piece_rows * FIRST // 10
    lines = norm_rows(norm_values(lines_in(total, piece_rows)))
    parts = (with_tail(total[:half], lines, out_refs[0].shape[0]), total[half:piece_rows])
    for ref, part in zip(out_refs, parts):
        ref[...] = part.astype(BF16)
    for ref, part in zip(out_refs[2:], parts):
        ref[...] = part


def with_tail(state, lines, rows):
    blank = jnp.zeros((rows - state.shape[0] - lines.shape[0], VDIM), F32)
    return jnp.concatenate([state, lines, blank], 0)


def join_kernel(tail, total_ref, *refs):
    out_at = -1 if refs[-1].dtype == BF16 else -2
    total = total_ref[...]
    for got_ref in refs[:out_at]:
        total = total + got_ref[...].astype(F32)
    if tail is not None:
        lines = norm_rows(norm_values(total[tail[0] : tail[1]]))
        total = with_tail(total[: tail[0]], lines, total.shape[0])
    refs[out_at][...] = total.astype(BF16)
    if out_at == -2:
        refs[-1][...] = total


def is_ahead(sign, other, here):
    return other < here if sign > 0 else other > here


def before_plane(sign, strides, refs, rows):
    total = 0.0
    for ref, (stride, distance) in zip(refs, strides):
        if distance:
            group = lax.div(lax.axis_index("ctx"), PLANE * stride)
            total = total + masked(is_ahead(sign, group ^ distance, group), ref[rows, :])
        else:
            total = total + ref[rows, :].astype(F32)
    return total


def piece_kernel(sign, strides, *refs):
    got_refs, moved_refs, pieces_ref = refs[:PLANE][::-1], refs[PLANE:-1], refs[-1]
    rank = lax.rem(lax.axis_index("ctx"), PLANE)
    count = len(strides)
    whole = pieces_ref.shape[1]
    cuts = [0, whole] if len(moved_refs) == count else [0, whole * FIRST // 10, whole]
    for part in range(len(cuts) - 1):
        deep = cuts[part + 1] - cuts[part]
        refs = moved_refs[part * count : (part + 1) * count]
        before = before_plane(sign, strides, refs, pl.ds(0, deep))
        rows = pl.ds(cuts[part], deep)
        for slot in range(PLANE):
            total = before
            for i in range(PLANE):
                if i != slot:
                    ahead = is_ahead(sign, rank ^ i, rank ^ slot)
                    total = total + masked(ahead, got_refs[i][rows, :])
            pieces_ref[slot, rows, :] = total.astype(BF16)


def score_kernel(qd_ref, kf_ref, vc_ref, low_ref, den_ref, num_ref):
    heads = kf_ref.shape[0]
    tokens = kf_ref.shape[2]
    key_at = lax.broadcasted_iota(jnp.int32, (tokens, tokens), 0)
    query_at = lax.broadcasted_iota(jnp.int32, (tokens, tokens), 1)
    causal = key_at <= query_at
    for head in range(heads):
        scores = jnp.where(causal, mm(kf_ref[head], qd_ref[head], TN), 0.0)
        den_ref[head : head + 1, :] = jnp.sum(scores, 0, keepdims=True)
        low = scores.astype(BF16)
        low_ref[head] = low
        at = head * VDIM
        num_ref[:, at : at + VDIM] = mm(low, vc_ref[:, at : at + VDIM], TN)


def scale_kernel(strides, den_ref, qd_ref, og_ref, *refs):
    *refs, inv_ref, sg_ref, own_ref, send_ref, slots = refs
    got_refs, moved_refs = refs[:PLANE][::-1], refs[PLANE:]
    rank = lax.rem(lax.axis_index("ctx"), PLANE)
    heads = qd_ref.shape[0]
    per_piece = heads // PLANE
    piece_rows = per_piece * ROWS
    half = piece_rows * FIRST // 10
    lines = before_plane(1, strides, moved_refs, pl.ds(half, moved_refs[0].shape[0] - half))
    lines = lines[: 15 * heads // 4]
    for i in range(1, PLANE):
        here = lines_in(got_refs[i], piece_rows)
        lines = lines + masked(is_ahead(1, rank ^ i, rank), here)
    norm = norm_values(lines)
    high = norm.astype(BF16).astype(F32)
    middle = (norm - high).astype(BF16).astype(F32)
    rest = norm - high - middle
    parts = jnp.concatenate([high, middle, rest, jnp.zeros_like(rest)], 0).astype(BF16)
    lines = []
    for head in range(heads):
        terms = mm(parts, qd_ref[head], NN)
        line = den_ref[head : head + 1, :] + terms[head : head + 1, :]
        line = line + terms[heads + head : heads + head + 1, :]
        lines.append(line + terms[2 * heads + head : 2 * heads + head + 1, :])
    inverse = (1.0 / jnp.concatenate(lines, 0)).T
    inv_ref[...] = inverse
    for head in range(heads):
        at = head * VDIM
        scaled = (og_ref[:, at : at + VDIM] * inverse[:, head : head + 1]).astype(BF16)
        sg_ref[:, at : at + VDIM] = scaled
        store_piece(rank, head, per_piece, mm(qd_ref[head], scaled, NN), slots, send_ref)
    own_ref[...] = slots[0]


def near_kernel(low_ref, sg_ref, vg_ref):
    for head in range(low_ref.shape[0]):
        at = head * VDIM
        vg_ref[:, at : at + VDIM] = mm(low_ref[head], sg_ref[:, at : at + VDIM], NN)


def attend_kernel(qt_ref, prior_ref, num_ref, inv_ref, w_ref, att_ref, part_ref):
    rank = lax.rem(lax.axis_index("ctx"), PLANE)
    heads = qt_ref.shape[0]
    per_piece = heads // PLANE
    for head in range(heads):
        at = head * VDIM
        prior = load_piece(rank, head, per_piece, prior_ref)
        total = num_ref[:, at : at + VDIM] + mm(qt_ref[head], prior, NN)
        att_ref[:, at : at + VDIM] = (total * inv_ref[:, head : head + 1]).astype(BF16)
    part_ref[...] = mm(att_ref[...], w_ref[:, columns_of(w_ref, 1)], NN).astype(BF16)


def mix_kernel(distance, att_ref, w_ref, part_ref):
    weight = w_ref[:, columns_of(w_ref, distance)]
    part_ref[...] = mm(att_ref[...], weight, NN).astype(part_ref.dtype)


def far_block(distance, kt_ref, near_ref, later_ref):
    per_piece = kt_ref.shape[0] // PLANE
    first = (lax.rem(lax.axis_index("ctx"), PLANE) ^ distance) * per_piece
    blocks = []
    for i in range(per_piece):
        columns = pl.ds(pl.multiple_of((first + i) * VDIM, VDIM), VDIM)
        later = later_ref[i * ROWS : (i + 1) * ROWS, :]
        total = near_ref[:, columns] + mm(kt_ref[first + i], later, NN)
        blocks.append(total.astype(BF16))
    return jnp.concatenate(blocks, 1)


def early_kernel(kt_ref, near_ref, *refs):
    *later_refs, block_ref = refs
    for distance, later_ref in enumerate(later_refs):
        block_ref[distance] = far_block(distance, kt_ref, near_ref, later_ref)


def late_kernel(kt_ref, near_ref, early_ref, *refs):
    *later_refs, vg_far, block_ref, sems = refs
    early, columns = early_ref.shape[0], early_ref.shape[2]
    rank = lax.rem(lax.axis_index("ctx"), PLANE)

    def send(distance, ref):
        start = pl.multiple_of((rank ^ distance) * columns, columns)
        return fetch(ref, vg_far.at[:, pl.ds(start, columns)], sems.at[distance])

    copies = [send(distance, early_ref.at[distance]) for distance in range(early)]
    for i, later_ref in enumerate(later_refs):
        block_ref[i] = far_block(early + i, kt_ref, near_ref, later_ref)
        copies.append(send(early + i, block_ref.at[i]))
    for copy in copies:
        copy.wait()


def sum_kernel(part_ref, *refs):
    *other_refs, mixed_far, mixed_ref, sems = refs
    copies = []
    deep = part_ref.shape[0] // PLANE
    for step in range(PLANE):
        rows = pl.ds(step * deep, deep)
        total = part_ref[rows, :]
        for other_ref in other_refs:
            total = total + other_ref[rows, :].astype(F32)
        mixed_ref[rows, :] = total.astype(BF16)
        copies.append(fetch(mixed_ref.at[rows], mixed_far.at[rows], sems.at[step]))
    for copy in copies:
        copy.wait()


def shifted(x, axis, by):
    peers = lax.axis_size(axis)
    pairs = [(i, i + by) for i in range(peers) if 0 <= i + by < peers]
    return lax.ppermute(x, axis, pairs)


def after(x, *others):
    return lax.optimization_barrier((x, *others))[0]


def planes_ahead(total, sent, sign, join, last=None):
    planes = lax.axis_size("ctx") // PLANE
    received, strides = [], []
    stride = 1
    while stride < planes:
        if (planes // stride) % 4 == 0:
            near = sent if last is None else after(sent, last)
            moved = [swapped(near if j == 1 else sent, "ctx", j, stride * PLANE) for j in range(1, 4)]
            strides += [(stride, j) for j in range(1, 4)]
            stride = stride * 4
        else:
            moved = [shifted(sent, "ctx", sign * stride * PLANE)]
            strides.append((stride, 0))
            stride = stride * 2
        received += moved
        if stride < planes:
            sent, total = join(total, moved, stride * 2 < planes)
    return received, strides


def swapped(x, axis, distance, stride=1):
    peers = lax.axis_size(axis)
    pairs = [(i, (i // stride ^ distance) * stride + i % stride) for i in range(peers)]
    return lax.ppermute(x, axis, pairs)


def handed_back(pieces):
    return [pieces[0]] + [swapped(pieces[j], "ctx", j) for j in range(1, PLANE)]


def per_device(queries, keys, values, conv_keys, conv_values, out_weight, cotangent):
    tokens = queries.shape[0]
    heads = queries.shape[1] // FEAT
    width = heads * VDIM
    columns = cotangent.shape[1]
    groups = lax.axis_size("head")
    piece_rows = heads // PLANE * ROWS
    extra = max(0, 15 * heads // 4 - SPARE * heads // PLANE)
    message = (piece_rows + -(-extra // 16) * 16, VDIM)
    S = jax.ShapeDtypeStruct
    step = 2 * tokens * ROWS * VDIM * heads
    project_flops = 2 * tokens * width * columns
    dma = pltpu.SemaphoreType.DMA
    vmem = pltpu.VMEM
    slots = vmem((PLANE, piece_rows, VDIM), F32)

    with jax.named_scope("edge"):
        last_rows = pl.pallas_call(
            edge_kernel,
            out_shape=S((CONV - 1, keys.shape[1] + width), BF16),
            in_specs=[pl.BlockSpec(memory_space=pltpu.HBM)] * 2,
            out_specs=pl.BlockSpec(memory_space=vmem),
            scratch_shapes=[vmem((16, keys.shape[1]), BF16), vmem((16, width), BF16), dma((2,))],
            compiler_params=pltpu.CompilerParams(vmem_limit_bytes=VMEM_LIMIT),
        )(in_hbm(keys), in_hbm(values))
        slabs = lax.axis_size("ctx")
        before = lax.ppermute(last_rows, "ctx", [(i, (i + 1) % slabs) for i in range(slabs)])
    with jax.named_scope("query_features"):
        arrays = (keys, values, conv_keys, conv_values)
        qd, *near_by = call(
            query_kernel,
            (after(queries, last_rows), *arrays),
            [S((heads, ROWS, tokens), BF16)] + [S(x.shape, x.dtype) for x in arrays],
            1 << 20,
            far=range(5),
            scratch=[vmem(queries.shape, BF16), dma((5,))],
        )
    with jax.named_scope("key_features"):
        outs = [
            S((heads, ROWS, tokens), BF16),
            S((tokens, width), BF16),
            S(message, F32),
            S((PLANE, *message), BF16),
        ]
        ops = (*near_by[:2], before, *near_by[2:])
        kf, vc, own, send = call(key_kernel, ops, outs, step, scratch=[slots])
    with jax.named_scope("cotangent"):
        cots = [swapped(after(cotangent, last_rows), "head", j) for j in range(1, groups)]
    with jax.named_scope("prior_share"):
        got = [swapped(send[j], "ctx", j) for j in range(1, PLANE)]

        more = lax.axis_size("ctx") > 4 * PLANE
        half = piece_rows * FIRST // 10
        count = 15 * heads // 4
        shapes = [(half + -(-count // 16) * 16, VDIM), (piece_rows - half, VDIM)]
        outs = [S(x, BF16) for x in shapes] + [S(x, F32) for x in shapes]
        body = functools.partial(share_kernel, piece_rows)
        sent = call(body, (own, *got[::-1]), outs[: 4 if more else 2], 1 << 20)
        total = sent[2:] if more else (None, None)
        got = [own] + got

        def join(tail, total, received, more):
            outs = [S(total.shape, BF16), S(total.shape, F32)]
            body = functools.partial(join_kernel, tail)
            made = call(body, (total, *received[::-1]), outs[: 2 if more else 1], 1 << 20)
            return made if more else (made[0], None)

    with jax.named_scope("scores"):
        outs = [
            S((heads, tokens, tokens), BF16),
            S((heads, tokens), F32),
            S((tokens, width), F32),
        ]
        low, den, num = call(score_kernel, (qd, kf, vc), outs, 400 * step)
    with jax.named_scope("turned"):
        outs = [S((heads, tokens, ROWS), BF16)] * 2
        qt, kt = call(turn_kernel, (after(qd, den), kf), outs, 1 << 22)
    with jax.named_scope("own_grad"):
        ops = (after(cotangent, den), out_weight)
        outs = [S((tokens, width), F32)]
        (own_grad,) = call(own_grad_kernel, ops, outs, project_flops)
    with jax.named_scope("prior_planes"):
        sent = lax.optimization_barrier((*sent[:2], qt, own_grad))[:2]
        norm_join = functools.partial(join, (half, half + count))
        rest, strides = planes_ahead(total[1], sent[1], 1, functools.partial(join, None))
        moved, _ = planes_ahead(total[0], sent[0], 1, norm_join)
    with jax.named_scope("out_grad"):
        ops = (after(own_grad, moved[0]), *cots, out_weight)
        (out_grad,) = call(
            grad_kernel, ops, [S((tokens, width), F32)], (groups - 1) * project_flops
        )
    with jax.named_scope("scaled_grad"):
        outs = [
            S((tokens, heads), F32),
            S((tokens, width), BF16),
            S((piece_rows, VDIM), F32),
            S((PLANE, piece_rows, VDIM), BF16),
        ]
        ops = (den, qd, out_grad, *got[::-1], *moved)
        body = functools.partial(scale_kernel, strides)
        inverse, scaled, own_later, send_later = call(body, ops, outs, step, scratch=[slots])
    with jax.named_scope("later_share"):
        got_later = [swapped(send_later[j], "ctx", j) for j in range(1, PLANE)]
    with jax.named_scope("prior_back"):
        body = functools.partial(piece_kernel, 1, strides)
        ops = (*got[::-1], *moved, after(rest[0], scaled), *rest[1:])
        (pieces,) = call(body, ops, [S((PLANE, piece_rows, VDIM), BF16)], 1 << 20)
        prior = handed_back(pieces)
        prior = jnp.stack([prior[0]] + prior[:0:-1], 0)
    with jax.named_scope("later_planes"):
        plain_join = functools.partial(join, None)
        sent_later, total_later = plain_join(own_later, got_later, more)
    with jax.named_scope("attended"):
        outs = [S((tokens, width), BF16), S((tokens, columns), BF16)]
        ops = (qt, prior, after(num, sent_later), inverse, out_weight)
        attended, part = call(attend_kernel, ops, outs, step + project_flops)
        parts = [swapped(part, "head", 1)]
    with jax.named_scope("later_planes"):
        moved_later, strides = planes_ahead(total_later, sent_later, -1, plain_join, part)
    with jax.named_scope("near"):
        ops = (low, after(scaled, sent_later))
        (near,) = call(near_kernel, ops, [S((tokens, width), F32)], 2 * step)
    with jax.named_scope("mixed"):
        for j in list(range(2, groups)) + [0]:
            outs = [S((tokens, columns), BF16 if j else F32)]
            body = functools.partial(mix_kernel, j)
            ops = (after(attended, sent_later), out_weight)
            (part,) = call(body, ops, outs, 2 * project_flops)
            if j:
                parts.append(swapped(part, "head", j))
    with jax.named_scope("later_back"):
        outs = [S((PLANE, piece_rows, VDIM), BF16)]
        body = functools.partial(piece_kernel, -1, strides)
        ops = (*got_later[::-1], own_later, after(moved_later[0], part, near), *moved_later[1:])
        (pieces,) = call(body, ops, outs, 1 << 20)
        later = handed_back(pieces)
    with jax.named_scope("far_grad"):
        block = (tokens, width // PLANE)
        outs = [S((2, *block), BF16)]
        (early,) = call(early_kernel, (kt, near, *later[:2]), outs, 16 * step)
        (value_grad,) = call(
            late_kernel,
            (kt, near, early, *later[2:]),
            [S((tokens, width), BF16)],
            16 * step,
            scratch=[vmem((PLANE - 2, *block), BF16), dma((PLANE,))],
            out_far=True,
        )
    with jax.named_scope("mixed_out"):
        (mixed_out,) = call(
            sum_kernel,
            (part, *[after(x, value_grad) for x in parts]),
            [S((tokens, columns), BF16)],
            1 << 20,
            scratch=[vmem((tokens, columns), BF16), dma((PLANE,))],
            out_far=True,
        )
    return mixed_out, value_grad


def solution(mesh):
    in_specs = (
        P("ctx", "head"),
        P("ctx", "head"),
        P("ctx", "head"),
        P(None, "head"),
        P(None, "head"),
        P("head", None),
        P("ctx", "head"),
    )
    out_specs = (P("ctx", "head"), P("ctx", "head"))
    return jax.shard_map(
        per_device, mesh=mesh, in_specs=in_specs, out_specs=out_specs, check_vma=False
    )
```
